32 devices in a mesh: dp: 16 (over z, y, x), tensor: 2 (over core).
Axes of the slice: x: 2, y: 2, z: 4, core: 2. Of those that a mesh axis runs over, the one named last changes fastest.
Arguments:
- leaf_tokens: bfloat16 [128, 8, 2048], P(('dp', 'tensor')), may hold values from -40 to 40
- attn_gain: float32 [2048], replicated, may hold values from 0.25 to 2.5
- w_query: bfloat16 [2048, 2048], P(None, 'tensor'), may hold values from -0.125 to 0.125
- w_key: bfloat16 [2048, 2048], P(None, 'tensor'), may hold values from -0.125 to 0.125
- w_value: bfloat16 [2048, 2048], P(None, 'tensor'), may hold values from -0.125 to 0.125
- w_out: bfloat16 [2048, 2048], P('tensor'), may hold values from -0.125 to 0.125
- prefix_kv: bfloat16 [2, 14336, 2048], P(None, 'dp', 'tensor'), may hold values from -104 to 104
- prefix_owner: int32 [128, 3], P('dp'), may hold values from 0 to 15, as said below
- prefix_start: int32 [128, 3], P('dp'), may hold values from 0 to 864, as said below
- prefix_len: int32 [128, 3], P('dp'), may hold values from 1 to 512, as said below
- mlp_gain: float32 [2048], replicated, may hold values from 0.25 to 2.5
- shared_in: bfloat16 [2048, 2, 1408], P(None, None, 'tensor'), may hold values from -0.125 to 0.125
- shared_out: bfloat16 [1408, 2048], P('tensor'), may hold values from -0.15625 to 0.15625
- expert_in: bfloat16 [64, 2048, 2, 1408], P('dp', None, None, 'tensor'), may hold values from -0.125 to 0.125
- expert_out: bfloat16 [64, 1408, 2048], P('dp', 'tensor'), may hold values from -0.15625 to 0.15625
- expert_ids: int32 [128, 8, 6], P('dp'), may hold values from 0 to 63, all different within a row; in each aligned block of 64 rows (0 to 63, 64 to 127, ..., all dimensions but the last counted through in order) at most 8 rows name the same one
- gate_weights: float32 [128, 8, 6], P('dp'), may hold values from 0.05 to 0.4
- request_of: int32 [128], P('dp'), may hold values from 0 to 127, as said below
Outputs:
- layer_out: bfloat16 [128, 8, 2048], P('dp', 'tensor')
The draws below stay inside these ranges and needn't reach their ends.
Inputs may be any that keep to these rules, and one draw needn't show every extreme that they name: `prefix_owner`: each data group owns exactly one first-level node, two second-level nodes and four third-level nodes; a first-level node serves 8 requests, a second-level node half as many, a third-level node a quarter. The 8 requests of one data group name 8 different owners at each level, and together over the three levels they name no owner more than twice. `prefix_start`: the first level starts at 0; the second at 512 or 640; the third at 768 + q * 32 with q from 0 to 3. `prefix_len`: A node has 1 to 512, 128 or 32 keys at the first, second or third level, each of these maxima reached. Requests naming the same owner and start at a level share that node and its length; each node lies under one node of the level above. `expert_ids`: each row names 6 different experts; in the rows of one data group (aligned blocks of 64 rows) no expert is named more than 8 times. `request_of`: A permutation; the 8 dealt requests of one data group go to 8 different data groups.
All inputs are finite; a program needn't handle non-finite values.
Results may differ from the reference program's by a relative error of at most 0.025.
Values may be sent and summed in bfloat16 or wider, within the bound.
No kernel may reach another device: no remote copies, remote signals or barrier semaphores. Data moves between devices by JAX's collectives and lax.ppermute only.
A program may use at most 128 MiB of HBM per device.

```python
import math
import jax
import jax.numpy as jnp
import numpy as np
from jax import lax

D = 2048
HEADS = 16
HEAD_DIM = 128
EXPERTS = 64
TOPK = 6
FF = 1408
SHARED = 1
LEAF_LEN = 8
MAX3 = 32
MAX2 = 128
MAX1 = 512
POOL_DEV = 896
POOL = 14336
R_DEV = 8
REQS = 128
CAP_E = 8
N_DP = 16
N_TENSOR = 2


def draw_leaf_tokens(key, part):
    noise_key, row_key, column_key = jax.random.split(jax.random.fold_in(key, 3), 3)
    full_shape = (REQS, LEAF_LEN, D)
    column_scale = jnp.exp(jax.random.uniform(column_key, (1, 1, D), jnp.float32, -1.15, 1.15))
    noise_rows = jax.random.truncated_normal(noise_key, -4.0, 4.0, full_shape, jnp.float32)
    row_scale = jnp.exp(jax.random.uniform(row_key, (REQS, LEAF_LEN, 1), jnp.float32, -1.15, 1.15))
    return (noise_rows * row_scale * column_scale).astype(jnp.bfloat16)


def draw_prefix_kv(key, part):
    key_noise, value_noise = jax.random.split(jax.random.fold_in(key, 5), 2)
    width_all = HEADS * HEAD_DIM
    key_part = jax.random.truncated_normal(key_noise, -4.0, 4.0, (1, POOL, width_all), jnp.float32)
    value_part = 2.0 * jax.random.truncated_normal(value_noise, -4.0, 4.0, (1, POOL, width_all), jnp.float32)
    return jnp.concatenate([key_part, value_part], axis=0).astype(jnp.bfloat16)


def ragged_lengths(one_key, node_count, longest):
    first_key, second_key = jax.random.split(one_key)
    raw_draw = jax.random.randint(first_key, (node_count,), 0, longest)
    lengths = 1 + raw_draw * raw_draw // longest
    forced = jax.random.randint(second_key, (), 0, node_count)
    return lengths.at[forced].set(longest)


def tree_tables(key):
    base_key = jax.random.fold_in(key, 7)
    groups = REQS // R_DEV
    order_key, slots_key, root_key, middle_key, lower_key = jax.random.split(base_key, 5)
    group_order = jax.random.permutation(order_key, groups)
    group_inverse = jnp.argsort(group_order)
    slot_keys = jax.random.split(slots_key, groups)
    local_slot = jax.vmap(lambda one_key: jax.random.permutation(one_key, R_DEV))(slot_keys)
    diagonal = (group_order[:, None] + local_slot) % groups
    half_size = R_DEV // 2
    quarter_size = R_DEV // 4
    half_index = local_slot // half_size
    quarter_index = local_slot // quarter_size
    owner_root = group_inverse[diagonal]
    owner_middle = group_inverse[(diagonal + half_size + half_size * half_index) % groups]
    owner_lower = group_inverse[(diagonal + R_DEV) % groups]
    root_lengths = ragged_lengths(root_key, groups, MAX1)
    middle_lengths = ragged_lengths(middle_key, groups * 2, MAX2).reshape(groups, 2)
    lower_lengths = ragged_lengths(lower_key, groups * 4, MAX3).reshape(groups, 4)
    owners = jnp.stack([owner_root, owner_middle, owner_lower], axis=-1).reshape(REQS, 3)
    starts = jnp.stack([jnp.zeros_like(local_slot), MAX1 + MAX2 * half_index, MAX1 + 2 * MAX2 + MAX3 * quarter_index], axis=-1).reshape(REQS, 3)
    lengths = jnp.stack([root_lengths[diagonal], middle_lengths[diagonal, half_index], lower_lengths[diagonal, quarter_index]], axis=-1).reshape(REQS, 3)
    return (owners.astype(jnp.int32), starts.astype(jnp.int32), lengths.astype(jnp.int32))


def draw_prefix_owner(key, part):
    return tree_tables(key)[0]


def draw_prefix_start(key, part):
    return tree_tables(key)[1]


def draw_prefix_len(key, part):
    return tree_tables(key)[2]


def draw_request_of(key, part):
    base_key = jax.random.fold_in(key, 11)
    groups = REQS // R_DEV
    shift_key, relabel_key, slots_key = jax.random.split(base_key, 3)
    shifts = jax.random.permutation(shift_key, groups)[:R_DEV]
    relabel = jax.random.permutation(relabel_key, groups)
    source_group = jnp.arange(groups)[:, None]
    target = relabel[(source_group + shifts[None, :]) % groups]
    slot_keys = jax.random.split(slots_key, groups)
    arrival = jax.vmap(lambda one_key: jax.random.permutation(one_key, R_DEV))(slot_keys)
    placed = arrival[target, jnp.arange(R_DEV)[None, :]]
    return (target * R_DEV + placed).reshape(REQS).astype(jnp.int32)


def levels(rng, dims, cuts, least, top_value):
    factor_of = 1.0
    for dim, blocks in cuts:
        draws = jax.random.uniform(jax.random.fold_in(jax.random.fold_in(rng, 6), dim), (blocks,), jnp.float32, least / len(cuts), top_value / len(cuts))
        factor_of = factor_of * jnp.repeat(jnp.exp(draws), dims[dim] // blocks).reshape((-1,) + (1,) * (len(dims) - 1 - dim))
    return factor_of


def deal_out(key, own, number, rows, count, top, limit, slope):
    ranking = jax.random.permutation(key, count)
    heavy_load, usual = shares(count, rows * top, limit, slope, True), shares(count, rows * top, limit, slope, False)
    places = jnp.arange(count)

    def named(tallies, turn):
        used = int((tallies > 0).sum())
        fixed = max(1, used // 4)
        moved = fixed + (places - fixed + turn * (used - fixed)) % max(1, count - fixed)
        return jnp.zeros((count,), jnp.int32).at[ranking[jnp.where(places < fixed, places, moved)]].set(jnp.asarray(tallies, jnp.int32))

    tallies = jnp.where(number % 4 == 0, named(heavy_load, number // 4), named(usual, number - number // 4 - 1))
    mixed = jax.random.permutation(jax.random.fold_in(own, 3), count)
    donor, sink = mixed[0:count // 2 * 2:2], mixed[1:count // 2 * 2:2]
    slack = jnp.minimum(tallies[donor] - 1, limit - tallies[sink]) // 2
    slack = jnp.where((donor == ranking[0]) | (sink == ranking[0]) | (tallies[sink] == 0), 0, jnp.maximum(slack, 0))
    moved = jax.random.randint(jax.random.fold_in(own, 4), (count // 2,), 0, 1 << 20) % (slack + 1)
    tallies = tallies.at[donor].add(-moved).at[sink].add(moved)
    labels = jnp.searchsorted(jnp.cumsum(tallies), jnp.arange(rows * top), side="right").astype(jnp.int32)
    listing = labels.reshape(top, rows).T
    listing = listing[jax.random.permutation(jax.random.fold_in(own, 1), rows)]
    turn = jax.random.randint(jax.random.fold_in(own, 2), (rows, 1), 0, top)
    return jnp.take_along_axis(listing, (jnp.arange(top)[None, :] + turn) % top, axis=1)


def shares(amount, total, reach, slope, full):
    weights = [(1 << 20) // math.isqrt(standing ** slope) + 1 for standing in range(1, amount + 1)]
    largest = reach if full else min(reach, max(-(-total // amount), total * weights[0] // sum(weights)))
    least = 1 if total - largest >= amount - 1 else 0
    given, spare = [largest] + [least] * (amount - 1), total - largest - least * (amount - 1)
    while spare > 0:
        movable = [i for i in range(1, amount) if given[i] < largest] or [i for i in range(1, amount) if given[i] < reach]
        whole, remaining = sum([weights[i] for i in movable]), spare
        for i in movable:
            more = min(reach - given[i], max(1, remaining * weights[i] // whole), spare)
            given[i] = given[i] + more
            spare = spare - more
    return np.array(given)


def scatter_about(stream_key, shape, scale, reach, cuts=(), kind=jnp.bfloat16):
    factor_of = levels(stream_key, shape, cuts, -0.22, 0.18) if cuts else 1.0
    entries = jax.random.normal(stream_key, shape, jnp.float32) * scale * factor_of
    return jnp.minimum(jnp.maximum(entries, -reach), reach).astype(kind)


def setup_inputs(seed: int = 0) -> dict:
    splits = jax.random.split(jax.random.key(seed), 19)
    leaf_tokens = draw_leaf_tokens(jax.random.fold_in(splits[18], 71), 0)
    attn_gain = jnp.clip(jnp.exp(jax.random.uniform(splits[1], (D,), jnp.float32, math.log(0.25), math.log(2.5))), 0.25, 2.5)
    w_query = scatter_about(splits[2], (D, HEADS * HEAD_DIM), D ** -0.5, 0.125, ((1, 2),))
    w_key = scatter_about(splits[3], (D, HEADS * HEAD_DIM), D ** -0.5, 0.125, ((1, 2),))
    w_value = scatter_about(splits[4], (D, HEADS * HEAD_DIM), D ** -0.5, 0.125, ((1, 2),))
    w_out = scatter_about(splits[5], (HEADS * HEAD_DIM, D), (HEADS * HEAD_DIM) ** -0.5, 0.125, ((0, 2),))
    prefix_kv = draw_prefix_kv(jax.random.fold_in(splits[18], 71), 0)
    prefix_owner = draw_prefix_owner(jax.random.fold_in(splits[18], 71), 0)
    prefix_start = draw_prefix_start(jax.random.fold_in(splits[18], 71), 0)
    prefix_len = draw_prefix_len(jax.random.fold_in(splits[18], 71), 0)
    mlp_gain = jnp.clip(jnp.exp(jax.random.uniform(splits[10], (D,), jnp.float32, math.log(0.25), math.log(2.5))), 0.25, 2.5)
    shared_in = scatter_about(splits[11], (D, 2, SHARED * FF), D ** -0.5, 0.125, ((2, 2),))
    shared_out = scatter_about(splits[12], (SHARED * FF, D), (SHARED * FF) ** -0.5, 0.15625, ((0, 2),))
    expert_in = scatter_about(splits[13], (EXPERTS, D, 2, FF), D ** -0.5, 0.125, ((0, 16), (3, 2)))
    expert_out = scatter_about(splits[14], (EXPERTS, FF, D), FF ** -0.5, 0.15625, ((0, 16), (1, 2)))
    expert_ids_keys = jax.random.split(jax.random.fold_in(splits[15], 1), REQS * LEAF_LEN // (R_DEV * LEAF_LEN))
    expert_ids_turns = jax.random.permutation(jax.random.fold_in(splits[15], 3), REQS * LEAF_LEN // (R_DEV * LEAF_LEN))
    expert_ids = jax.vmap(lambda own, number: deal_out(jax.random.fold_in(splits[15], 2), own, number, R_DEV * LEAF_LEN, EXPERTS, TOPK, CAP_E, 1))(expert_ids_keys, expert_ids_turns).reshape((REQS, LEAF_LEN, TOPK))
    gate_weights = jnp.clip(0.05 + 0.35 * jax.random.uniform(splits[16], (REQS, LEAF_LEN, TOPK), jnp.float32) ** levels(splits[16], (REQS, LEAF_LEN, TOPK), ((0, 16),), -0.2, 0.2), 0.05, 0.4)
    request_of = draw_request_of(jax.random.fold_in(splits[18], 71), 0)
    return {"leaf_tokens": leaf_tokens, "attn_gain": attn_gain, "w_query": w_query, "w_key": w_key, "w_value": w_value, "w_out": w_out, "prefix_kv": prefix_kv, "prefix_owner": prefix_owner, "prefix_start": prefix_start, "prefix_len": prefix_len, "mlp_gain": mlp_gain, "shared_in": shared_in, "shared_out": shared_out, "expert_in": expert_in, "expert_out": expert_out, "expert_ids": expert_ids, "gate_weights": gate_weights, "request_of": request_of}


EPS = 1e-06
ROPE_BASE = 10000.0

def rms_scaled(values, gain_vector):
    mean_square = lax.optimization_barrier(jnp.mean(values * values, axis=-1, keepdims=True))
    return values * lax.rsqrt(mean_square + EPS) * gain_vector

def rotate_heads(values, positions):
    head_dim = values.shape[-1]
    half_dim = head_dim // 2
    frequency = ROPE_BASE ** (-2.0 * jnp.arange(half_dim, dtype=jnp.float32) / head_dim)
    angles = positions[..., None, None] * frequency
    cosine = jnp.cos(angles)
    sine_part = jnp.sin(angles)
    first_half = values[..., :half_dim]
    second_half = values[..., half_dim:]
    return jnp.concatenate([first_half * cosine - second_half * sine_part, second_half * cosine + first_half * sine_part], axis=-1)

def softmax_parts(scores, visible):
    scores = jnp.where(visible, scores, -jnp.inf)
    highest = lax.optimization_barrier(jnp.max(scores, axis=-1, keepdims=True))
    anchor = jnp.where(jnp.isfinite(highest), highest, 0.0)
    weights = jnp.exp(scores - anchor)
    totals = lax.optimization_barrier(jnp.sum(weights, axis=-1, keepdims=True))
    return (weights, anchor, totals)

def rounded_weights(weights):
    return lax.optimization_barrier(weights.astype(jnp.bfloat16)).astype(jnp.float32)

def merge_parts(outputs, log_totals):
    stacked = jnp.stack(log_totals, axis=0)
    highest = lax.optimization_barrier(jnp.max(stacked, axis=0))
    scales = jnp.exp(stacked - highest)
    weighted = scales[0][..., None] * outputs[0]
    for part_index in range(1, len(outputs)):
        weighted = weighted + scales[part_index][..., None] * outputs[part_index]
    return weighted / lax.optimization_barrier(jnp.sum(scales, axis=0))[..., None]

def reference(leaf_tokens, attn_gain, w_query, w_key, w_value, w_out, prefix_kv, prefix_owner, prefix_start, prefix_len, mlp_gain, shared_in, shared_out, expert_in, expert_out, expert_ids, gate_weights, request_of):
    token_count = REQS * LEAF_LEN
    head_width = HEADS * HEAD_DIM
    score_scale = HEAD_DIM ** (-0.5)
    residual = leaf_tokens.astype(jnp.float32)
    normed_attn = rms_scaled(residual, attn_gain).astype(jnp.bfloat16).reshape(token_count, D)
    positions = lax.optimization_barrier(jnp.sum(prefix_len, axis=1)).astype(jnp.float32)[:, None] + jnp.arange(LEAF_LEN, dtype=jnp.float32)[None, :]

    def project(weight):
        return jnp.dot(normed_attn, weight, preferred_element_type=jnp.float32).reshape(REQS, LEAF_LEN, HEADS, HEAD_DIM)
    queries = rotate_heads(project(w_query), positions).astype(jnp.bfloat16)
    key_rows = rotate_heads(project(w_key), positions).astype(jnp.bfloat16)
    leaf_values = project(w_value).astype(jnp.bfloat16)
    windows = (MAX1, MAX2, MAX3)
    causal = jnp.arange(LEAF_LEN)[:, None] >= jnp.arange(LEAF_LEN)[None, :]

    def attend(request):
        query_rows = queries[request].astype(jnp.float32)
        scores = jnp.einsum('ihd,jhd->hij', query_rows, key_rows[request].astype(jnp.float32)) * score_scale
        weights, anchor, totals = softmax_parts(scores, causal[None])
        mixed_leaf = jnp.einsum('hij,jhd->ihd', rounded_weights(weights), leaf_values[request].astype(jnp.float32))
        outputs = [mixed_leaf / jnp.transpose(totals, (1, 0, 2))]
        log_totals = [jnp.transpose(anchor + jnp.log(totals), (1, 0, 2))[..., 0]]
        zero_index = jnp.zeros((), jnp.int32)
        for tree_level in range(3):
            node_begin = (prefix_owner[request, tree_level] * POOL_DEV + prefix_start[request, tree_level]).astype(jnp.int32)
            node_window = lax.dynamic_slice(prefix_kv, (zero_index, node_begin, zero_index), (2, windows[tree_level], head_width))
            node_window = node_window.astype(jnp.float32).reshape(2, windows[tree_level], HEADS, HEAD_DIM)
            scores = jnp.einsum('ihd,khd->hik', query_rows, node_window[0]) * score_scale
            visible = jnp.arange(windows[tree_level]) < prefix_len[request, tree_level]
            weights, anchor, totals = softmax_parts(scores, visible[None, None, :])
            mixed_level = jnp.einsum('hik,khd->ihd', rounded_weights(weights), node_window[1])
            outputs.append(mixed_level / jnp.transpose(totals, (1, 0, 2)))
            log_totals.append(jnp.transpose(anchor + jnp.log(totals), (1, 0, 2))[..., 0])
        return merge_parts(outputs, log_totals).astype(jnp.bfloat16).reshape(LEAF_LEN, head_width)
    attended = lax.map(attend, jnp.arange(REQS))
    attn_sum = jnp.dot(attended.reshape(token_count, head_width), w_out, preferred_element_type=jnp.float32)
    residual_mid = residual + attn_sum.reshape(REQS, LEAF_LEN, D)
    normed_mlp = rms_scaled(residual_mid, mlp_gain).astype(jnp.bfloat16).reshape(token_count, D)
    shared_width = SHARED * FF
    gate_up = jnp.dot(normed_mlp, shared_in.reshape(D, 2 * shared_width), preferred_element_type=jnp.float32)
    shared_hidden = (jax.nn.silu(gate_up[:, :shared_width]) * gate_up[:, shared_width:]).astype(jnp.bfloat16)
    shared_part = jnp.dot(shared_hidden, shared_out, preferred_element_type=jnp.float32)
    flat_ids = expert_ids.reshape(token_count, TOPK)
    flat_gates = gate_weights.reshape(token_count, TOPK)
    most_rows = N_DP * CAP_E
    slice_width = FF // N_TENSOR

    def add_expert(routed, expert):
        hit_mask = flat_ids == expert
        gate_sum = lax.optimization_barrier(jnp.sum(jnp.where(hit_mask, flat_gates, 0.0), axis=1))
        member = jnp.any(hit_mask, axis=1)
        chosen = jnp.nonzero(member, size=most_rows, fill_value=0)[0]
        present = (jnp.arange(most_rows) < jnp.sum(member.astype(jnp.int32))).astype(jnp.float32)
        inputs = normed_mlp[chosen]
        weight_in = expert_in[expert]
        weight_back = expert_out[expert]
        expert_value = jnp.zeros((most_rows, D), jnp.float32)
        for part_index in range(N_TENSOR):
            first_unit = part_index * slice_width
            gate_part = jnp.dot(inputs, weight_in[:, 0, first_unit:first_unit + slice_width], preferred_element_type=jnp.float32)
            up_part = jnp.dot(inputs, weight_in[:, 1, first_unit:first_unit + slice_width], preferred_element_type=jnp.float32)
            slice_hidden = (jax.nn.silu(gate_part) * up_part).astype(jnp.bfloat16)
            slice_out = jnp.dot(slice_hidden, weight_back[first_unit:first_unit + slice_width], preferred_element_type=jnp.float32).astype(jnp.bfloat16)
            expert_value = expert_value + lax.optimization_barrier(slice_out).astype(jnp.float32)
        routed = routed.at[chosen].add(expert_value * (gate_sum[chosen] * present)[:, None])
        return (routed, None)
    routed = lax.scan(add_expert, jnp.zeros((token_count, D), jnp.float32), jnp.arange(EXPERTS))[0]
    mixed_rows = (residual_mid.reshape(token_count, D) + shared_part + routed).astype(jnp.bfloat16).reshape(REQS, LEAF_LEN, D)
    return jnp.zeros_like(mixed_rows).at[request_of].set(mixed_rows)
```

```python
import functools

import jax
import jax.numpy as jnp
from jax import lax
from jax.experimental import pallas as pl
from jax.experimental.pallas import tpu as pltpu
from jax.sharding import PartitionSpec as P

HEAD_DIM = 128
EPS = 1e-06
ROPE_BASE = 10000.0
LANES = 128
HIDE = -1e30
LOG2E = 1.4426950408889634
LN2 = 0.6931471805599453
MIB = 1 << 20

f32 = jnp.float32
bf16 = jnp.bfloat16


def dot(a, b):
    return lax.dot_general(a, b, (((1,), (0,)), ((), ())), preferred_element_type=f32)


def dot_nt(a, b):
    return lax.dot_general(a, b, (((1,), (1,)), ((), ())), preferred_element_type=f32)


def iota(shape, dim):
    return lax.broadcasted_iota(jnp.int32, shape, dim).astype(f32)


def divided(index, by):
    quotient = jnp.floor((index + 0.5) * (1.0 / by))
    return quotient, index - by * quotient


def one_hot(condition):
    return jnp.where(condition, 1.0, 0.0).astype(bf16)


def rms(values, gain):
    mean_square = jnp.mean(values * values, axis=-1, keepdims=True)
    return (values * lax.rsqrt(mean_square + EPS) * gain).astype(bf16)


def ring_get(piece, count):
    pieces = [piece]
    for step in range(1, count):
        pieces.append(
            lax.ppermute(piece, "tensor", [((i + step) % count, i) for i in range(count)])
        )
    return pieces


def ring_send(pieces):
    count = len(pieces)
    arrived = [pieces[0]]
    for step in range(1, count):
        arrived.append(
            lax.ppermute(pieces[step], "tensor", [(i, (i + step) % count) for i in range(count)])
        )
    return arrived


def exchange(rows, groups):
    blocks = rows.reshape(groups, rows.shape[0] // groups, rows.shape[1])
    return lax.all_to_all(blocks, "dp", split_axis=0, concat_axis=0, tiled=True).reshape(rows.shape)


def whole():
    return pl.BlockSpec(memory_space=pltpu.VMEM)


def scalar():
    return pl.BlockSpec(memory_space=pltpu.SMEM)


def params(mib, grid=0):
    return pltpu.CompilerParams(
        vmem_limit_bytes=mib * MIB,
        dimension_semantics=("arbitrary",) * grid if grid else None,
    )


def cost(flops, nbytes):
    return pl.CostEstimate(flops=int(flops), bytes_accessed=int(nbytes), transcendentals=0)


def routing_kernel(
    table_ref, ids_ref, gates_ref,
    place_ref, meta_ref, pick_ref, send_ref, high_ref, low_ref, final_ref,
    *, requests, leaf_len, groups, capacity, experts,
):
    items = 3 * requests
    rows = requests * leaf_len
    table = table_ref[...].astype(f32)
    owner, start, length = table[0:1], table[1:2], table[2:3]
    dest, place = table[3:4, :requests], table[4:5, :requests]
    down, across = iota((items, items), 0), iota((items, items), 1)
    owner_down = jnp.sum(jnp.where(down == across, owner, 0.0), axis=1, keepdims=True)
    earlier = jnp.where((owner_down == owner) & (down < across), 1.0, 0.0)
    slot = owner * 2.0 + jnp.sum(earlier, axis=0, keepdims=True)
    slot_rows = groups * 2 * leaf_len
    row_slot, row_token = divided(iota((slot_rows, 1), 0), leaf_len)
    request_of_row, token_of_row = divided(iota((1, rows), 1), leaf_len)
    named = slot == row_slot
    _, item_request = divided(iota((items, 1), 0), requests)
    placed = dot(one_hot(named), one_hot(item_request == request_of_row))
    place_ref[...] = jnp.where(row_token == token_of_row, placed, 0.0).astype(bf16)

    first_key = jnp.sum(jnp.where(named, start, 0.0), axis=1, keepdims=True)
    key_count = jnp.sum(jnp.where(named, length, 0.0), axis=1, keepdims=True)
    row_group, _ = divided(row_slot, 2)
    tag = jnp.sum(jnp.where(dest == row_group, place + 1.0, 0.0), axis=1, keepdims=True)
    lane = iota((1, LANES), 1)
    meta = jnp.zeros((slot_rows, LANES), f32)
    for at, value in enumerate(divided(first_key, 32) + divided(key_count, 32) + (tag,)):
        meta = jnp.where(lane == at, value, meta)
    meta_ref[...] = meta.astype(bf16)

    row_request, row_place = divided(iota((rows, 1), 0), leaf_len)
    item_across = iota((1, items), 1)
    slot_across, token_across = divided(iota((1, slot_rows), 1), leaf_len)
    for level in range(3):
        mine = item_across == row_request + level * requests
        slot_down = jnp.sum(jnp.where(mine, slot, 0.0), axis=1, keepdims=True)
        pick_ref[level] = one_hot((slot_down == slot_across) & (row_place == token_across))

    ids = ids_ref[...].astype(f32)
    gates = gates_ref[...]
    expert_down = iota((experts, 1), 0)
    member = jnp.zeros((experts, rows), f32)
    gate = jnp.zeros((experts, rows), f32)
    for choice in range(ids.shape[0]):
        hit = ids[choice : choice + 1] == expert_down
        member = member + jnp.where(hit, 1.0, 0.0)
        gate = gate + jnp.where(hit, gates[choice : choice + 1], 0.0)
    ahead = one_hot(iota((rows, rows), 0) < iota((rows, rows), 1))
    member = member.astype(bf16)
    before = dot(member, ahead).astype(bf16)
    slots = experts * capacity
    slot_expert, slot_place = divided(iota((slots, 1), 0), capacity)
    spread = one_hot(slot_expert == iota((1, experts), 1))
    taken = (dot(spread, member) > 0.5) & (dot(spread, before) == slot_place)
    send_ref[...] = one_hot(taken)
    high = gate.astype(bf16)
    low = (gate - high.astype(f32)).astype(bf16)
    for part, ref in ((high, high_ref), (low, low_ref)):
        ref[...] = jnp.transpose(jnp.where(taken, dot(spread, part), 0.0)).astype(bf16)

    final_rows = groups * leaf_len
    final_group, final_token = divided(iota((final_rows, 1), 0), leaf_len)
    going = dot(
        one_hot(dest == final_group),
        one_hot(iota((requests, 1), 0) == request_of_row),
    )
    final_ref[...] = jnp.where(final_token == token_of_row, going, 0.0).astype(bf16)


def rotated(product, cosine, sine, heads):
    columns = []
    for head in range(heads):
        part = product[:, head * HEAD_DIM : (head + 1) * HEAD_DIM]
        columns.append(part * cosine + pltpu.roll(part, HEAD_DIM // 2, 1) * sine)
    return jnp.concatenate(columns, axis=1).astype(bf16)


def query_kernel(*refs, tensors, heads):
    index_ref, pieces, refs = refs[0], refs[1 : 1 + tensors], refs[1 + tensors :]
    (gain_ref, weight_ref, cos_ref, sin_ref, place_ref, meta_ref,
     raw_ref, normed_ref, query_ref, send_ref, rows_ref) = refs
    step = pl.program_id(0)
    shard = pieces[0].shape[0]

    @pl.when(step == 0)
    def _():
        for at, piece in enumerate(pieces):
            owner = lax.rem(index_ref[0] + at, tensors)
            rows_ref[pl.ds(pl.multiple_of(owner * shard, shard), shard), :] = piece[...]
        raw_ref[...] = rows_ref[...]
        normed_ref[...] = rms(rows_ref[...].astype(f32), gain_ref[...])
        send_ref[:, send_ref.shape[1] - LANES :] = meta_ref[...]

    product = dot(normed_ref[...], weight_ref[...])
    query = rotated(product, cos_ref[...], sin_ref[...], heads)
    query_ref[...] = query
    width = heads * HEAD_DIM
    send_ref[:, pl.ds(pl.multiple_of(step * width, width), width)] = dot(
        place_ref[...], query
    ).astype(bf16)


def leaf_kernel(
    normed_ref, query_ref, key_ref, value_ref, cos_ref, sin_ref, out_ref, lse_ref,
    *, heads, leaf_len, scale,
):
    step = pl.program_id(0)
    normed = normed_ref[...]
    rows = normed.shape[0]
    keys = rotated(dot(normed, key_ref[...]), cos_ref[...], sin_ref[...], heads)
    values = dot(normed, value_ref[...]).astype(bf16)
    down, across = iota((rows, 1), 0), iota((1, rows), 1)
    visible = (divided(down, leaf_len)[0] == divided(across, leaf_len)[0]) & (across <= down)
    lane = lax.broadcasted_iota(jnp.int32, (1, LANES), 1)

    @pl.when(step == 0)
    def _():
        lse_ref[...] = jnp.zeros_like(lse_ref)

    for head in range(heads):
        at = slice(head * HEAD_DIM, (head + 1) * HEAD_DIM)
        scores = jnp.where(visible, dot_nt(query_ref[:, at], keys[:, at]) * scale, HIDE)
        highest = jnp.max(scores, axis=1, keepdims=True)
        weights = jnp.exp(scores - highest)
        total = jnp.sum(weights, axis=1, keepdims=True)
        out_ref[:, at] = dot(weights.astype(bf16), values[:, at]) / total
        lse = highest + jnp.log(total)
        lse_ref[...] = jnp.where(lane == step * heads + head, lse, lse_ref[...])


def owner_kernel(
    query_ref, meta_ref, kv_ref, back_ref, bias_ref, lse_ref, *, heads, all_heads, scale
):
    step = pl.program_id(0)
    rows, keys = bias_ref.shape
    width = heads * HEAD_DIM
    lane = lax.broadcasted_iota(jnp.int32, (1, LANES), 1)

    @pl.when(step == 0)
    def _():
        meta = meta_ref[...].astype(f32)
        first = meta[:, 0:1] * 32.0 + meta[:, 1:2]
        last = first + meta[:, 2:3] * 32.0 + meta[:, 3:4]
        key = iota((1, keys), 1)
        bias_ref[...] = jnp.where((key >= first) & (key < last), 0.0, HIDE)
        lse_ref[...] = jnp.zeros_like(lse_ref)

    chunk = 64
    for head in range(heads):
        at = slice(head * HEAD_DIM, (head + 1) * HEAD_DIM)
        here = lane == step * heads + head
        there = lane == step * heads + head + all_heads
        for low in range(0, rows, chunk):
            part = slice(low, low + chunk)
            scores = dot_nt(query_ref[part, at], kv_ref[0, :, at]) * (scale * LOG2E)
            scores = scores + bias_ref[part, :]
            highest = jnp.max(scores, axis=1, keepdims=True)
            weights = jnp.exp2(scores - highest)
            total = jnp.sum(weights, axis=1, keepdims=True)
            out = dot(weights.astype(bf16), kv_ref[1, :, at]) / total
            lane_at = pl.multiple_of(step * width + head * HEAD_DIM, HEAD_DIM)
            back_ref[part, pl.ds(lane_at, HEAD_DIM)] = out.astype(bf16)
            lse = highest * LN2 + jnp.log(total)
            lse_high = lse.astype(bf16).astype(f32)
            kept = jnp.where(here, lse_high, lse_ref[part, :])
            lse_ref[part, :] = jnp.where(there, lse - lse_high, kept)

    @pl.when(step == pl.num_programs(0) - 1)
    def _():
        back_ref[:, back_ref.shape[1] - LANES :] = lse_ref[...].astype(bf16)


def merge_kernel(back_ref, pick_ref, leaf_ref, lse_ref, weight_ref, out_ref, attended_ref, *, heads):
    width = heads * HEAD_DIM

    @pl.when(pl.program_id(0) == 0)
    def _():
        back = back_ref[...]
        outputs, sums = [leaf_ref[...]], [lse_ref[...]]
        for level in range(3):
            rows = dot(pick_ref[level], back)
            outputs.append(rows[:, :width])
            tail = rows[:, width:]
            sums.append(tail + pltpu.roll(tail, LANES - heads, 1))
        highest = functools.reduce(jnp.maximum, sums)
        scales = [jnp.exp(one - highest) for one in sums]
        total = sum(scales[1:], scales[0])
        scales = [one / total for one in scales]
        for head in range(heads):
            at = slice(head * HEAD_DIM, (head + 1) * HEAD_DIM)
            mixed = sum(
                scales[i][:, head : head + 1] * outputs[i][:, at] for i in range(4)
            )
            attended_ref[:, at] = mixed.astype(bf16)

    out_ref[...] = dot(attended_ref[...], weight_ref[...]).astype(bf16)


def middle_kernel(*refs, tensors):
    index_ref, raw_ref, gain_ref, send_ref = refs[:4]
    pieces = refs[4 : 4 + tensors]
    normed_ref, own_ref, rows_ref, resid_ref = refs[4 + tensors :]
    width = own_ref.shape[1]
    own = pl.ds(pl.multiple_of(index_ref[0] * width, width), width)
    total = raw_ref[...].astype(f32)
    for piece in pieces:
        total = total + piece[...].astype(f32)
    resid_ref[...] = total
    own_ref[...] = resid_ref[:, own]
    normed_ref[...] = rms(total, gain_ref[...])
    rows_ref[...] = dot(send_ref[...], normed_ref[:, own]).astype(bf16)


def shared_kernel(*refs, tensors):
    index_ref, rows_ref, in_ref, down_ref = refs[:4]
    pieces, total_ref = refs[4 : 4 + tensors], refs[4 + tensors]
    rows = rows_ref[...]
    gate = dot_nt(rows, in_ref[0])
    up = dot_nt(rows, in_ref[1])
    hidden = (gate / (1.0 + jnp.exp(-gate)) * up).astype(bf16)
    total_ref[...] = dot(hidden, down_ref[...])
    width = pieces[0].shape[1]
    for at, piece in enumerate(pieces):
        column = lax.rem(index_ref[0] + at, tensors) * width
        piece[...] = total_ref[:, pl.ds(pl.multiple_of(column, width), width)].astype(bf16)


def expert_kernel(*refs, tensors, experts, capacity):
    index_ref, arrived, refs = refs[0], refs[1 : 1 + tensors], refs[1 + tensors :]
    in_ref, down_ref, refs = refs[0], refs[1], refs[2:]
    pieces, rows_ref, total_ref = refs[:tensors], refs[tensors], refs[tensors + 1]
    expert = pl.program_id(0)
    groups, _, width = arrived[0].shape
    count = groups * capacity

    @pl.when(expert == 0)
    def _():
        for at, piece in enumerate(arrived):
            column = lax.rem(index_ref[0] + at, tensors) * width
            columns = pl.ds(pl.multiple_of(column, width), width)
            values = piece[...].astype(f32)
            for e in range(experts):
                mine = values[:, e * capacity : (e + 1) * capacity, :].reshape(count, width)
                rows_ref[e, :, columns] = mine.astype(bf16)

    rows = rows_ref[expert]
    gate = dot_nt(rows, in_ref[0, 0])
    up = dot_nt(rows, in_ref[0, 1])
    hidden = (gate / (1.0 + jnp.exp(-gate)) * up).astype(bf16)
    value = dot(hidden, down_ref[0])
    at = pl.ds(pl.multiple_of(expert * capacity, capacity), capacity)
    total_ref[:, at, :] = value.reshape(groups, capacity, value.shape[1])

    @pl.when(expert == experts - 1)
    def _():
        for at, piece in enumerate(pieces):
            column = lax.rem(index_ref[0] + at, tensors) * width
            columns = pl.ds(pl.multiple_of(column, width), width)
            piece[...] = total_ref[:, :, columns].astype(bf16)


def combine_kernel(*refs, tensors):
    returned_ref, high_ref, low_ref, resid_ref, final_ref = refs[:5]
    shared, out_ref = refs[5 : 5 + tensors], refs[5 + tensors]
    returned = returned_ref[...]
    total = resid_ref[...]
    for piece in shared:
        total = total + piece[...].astype(f32)
    total = total + dot(high_ref[...], returned) + dot(low_ref[...], returned)
    out_ref[...] = dot(final_ref[...], total.astype(bf16)).astype(bf16)


def settle_kernel(*refs, tensors, leaf_len):
    index_ref, meta_ref, rows_ref = refs[:3]
    pieces = refs[3:]
    slot_rows, final_rows = meta_ref.shape[0], rows_ref.shape[0]
    places = pieces[0].shape[0]
    share = leaf_len // tensors
    tag_down = meta_ref[...].astype(f32)[:, 4:5]
    group, token = divided(iota((1, final_rows), 1), leaf_len)
    source = iota((slot_rows, 1), 0) == group * (2.0 * leaf_len) + token
    tag = jnp.sum(jnp.where(source, tag_down, 0.0), axis=0, keepdims=True)
    request, position = divided(iota((places, 1), 0), share)
    for at, piece in enumerate(pieces):
        shift = (lax.rem(index_ref[0] + at, tensors) * share).astype(f32)
        chosen = one_hot((tag == request + 1.0) & (token == position + shift))
        piece[...] = dot(chosen, rows_ref[...]).astype(bf16)


def on_device(
    leaf_tokens,
    attn_gain,
    w_query,
    w_key,
    w_value,
    w_out,
    prefix_kv,
    prefix_owner,
    prefix_start,
    prefix_len,
    mlp_gain,
    shared_in,
    shared_out,
    expert_in,
    expert_out,
    expert_ids,
    gate_weights,
    request_of,
):
    groups = lax.axis_size("dp")
    tensors = lax.axis_size("tensor")
    index = lax.axis_index("tensor").astype(jnp.int32).reshape(1)
    shard_requests, leaf_len, model_width = leaf_tokens.shape
    requests = prefix_owner.shape[0]
    rows = requests * leaf_len
    local_width = w_query.shape[1]
    local_heads = local_width // HEAD_DIM
    scale = HEAD_DIM ** (-0.5)
    column_share = model_width // tensors
    top_count = expert_ids.shape[2]
    local_experts = expert_in.shape[0]
    experts = local_experts * groups
    assignments = rows * top_count
    capacity = tensors * max(1, assignments * 4 // (experts * 3 * tensors))
    slots = experts * capacity
    slot_rows = groups * 2 * leaf_len
    final_rows = groups * leaf_len
    shape = jax.ShapeDtypeStruct

    raw_pieces = ring_get(leaf_tokens.reshape(shard_requests * leaf_len, model_width), tensors)

    pad = ((0, 0), (0, 2 * requests))
    table = jnp.concatenate(
        [
            prefix_owner.T.reshape(1, -1),
            prefix_start.T.reshape(1, -1),
            prefix_len.T.reshape(1, -1),
            jnp.pad((request_of // requests).reshape(1, -1), pad),
            jnp.pad((request_of % requests).reshape(1, -1), pad),
        ],
        axis=0,
    )
    ids = jnp.transpose(expert_ids, (2, 0, 1)).reshape(top_count, rows)
    gates = jnp.transpose(gate_weights, (2, 0, 1)).reshape(top_count, rows)
    place, meta, pick, send, gate_high, gate_low, final = pl.pallas_call(
        functools.partial(
            routing_kernel, requests=requests, leaf_len=leaf_len, groups=groups,
            capacity=capacity, experts=experts,
        ),
        out_shape=[
            shape((slot_rows, rows), bf16),
            shape((slot_rows, LANES), bf16),
            shape((3, rows, slot_rows), bf16),
            shape((slots, rows), bf16),
            shape((rows, slots), bf16),
            shape((rows, slots), bf16),
            shape((final_rows, rows), bf16),
        ],
        in_specs=[whole()] * 3,
        out_specs=[whole()] * 7,
        compiler_params=params(24),
        name="routing",
    )(table, ids, gates)

    offsets = jnp.sum(prefix_len, axis=1).astype(f32)
    positions = (offsets[:, None] + jnp.arange(leaf_len, dtype=f32)[None, :]).reshape(rows, 1)
    half = HEAD_DIM // 2
    frequency = ROPE_BASE ** (-2.0 * jnp.arange(half, dtype=f32) / HEAD_DIM)
    angles = positions * frequency[None, :]
    cosine = jnp.concatenate([jnp.cos(angles)] * 2, axis=1)
    sine = jnp.concatenate([-jnp.sin(angles), jnp.sin(angles)], axis=1)

    step_heads = min(2, local_heads)
    step_width = step_heads * HEAD_DIM
    steps = local_heads // step_heads
    fixed = lambda *dims: pl.BlockSpec(dims, lambda i: (0,) * len(dims))
    columns = lambda *dims: pl.BlockSpec(dims, lambda i: (0,) * (len(dims) - 1) + (i,))
    send_width = local_width + LANES
    shard_rows = shard_requests * leaf_len
    raw, normed, query, query_send = pl.pallas_call(
        functools.partial(query_kernel, tensors=tensors, heads=step_heads),
        grid=(steps,),
        out_shape=[
            shape((rows, model_width), bf16),
            shape((rows, model_width), bf16),
            shape((rows, local_width), bf16),
            shape((slot_rows, send_width), bf16),
        ],
        in_specs=[scalar()]
        + [fixed(shard_rows, model_width)] * tensors
        + [
            fixed(1, model_width),
            columns(model_width, step_width),
            fixed(rows, LANES),
            fixed(rows, LANES),
            fixed(slot_rows, rows),
            fixed(slot_rows, LANES),
        ],
        out_specs=[
            fixed(rows, model_width),
            fixed(rows, model_width),
            columns(rows, step_width),
            fixed(slot_rows, send_width),
        ],
        scratch_shapes=[pltpu.VMEM((rows, model_width), bf16)],
        compiler_params=params(24, 1),
        cost_estimate=cost(2 * rows * model_width * local_width, 2 * model_width * local_width),
        name="queries",
    )(
        index, *raw_pieces, attn_gain.reshape(1, -1), w_query, cosine, sine, place, meta
    )

    query_arrived = exchange(query_send, groups)

    leaf_out, leaf_lse = pl.pallas_call(
        functools.partial(leaf_kernel, heads=step_heads, leaf_len=leaf_len, scale=scale),
        grid=(steps,),
        out_shape=[shape((rows, local_width), f32), shape((rows, LANES), f32)],
        in_specs=[
            fixed(rows, model_width),
            columns(rows, step_width),
            columns(model_width, step_width),
            columns(model_width, step_width),
            fixed(rows, LANES),
            fixed(rows, LANES),
        ],
        out_specs=[columns(rows, step_width), fixed(rows, LANES)],
        compiler_params=params(24, 1),
        cost_estimate=cost(4 * rows * model_width * local_width, 4 * model_width * local_width),
        name="leaf",
    )(normed, query, w_key, w_value, cosine, sine)

    pool = prefix_kv.shape[1]
    back_send = pl.pallas_call(
        functools.partial(owner_kernel, heads=step_heads, all_heads=local_heads, scale=scale),
        grid=(steps,),
        out_shape=shape((slot_rows, send_width), bf16),
        in_specs=[
            columns(slot_rows, step_width),
            pl.BlockSpec((slot_rows, LANES), lambda i: (0, local_heads)),
            columns(2, pool, step_width),
        ],
        out_specs=fixed(slot_rows, send_width),
        scratch_shapes=[pltpu.VMEM((slot_rows, pool), f32), pltpu.VMEM((slot_rows, LANES), f32)],
        compiler_params=params(32, 1),
        cost_estimate=cost(4 * slot_rows * pool * local_width, 4 * pool * local_width),
        name="owner",
    )(query_arrived, query_arrived, prefix_kv)

    back = exchange(back_send, groups)

    out_step = min(512, model_width)
    partial_out = pl.pallas_call(
        functools.partial(merge_kernel, heads=local_heads),
        grid=(model_width // out_step,),
        out_shape=shape((rows, model_width), bf16),
        in_specs=[
            fixed(slot_rows, send_width),
            fixed(3, rows, slot_rows),
            fixed(rows, local_width),
            fixed(rows, LANES),
            columns(local_width, out_step),
        ],
        out_specs=columns(rows, out_step),
        scratch_shapes=[pltpu.VMEM((rows, local_width), bf16)],
        compiler_params=params(24, 1),
        cost_estimate=cost(2 * rows * local_width * model_width, 2 * local_width * model_width),
        name="merge",
    )(back, pick, leaf_out, leaf_lse, w_out)

    out_pieces = ring_get(partial_out, tensors)

    normed_mlp, resid_own, send_rows = pl.pallas_call(
        functools.partial(middle_kernel, tensors=tensors),
        out_shape=[
            shape((rows, model_width), bf16),
            shape((rows, column_share), f32),
            shape((slots, column_share), bf16),
        ],
        in_specs=[scalar()] + [whole()] * (3 + tensors),
        out_specs=[whole()] * 3,
        scratch_shapes=[pltpu.VMEM((rows, model_width), f32)],
        compiler_params=params(24),
        cost_estimate=cost(2 * slots * rows * column_share, 4 * slots * column_share),
        name="middle",
    )(index, raw, mlp_gain.reshape(1, -1), send, *out_pieces)

    arrived = exchange(send_rows, groups)

    hidden = shared_out.shape[0]
    shared_pieces = pl.pallas_call(
        functools.partial(shared_kernel, tensors=tensors),
        out_shape=[shape((rows, column_share), bf16)] * tensors,
        in_specs=[scalar()] + [whole()] * 3,
        out_specs=[whole()] * tensors,
        scratch_shapes=[pltpu.VMEM((rows, model_width), f32)],
        compiler_params=params(24),
        cost_estimate=cost(6 * rows * hidden * model_width, 6 * hidden * model_width),
        name="shared",
    )(index, normed_mlp, jnp.transpose(shared_in, (1, 2, 0)), shared_out)
    shared_pieces = ring_send(shared_pieces)

    block = local_experts * capacity
    arrived_pieces = ring_get(arrived.reshape(groups, block, column_share), tensors)
    expert_hidden = expert_out.shape[1]
    partial_pieces = pl.pallas_call(
        functools.partial(
            expert_kernel, tensors=tensors, experts=local_experts, capacity=capacity
        ),
        grid=(local_experts,),
        out_shape=[shape((groups, block, column_share), bf16)] * tensors,
        in_specs=[scalar()]
        + [fixed(groups, block, column_share)] * tensors
        + [
            pl.BlockSpec((1, 2, expert_hidden, model_width), lambda i: (i, 0, 0, 0)),
            pl.BlockSpec((1, expert_hidden, model_width), lambda i: (i, 0, 0)),
        ],
        out_specs=[fixed(groups, block, column_share)] * tensors,
        scratch_shapes=[
            pltpu.VMEM((local_experts, groups * capacity, model_width), bf16),
            pltpu.VMEM((groups, block, model_width), f32),
        ],
        compiler_params=params(48, 1),
        cost_estimate=cost(
            6 * slots * expert_hidden * model_width,
            6 * local_experts * expert_hidden * model_width,
        ),
        name="experts",
    )(index, *arrived_pieces, jnp.transpose(expert_in, (0, 2, 3, 1)), expert_out)
    partial_pieces = ring_send(partial_pieces)
    summed = sum(piece.astype(f32) for piece in partial_pieces).astype(bf16)

    returned = exchange(summed.reshape(slots, column_share), groups)

    final_send = pl.pallas_call(
        functools.partial(combine_kernel, tensors=tensors),
        out_shape=shape((final_rows, column_share), bf16),
        in_specs=[whole()] * (5 + tensors),
        out_specs=whole(),
        compiler_params=params(24),
        name="combine",
    )(returned, gate_high, gate_low, resid_own, final, *shared_pieces)

    final_arrived = exchange(final_send, groups)

    places = requests * (leaf_len // tensors)
    settled = pl.pallas_call(
        functools.partial(settle_kernel, tensors=tensors, leaf_len=leaf_len),
        grid=(1,),
        out_shape=[shape((places, column_share), bf16)] * tensors,
        in_specs=[
            scalar(),
            pl.BlockSpec((slot_rows, LANES), lambda i: (0, local_heads)),
            fixed(final_rows, column_share),
        ],
        out_specs=[fixed(places, column_share)] * tensors,
        compiler_params=params(24, 1),
        name="settle",
    )(index, query_arrived, final_arrived)
    settled = ring_send(settled)
    if tensors == 2:
        first = index[0] == 0
        own, other = settled
        result = jnp.concatenate(
            [jnp.where(first, own, other), jnp.where(first, other, own)], axis=1
        )
    else:
        result = jnp.zeros((places, model_width), bf16)
        for at, piece in enumerate(settled):
            column = ((index[0] - at + tensors) % tensors) * column_share
            result = lax.dynamic_update_slice(result, piece, (0, column))
    return result.reshape(requests, leaf_len // tensors, model_width)


def solution(mesh):
    in_specs = (
        P(("dp", "tensor"), None, None),
        P(),
        P(None, "tensor"),
        P(None, "tensor"),
        P(None, "tensor"),
        P("tensor", None),
        P(None, "dp", "tensor"),
        P("dp", None),
        P("dp", None),
        P("dp", None),
        P(),
        P(None, None, "tensor"),
        P("tensor", None),
        P("dp", None, None, "tensor"),
        P("dp", "tensor", None),
        P("dp", None, None),
        P("dp", None, None),
        P("dp"),
    )
    out_specs = P("dp", "tensor", None)
    return jax.shard_map(
        on_device, mesh=mesh, in_specs=in_specs, out_specs=out_specs, check_vma=False
    )
```

```python
import functools
import math

import jax
import jax.numpy as jnp
from jax import lax
from jax.experimental import pallas as pl
from jax.experimental.pallas import tpu as pltpu
from jax.sharding import PartitionSpec as P

HEAD_DIM = 128
EPS = 1e-06
ROPE_BASE = 10000.0
LANES = 128
HIDE = -1e30
LOG2E = 1.4426950408889634
LN2 = 0.6931471805599453
LEVEL_KEYS = (512, 256, 128)
MIB = 1 << 20

f32 = jnp.float32
bf16 = jnp.bfloat16


def dot(a, b):
    return lax.dot_general(a, b, (((1,), (0,)), ((), ())), preferred_element_type=f32)


def dot_nt(a, b):
    return lax.dot_general(a, b, (((1,), (1,)), ((), ())), preferred_element_type=f32)


def iota(shape, dim):
    return lax.broadcasted_iota(jnp.int32, shape, dim).astype(f32)


def divided(index, by):
    quotient = jnp.floor((index + 0.5) * (1.0 / by))
    return quotient, index - by * quotient


def one_hot(condition):
    return jnp.where(condition, 1.0, 0.0).astype(bf16)


def rms(values, gain):
    mean_square = jnp.mean(values * values, axis=-1, keepdims=True)
    return (values * lax.rsqrt(mean_square + EPS) * gain).astype(bf16)


def ring_get(piece, count):
    pieces = [piece]
    for step in range(1, count):
        pieces.append(
            lax.ppermute(piece, "tensor", [((i + step) % count, i) for i in range(count)])
        )
    return pieces


def ring_send(pieces):
    count = len(pieces)
    arrived = [pieces[0]]
    for step in range(1, count):
        arrived.append(
            lax.ppermute(pieces[step], "tensor", [(i, (i + step) % count) for i in range(count)])
        )
    return arrived


def exchange(rows, groups, halves=False):
    size = groups // 2 if halves else groups
    blocks = rows.reshape(size, rows.shape[0] // size, rows.shape[1])
    parts = [list(range(size)), list(range(size, groups))] if halves else None
    return lax.all_to_all(
        blocks, "dp", split_axis=0, concat_axis=0, tiled=True, axis_index_groups=parts
    ).reshape(rows.shape)


def from_partner(array, groups):
    return lax.ppermute(array, "dp", [(i, (i + groups // 2) % groups) for i in range(groups)])


def in_hbm(array):
    return pltpu.with_memory_space_constraint(array, pltpu.HBM)


def whole():
    return pl.BlockSpec(memory_space=pltpu.VMEM)


def scalar():
    return pl.BlockSpec(memory_space=pltpu.SMEM)


def params(mib, grid=0):
    return pltpu.CompilerParams(
        vmem_limit_bytes=mib * MIB,
        dimension_semantics=("arbitrary",) * grid if grid else None,
    )


def cost(flops, nbytes):
    return pl.CostEstimate(flops=int(flops), bytes_accessed=int(nbytes), transcendentals=0)


def upright(row):
    size = row.shape[1]
    diagonal = iota((size, size), 0) == iota((size, size), 1)
    return jnp.sum(jnp.where(diagonal, row, 0.0), axis=1, keepdims=True)


def in_rows(values, leaf_len):
    choices, requests, _ = values.shape
    rows = requests * leaf_len
    request_of_row, token_of_row = divided(iota((1, rows), 1), leaf_len)
    flat = values.astype(f32).reshape(choices * requests, leaf_len).astype(bf16)
    spread = dot(flat, one_hot(iota((leaf_len, 1), 0) == token_of_row))
    _, request = divided(iota((choices * requests, 1), 0), requests)
    kept = jnp.where(request == request_of_row, spread, 0.0)
    return jnp.sum(kept.reshape(choices, requests, rows), axis=1)


def across_rows(column):
    size = column.shape[0]
    diagonal = iota((size, size), 0) == iota((size, size), 1)
    return jnp.sum(jnp.where(diagonal, column, 0.0), axis=0, keepdims=True)


def owner_slots(owner):
    rows = []
    for level in range(3):
        mine, repeated = owner[level : level + 1], 0.0
        for earlier in range(level):
            same = upright(owner[earlier : earlier + 1]) == mine
            repeated = repeated + jnp.max(jnp.where(same, 1.0, 0.0), axis=0, keepdims=True)
        rows.append(mine * 2.0 + repeated)
    return rows


def prelude_kernel(
    owner_ref, start_ref, length_ref, request_ref, ids_ref, gates_ref,
    place_ref, meta_ref, cos_ref, sin_ref, table_ref,
    *, leaf_len,
):
    requests = owner_ref.shape[1]
    slot_rows, rows = place_ref.shape
    start, length = start_ref[...].astype(f32), length_ref[...].astype(f32)
    row_slot, row_token = divided(iota((slot_rows, 1), 0), leaf_len)
    request_of_row, token_of_row = divided(iota((1, rows), 1), leaf_len)
    named, first_key, key_count = 0.0, 0.0, 0.0
    for level, slot in enumerate(owner_slots(owner_ref[...].astype(f32))):
        here = jnp.where(slot == row_slot, 1.0, 0.0)
        named = named + here
        first_key = first_key + here * start[level : level + 1]
        key_count = key_count + here * length[level : level + 1]
    placed = dot(named.astype(bf16), one_hot(iota((requests, 1), 0) == request_of_row))
    place_ref[...] = jnp.where(row_token == token_of_row, placed, 0.0).astype(bf16)

    first_key = jnp.sum(first_key, axis=1, keepdims=True)
    key_count = jnp.sum(key_count, axis=1, keepdims=True)
    dest, place = divided(request_ref[...].astype(f32), requests)
    row_group, _ = divided(row_slot, 2)
    tag = jnp.sum(jnp.where(dest == row_group, place + 1.0, 0.0), axis=1, keepdims=True)
    lane = iota((1, LANES), 1)
    meta = jnp.zeros((slot_rows, LANES), f32)
    for at, value in enumerate(divided(first_key, 32) + divided(key_count, 32) + (tag,)):
        meta = jnp.where(lane == at, value, meta)
    meta_ref[...] = meta.astype(bf16)

    offsets = length[0:1] + length[1:2] + length[2:3]
    row_request, row_place = divided(iota((rows, 1), 0), leaf_len)
    mine = iota((1, requests), 1) == row_request
    position = jnp.sum(jnp.where(mine, offsets, 0.0), axis=1, keepdims=True) + row_place
    half = HEAD_DIM // 2
    pair = jnp.where(lane < half, lane, lane - half)
    angle = position * jnp.exp(pair * (-2.0 * math.log(ROPE_BASE) / HEAD_DIM))
    cos_ref[...] = jnp.cos(angle)
    sin_ref[...] = jnp.sin(angle) * jnp.where(lane < half, -1.0, 1.0)

    gates = gates_ref[...]
    gates_high = gates.astype(bf16).astype(f32)
    choices = gates.shape[0]
    for at, values in enumerate((ids_ref[...], gates_high, gates - gates_high)):
        table_ref[at * choices : (at + 1) * choices, :] = in_rows(values, leaf_len)
    dest_down = jnp.sum(jnp.where(mine, dest, 0.0), axis=1, keepdims=True)
    last = 3 * choices
    size = table_ref.shape[0] - last
    table_ref[last:, :] = jnp.broadcast_to(across_rows(dest_down), (size, rows))


def routing_kernel(
    half_ref, after_ref, owner_ref, table_ref, far_table_ref,
    pick_ref, send_ref, high_ref, low_ref, final_ref,
    *, leaf_len, groups, capacity, experts, choices,
):
    requests = owner_ref.shape[1]
    rows = requests * leaf_len
    slot_rows = groups * 2 * leaf_len
    row_request, row_place = divided(iota((rows, 1), 0), leaf_len)
    _, token_of_row = divided(iota((1, rows), 1), leaf_len)
    slot_across, token_across = divided(iota((1, slot_rows), 1), leaf_len)
    mine = iota((1, requests), 1) == row_request
    for level, slot in enumerate(owner_slots(owner_ref[...].astype(f32))):
        slot_down = jnp.sum(jnp.where(mine, slot, 0.0), axis=1, keepdims=True)
        pick_ref[level] = one_hot((slot_down == slot_across) & (row_place == token_across))

    slots = send_ref.shape[0]
    local = experts // groups
    block, slot_place = divided(iota((slots, 1), 0), capacity)
    block, local_expert = divided(block, local)
    device, slot_source = divided(block, 2)
    first_expert = (half_ref[0] * (experts // 2)).astype(f32)
    spread = one_hot(first_expert + device * local + local_expert == iota((1, experts), 1))
    expert_down = iota((experts, 1), 0)
    ahead = one_hot(iota((rows, rows), 0) < iota((rows, rows), 1))
    final_group, final_token = divided(iota((slot_rows, 1), 0), leaf_len)
    final_group, final_source = divided(final_group, 2)
    send, high, low, final = [], [], [], []
    for source, table in enumerate((table_ref[...], far_table_ref[...])):
        member, gate_high, gate_low = 0.0, 0.0, 0.0
        for choice in range(choices):
            hit = jnp.where(table[choice : choice + 1] == expert_down, 1.0, 0.0)
            member = member + hit
            gate_high = gate_high + hit * table[choices + choice : choices + choice + 1]
            gate_low = gate_low + hit * table[2 * choices + choice : 2 * choices + choice + 1]
        member = member.astype(bf16)
        before = dot(member, ahead).astype(bf16)
        taken = (dot(spread, member) > 0.5) & (dot(spread, before) == slot_place)
        taken = taken & (slot_source == source)
        send.append(jnp.where(taken, 1.0, 0.0))
        high.append(jnp.where(taken, dot(spread, gate_high.astype(bf16)), 0.0))
        low.append(jnp.where(taken, dot(spread, gate_low.astype(bf16)), 0.0))
        going = (table[3 * choices : 3 * choices + 1] == final_group) & (final_source == source)
        final.append(jnp.where(going & (final_token == token_of_row), 1.0, 0.0))
    send_ref[...] = jnp.concatenate(send, axis=1).astype(bf16)
    high_ref[...] = jnp.transpose(jnp.concatenate(high, axis=1)).astype(bf16)
    low_ref[...] = jnp.transpose(jnp.concatenate(low, axis=1)).astype(bf16)
    final_ref[...] = jnp.concatenate(final, axis=1).astype(bf16)


def rotated(product, cosine, sine, heads):
    columns = []
    for head in range(heads):
        part = product[:, head * HEAD_DIM : (head + 1) * HEAD_DIM]
        columns.append(part * cosine + pltpu.roll(part, HEAD_DIM // 2, 1) * sine)
    return jnp.concatenate(columns, axis=1).astype(bf16)


def query_kernel(*refs, tensors, heads):
    index_ref, pieces, refs = refs[0], refs[1 : 1 + tensors], refs[1 + tensors :]
    (gain_ref, weight_ref, cos_ref, sin_ref, place_ref, meta_ref,
     raw_ref, normed_ref, query_ref, send_ref, buffer_ref, semaphores) = refs
    width = heads * HEAD_DIM
    copies = column_copies(weight_ref, buffer_ref, semaphores, width)
    shard = pieces[0].shape[0]
    for at, piece in enumerate(pieces):
        owner = lax.rem(index_ref[0] + at, tensors)
        raw_ref[pl.ds(pl.multiple_of(owner * shard, shard), shard), :] = piece[...]
    normed_ref[...] = rms(raw_ref[...].astype(f32), gain_ref[...])
    send_ref[:, send_ref.shape[1] - LANES :] = meta_ref[...]
    for at, copy in enumerate(copies):
        copy.wait()
        columns = slice(at * width, (at + 1) * width)
        product = dot(normed_ref[...], buffer_ref[:, columns])
        query = rotated(product, cos_ref[...], sin_ref[...], heads)
        query_ref[:, columns] = query
        send_ref[:, columns] = dot(place_ref[...], query).astype(bf16)


def leaf_kernel(
    normed_ref, query_ref, key_ref, value_ref, cos_ref, sin_ref, out_ref, lse_ref,
    *, heads, leaf_len, scale,
):
    step = pl.program_id(0)
    normed = normed_ref[...]
    rows = normed.shape[0]
    keys = rotated(dot(normed, key_ref[...]), cos_ref[...], sin_ref[...], heads)
    values = dot(normed, value_ref[...]).astype(bf16)
    down, across = iota((rows, 1), 0), iota((1, rows), 1)
    visible = (divided(down, leaf_len)[0] == divided(across, leaf_len)[0]) & (across <= down)
    lane = lax.broadcasted_iota(jnp.int32, (1, LANES), 1)

    @pl.when(step == 0)
    def _():
        lse_ref[...] = jnp.zeros_like(lse_ref)

    for head in range(heads):
        at = slice(head * HEAD_DIM, (head + 1) * HEAD_DIM)
        scores = jnp.where(visible, dot_nt(query_ref[:, at], keys[:, at]) * scale, HIDE)
        highest = jnp.max(scores, axis=1, keepdims=True)
        weights = jnp.exp(scores - highest)
        total = jnp.sum(weights, axis=1, keepdims=True)
        out_ref[:, at] = dot(weights.astype(bf16), values[:, at]) / total
        lse = highest + jnp.log(total)
        lse_ref[...] = jnp.where(lane == step * heads + head, lse, lse_ref[...])


def owner_kernel(
    arrived_ref, kv_ref, back_ref, query_ref, out_ref,
    *, heads, requests, leaf_len, scale,
):
    slot_rows = arrived_ref.shape[0]
    width = heads * HEAD_DIM
    count = requests * leaf_len
    packed = arrived_ref[:, width:]
    meta = packed.astype(f32)
    first = meta[:, 0:1] * 32.0 + meta[:, 1:2]
    used = meta[:, 2:3] + meta[:, 3:4] > 0.0
    begins = [sum(LEVEL_KEYS[:level]) for level in range(3)]
    level = jnp.where(first >= begins[1], 1.0, 0.0) + jnp.where(first >= begins[2], 1.0, 0.0)
    level = jnp.where(used, level, 3.0)
    lane = lax.broadcasted_iota(jnp.int32, (1, LANES), 1)
    of_level = level == lane.astype(f32)
    ahead = one_hot(iota((slot_rows, slot_rows), 1) < iota((slot_rows, slot_rows), 0))
    rank = dot(ahead, one_hot(of_level))
    rank = jnp.sum(jnp.where(of_level, rank, 0.0), axis=1, keepdims=True)
    target = jnp.where(used, level * count + rank, -1.0)
    spread = jnp.where(target == iota((1, 3 * count), 1), 1.0, 0.0)
    ordered = jnp.transpose(spread).astype(bf16)
    query_ref[...] = dot(ordered, arrived_ref[:, :width]).astype(bf16)
    meta = dot(ordered, packed)
    first = meta[:, 0:1] * 32.0 + meta[:, 1:2]
    last = first + meta[:, 2:3] * 32.0 + meta[:, 3:4]
    for level in range(3):
        size = LEVEL_KEYS[level]
        part = slice(level * count, (level + 1) * count)
        keys = slice(begins[level], begins[level] + size)
        key = iota((1, size), 1) + float(begins[level])
        bias = jnp.where((key >= first[part]) & (key < last[part]), 0.0, HIDE)
        ones = jnp.ones((size, HEAD_DIM), bf16)
        sums = jnp.zeros((count, LANES), f32)
        for head in range(heads):
            at = slice(head * HEAD_DIM, (head + 1) * HEAD_DIM)
            scores = dot_nt(query_ref[part, at], kv_ref[0, keys, at]) * (scale * LOG2E) + bias
            highest = jnp.max(scores, axis=1, keepdims=True)
            weights = jnp.exp2(scores - highest).astype(bf16)
            both = dot(weights, jnp.concatenate([kv_ref[1, keys, at], ones], axis=1))
            total = both[:, HEAD_DIM:]
            out_ref[part, at] = (both[:, :HEAD_DIM] / total).astype(bf16)
            lse = highest * LN2 + jnp.log(total)
            lse_high = lse.astype(bf16).astype(f32)
            sums = jnp.where(lane == head, lse_high, sums)
            sums = jnp.where(lane == head + heads, lse - lse_high, sums)
        out_ref[part, width:] = sums.astype(bf16)
    back_ref[...] = dot(spread.astype(bf16), out_ref[...]).astype(bf16)


def column_copies(source_ref, target_ref, semaphores, step):
    copies = []
    for at in range(source_ref.shape[1] // step):
        columns = pl.ds(at * step, step)
        copy = pltpu.make_async_copy(
            source_ref.at[:, columns], target_ref.at[:, columns], semaphores.at[at]
        )
        copy.start()
        copies.append(copy)
    return copies


def merge_kernel(
    back_ref, pick_ref, leaf_ref, lse_ref, weight_ref, out_ref, buffer_ref, attended_ref, semaphores,
    *, heads, step,
):
    copies = column_copies(weight_ref, buffer_ref, semaphores, step)
    width = heads * HEAD_DIM
    back = back_ref[...]
    outputs, sums = [leaf_ref[...]], [lse_ref[...]]
    for level in range(3):
        rows = dot(pick_ref[level], back)
        outputs.append(rows[:, :width])
        tail = rows[:, width:]
        sums.append(tail + pltpu.roll(tail, LANES - heads, 1))
    highest = functools.reduce(jnp.maximum, sums)
    scales = [jnp.exp(one - highest) for one in sums]
    total = sum(scales[1:], scales[0])
    scales = [one / total for one in scales]
    for head in range(heads):
        at = slice(head * HEAD_DIM, (head + 1) * HEAD_DIM)
        mixed = sum(scales[i][:, head : head + 1] * outputs[i][:, at] for i in range(4))
        attended_ref[:, at] = mixed.astype(bf16)
    for at, copy in enumerate(copies):
        copy.wait()
        columns = slice(at * step, (at + 1) * step)
        out_ref[:, columns] = dot(attended_ref[...], buffer_ref[:, columns]).astype(bf16)


def middle_kernel(*refs, tensors):
    index_ref, raw_ref, gain_ref = refs[:3]
    pieces = refs[3 : 3 + tensors]
    normed_ref, own_ref, resid_own_ref, resid_ref = refs[3 + tensors :]
    width = own_ref.shape[1]
    own = pl.ds(pl.multiple_of(index_ref[0] * width, width), width)
    total = raw_ref[...].astype(f32)
    for piece in pieces:
        total = total + piece[...].astype(f32)
    resid_ref[...] = total
    resid_own_ref[...] = resid_ref[:, own]
    normed_ref[...] = rms(total, gain_ref[...])
    own_ref[...] = normed_ref[:, own]


def dispatch_kernel(after_ref, also_after_ref, send_ref, own_ref, far_ref, out_ref):
    both = jnp.concatenate([own_ref[...], far_ref[...]], axis=0)
    out_ref[...] = dot(send_ref[...], both).astype(bf16)


def shared_kernel(*refs, tensors):
    index_ref, rows_ref, in_hbm_ref, down_hbm_ref = refs[:4]
    pieces, refs = refs[4 : 4 + tensors], refs[4 + tensors :]
    in_ref, down_ref, total_ref, semaphores = refs
    copies = [
        pltpu.make_async_copy(in_hbm_ref.at[0], in_ref.at[0], semaphores.at[0]),
        pltpu.make_async_copy(in_hbm_ref.at[1], in_ref.at[1], semaphores.at[1]),
        pltpu.make_async_copy(down_hbm_ref, down_ref, semaphores.at[2]),
    ]
    for copy in copies:
        copy.start()
    rows = rows_ref[...]
    copies[0].wait()
    gate = dot_nt(rows, in_ref[0])
    copies[1].wait()
    up = dot_nt(rows, in_ref[1])
    hidden = (gate / (1.0 + jnp.exp(-gate)) * up).astype(bf16)
    copies[2].wait()
    total_ref[...] = dot(hidden, down_ref[...])
    width = pieces[0].shape[1]
    for at, piece in enumerate(pieces):
        column = lax.rem(index_ref[0] + at, tensors) * width
        piece[...] = total_ref[:, pl.ds(pl.multiple_of(column, width), width)].astype(bf16)


def load_kernel(after_ref, in_ref, down_ref, in_out_ref, down_out_ref, semaphores):
    copies = [
        pltpu.make_async_copy(in_ref.at[0], in_out_ref, semaphores.at[0]),
        pltpu.make_async_copy(down_ref.at[0], down_out_ref, semaphores.at[1]),
    ]
    for copy in copies:
        copy.start()
    for copy in copies:
        copy.wait()


def rows_of_experts(piece, experts, capacity):
    groups, _, width = piece.shape
    values = piece[...].astype(f32)
    for e in range(experts):
        mine = values[:, e * capacity : (e + 1) * capacity, :].reshape(groups * capacity, width)
        yield mine.astype(bf16)


def expert_kernel(*refs, tensors, experts, capacity):
    index_ref, arrived, refs = refs[0], refs[1 : 1 + tensors], refs[1 + tensors :]
    (first_in_ref, first_down_ref, in_hbm_ref, down_hbm_ref), refs = refs[:4], refs[4:]
    pieces, refs = refs[:tensors], refs[tensors:]
    in_ref, down_ref, rows_ref, total_ref, semaphores = refs
    copies = []
    for e in range(1, experts):
        copies.append(
            (
                pltpu.make_async_copy(in_hbm_ref.at[e], in_ref.at[e - 1], semaphores.at[0, e]),
                pltpu.make_async_copy(down_hbm_ref.at[e], down_ref.at[e - 1], semaphores.at[1, e]),
            )
        )
        for copy in copies[-1]:
            copy.start()
    groups, _, width = arrived[0].shape
    columns = [
        pl.ds(pl.multiple_of(lax.rem(index_ref[0] + at, tensors) * width, width), width)
        for at in range(tensors)
    ]
    for at, piece in enumerate(arrived):
        for e, rows in enumerate(rows_of_experts(piece, experts, capacity)):
            rows_ref[e, :, columns[at]] = rows
    for e in range(experts):
        if e == 0:
            gate_weight, up_weight, down = first_in_ref.at[0], first_in_ref.at[1], first_down_ref
        else:
            gate_weight, up_weight, down = in_ref.at[e - 1, 0], in_ref.at[e - 1, 1], down_ref.at[e - 1]
            copies[e - 1][0].wait()
        gate = dot_nt(rows_ref[e], gate_weight[...])
        up = dot_nt(rows_ref[e], up_weight[...])
        hidden = (gate / (1.0 + jnp.exp(-gate)) * up).astype(bf16)
        if e > 0:
            copies[e - 1][1].wait()
        mine = slice(e * capacity, (e + 1) * capacity)
        for at in range(tensors):
            value = dot(hidden, down[:, columns[at]])
            total_ref[at, :, mine, :] = value.reshape(groups, capacity, width)
    for at, piece in enumerate(pieces):
        piece[...] = total_ref[at].astype(bf16)


def add_kernel(*refs):
    out_ref = refs[-1]
    out_ref[...] = sum(piece[...].astype(f32) for piece in refs[:-1]).astype(bf16)


def combine_kernel(*refs, tensors):
    returned_ref, high_ref, low_ref, resid_ref, final_ref = refs[:5]
    shared, out_ref = refs[5 : 5 + tensors], refs[5 + tensors]
    returned = returned_ref[...]
    routed = dot(high_ref[...], returned) + dot(low_ref[...], returned)
    rows = resid_ref.shape[0]
    total = resid_ref[...]
    for piece in shared:
        total = total + piece[...].astype(f32)
    both = jnp.concatenate([total + routed[:rows], routed[rows:]], axis=0).astype(bf16)
    out_ref[...] = dot(final_ref[...], both).astype(bf16)


def settle_kernel(*refs, tensors, leaf_len, groups):
    index_ref, meta_ref, rows_ref = refs[:3]
    pieces = refs[3:]
    slot_rows = meta_ref.shape[0]
    places = pieces[0].shape[0]
    share = leaf_len // tensors
    tag_down = meta_ref[...].astype(f32)[:, 4:5]
    block, token = divided(iota((1, slot_rows), 1), leaf_len)
    group, source = divided(block, 2)
    _, home = divided(group + source * (groups // 2), groups)
    tagged = iota((slot_rows, 1), 0) == home * (2.0 * leaf_len) + token
    tag = jnp.sum(jnp.where(tagged, tag_down, 0.0), axis=0, keepdims=True)
    request, position = divided(iota((places, 1), 0), share)
    for at, piece in enumerate(pieces):
        shift = (lax.rem(index_ref[0] + at, tensors) * share).astype(f32)
        chosen = one_hot((tag == request + 1.0) & (token == position + shift))
        piece[...] = dot(chosen, rows_ref[...]).astype(bf16)


def on_device(
    leaf_tokens,
    attn_gain,
    w_query,
    w_key,
    w_value,
    w_out,
    prefix_kv,
    prefix_owner,
    prefix_start,
    prefix_len,
    mlp_gain,
    shared_in,
    shared_out,
    expert_in,
    expert_out,
    expert_ids,
    gate_weights,
    request_of,
):
    groups = lax.axis_size("dp")
    tensors = lax.axis_size("tensor")
    index = lax.axis_index("tensor").astype(jnp.int32).reshape(1)
    shard_requests, leaf_len, model_width = leaf_tokens.shape
    requests = prefix_owner.shape[0]
    rows = requests * leaf_len
    local_width = w_query.shape[1]
    local_heads = local_width // HEAD_DIM
    scale = HEAD_DIM ** (-0.5)
    column_share = model_width // tensors
    top_count = expert_ids.shape[2]
    local_experts = expert_in.shape[0]
    experts = local_experts * groups
    assignments = rows * top_count
    capacity = tensors * max(1, assignments * 4 // (experts * 3 * tensors))
    slots = experts * capacity
    slot_rows = groups * 2 * leaf_len
    shape = jax.ShapeDtypeStruct

    raw_pieces = ring_get(leaf_tokens.reshape(shard_requests * leaf_len, model_width), tensors)

    owner_rows, request_row = prefix_owner.T, request_of.reshape(1, requests)
    table_rows = -(-(3 * top_count + 1) // 8) * 8
    place, meta, cosine, sine, table = pl.pallas_call(
        functools.partial(prelude_kernel, leaf_len=leaf_len),
        out_shape=[
            shape((slot_rows, rows), bf16),
            shape((slot_rows, LANES), bf16),
            shape((rows, LANES), f32),
            shape((rows, LANES), f32),
            shape((table_rows, rows), f32),
        ],
        in_specs=[whole()] * 6,
        out_specs=[whole()] * 5,
        compiler_params=params(24),
        name="prelude",
    )(
        in_hbm(owner_rows), in_hbm(prefix_start.T), in_hbm(prefix_len.T), in_hbm(request_row),
        in_hbm(jnp.transpose(expert_ids, (2, 0, 1))),
        in_hbm(jnp.transpose(gate_weights, (2, 0, 1))),
    )
    far_table = from_partner(table, groups)

    step_heads = min(2, local_heads)
    step_width = step_heads * HEAD_DIM
    steps = local_heads // step_heads
    query_heads = min(4, local_heads)
    fixed = lambda *dims: pl.BlockSpec(dims, lambda i: (0,) * len(dims))
    columns = lambda *dims: pl.BlockSpec(dims, lambda i: (0,) * (len(dims) - 1) + (i,))
    send_width = local_width + LANES
    raw, normed, query, query_send = pl.pallas_call(
        functools.partial(query_kernel, tensors=tensors, heads=query_heads),
        out_shape=[
            shape((rows, model_width), bf16),
            shape((rows, model_width), bf16),
            shape((rows, local_width), bf16),
            shape((slot_rows, send_width), bf16),
        ],
        in_specs=[scalar()]
        + [whole()] * (tensors + 1)
        + [pl.BlockSpec(memory_space=pltpu.HBM)]
        + [whole()] * 4,
        out_specs=[whole()] * 4,
        scratch_shapes=[
            pltpu.VMEM((model_width, local_width), bf16),
            pltpu.SemaphoreType.DMA((local_heads // query_heads,)),
        ],
        compiler_params=params(24),
        cost_estimate=cost(2 * rows * model_width * local_width, 2 * model_width * local_width),
        name="queries",
    )(
        index, in_hbm(raw_pieces[0]), *raw_pieces[1:], in_hbm(attn_gain.reshape(1, -1)), in_hbm(w_query),
        cosine, sine, place, meta,
    )

    query_arrived = exchange(query_send, groups)

    leaf_out, leaf_lse = pl.pallas_call(
        functools.partial(leaf_kernel, heads=step_heads, leaf_len=leaf_len, scale=scale),
        grid=(steps,),
        out_shape=[shape((rows, local_width), f32), shape((rows, LANES), f32)],
        in_specs=[
            fixed(rows, model_width),
            columns(rows, step_width),
            columns(model_width, step_width),
            columns(model_width, step_width),
            fixed(rows, LANES),
            fixed(rows, LANES),
        ],
        out_specs=[columns(rows, step_width), fixed(rows, LANES)],
        compiler_params=params(24, 1),
        cost_estimate=cost(4 * rows * model_width * local_width, 4 * model_width * local_width),
        name="leaf",
    )(normed, query, in_hbm(w_key), in_hbm(w_value), cosine, sine)

    half = (lax.axis_index("dp") // (groups // 2)).astype(jnp.int32).reshape(1)
    pick, send, gate_high, gate_low, final = pl.pallas_call(
        functools.partial(
            routing_kernel, leaf_len=leaf_len, groups=groups, capacity=capacity, experts=experts,
            choices=top_count,
        ),
        out_shape=[
            shape((3, rows, slot_rows), bf16),
            shape((slots, 2 * rows), bf16),
            shape((2 * rows, slots), bf16),
            shape((2 * rows, slots), bf16),
            shape((slot_rows, 2 * rows), bf16),
        ],
        in_specs=[scalar(), pl.BlockSpec(memory_space=pl.ANY)] + [whole()] * 3,
        out_specs=[whole()] * 5,
        compiler_params=params(24),
        cost_estimate=cost(1 << 30, 1 << 20),
        name="routing",
    )(half, query_arrived, owner_rows, table, far_table)

    pool = prefix_kv.shape[1]
    back_send = pl.pallas_call(
        functools.partial(
            owner_kernel, heads=local_heads, requests=requests, leaf_len=leaf_len, scale=scale
        ),
        out_shape=shape((slot_rows, send_width), bf16),
        in_specs=[whole()] * 2,
        out_specs=whole(),
        scratch_shapes=[
            pltpu.VMEM((3 * rows, local_width), bf16),
            pltpu.VMEM((3 * rows, send_width), bf16),
        ],
        compiler_params=params(32),
        cost_estimate=cost(4 * slot_rows * pool * local_width, 4 * pool * local_width),
        name="owner",
    )(query_arrived, prefix_kv)

    back = exchange(back_send, groups)

    out_step = min(512, model_width)
    partial_out = pl.pallas_call(
        functools.partial(merge_kernel, heads=local_heads, step=out_step),
        out_shape=shape((rows, model_width), bf16),
        in_specs=[whole()] * 4 + [pl.BlockSpec(memory_space=pltpu.HBM)],
        out_specs=whole(),
        scratch_shapes=[
            pltpu.VMEM((local_width, model_width), bf16),
            pltpu.VMEM((rows, local_width), bf16),
            pltpu.SemaphoreType.DMA((model_width // out_step,)),
        ],
        compiler_params=params(24),
        cost_estimate=cost(2 * rows * local_width * model_width, 2 * local_width * model_width),
        name="merge",
    )(back, pick, leaf_out, leaf_lse, in_hbm(w_out))

    out_pieces = ring_get(partial_out, tensors)

    normed_mlp, own_columns, resid_own = pl.pallas_call(
        functools.partial(middle_kernel, tensors=tensors),
        out_shape=[
            shape((rows, model_width), bf16),
            shape((rows, column_share), bf16),
            shape((rows, column_share), f32),
        ],
        in_specs=[scalar()] + [whole()] * (2 + tensors),
        out_specs=[whole()] * 3,
        scratch_shapes=[pltpu.VMEM((rows, model_width), f32)],
        compiler_params=params(24),
        name="middle",
    )(index, raw, mlp_gain.reshape(1, -1), *out_pieces)

    far_columns = from_partner(own_columns, groups)
    hbm = pl.BlockSpec(memory_space=pltpu.HBM)
    hidden = shared_out.shape[0]
    shared_pieces = pl.pallas_call(
        functools.partial(shared_kernel, tensors=tensors),
        out_shape=[shape((rows, column_share), bf16)] * tensors,
        in_specs=[scalar(), whole(), hbm, hbm],
        out_specs=[whole()] * tensors,
        scratch_shapes=[
            pltpu.VMEM((2, hidden, model_width), bf16),
            pltpu.VMEM((hidden, model_width), bf16),
            pltpu.VMEM((rows, model_width), f32),
            pltpu.SemaphoreType.DMA((3,)),
        ],
        compiler_params=params(16),
        cost_estimate=cost(1, 1),
        name="shared",
    )(index, normed_mlp, in_hbm(jnp.transpose(shared_in, (1, 2, 0))), in_hbm(shared_out))
    expert_hidden = expert_out.shape[1]
    expert_in = in_hbm(jnp.transpose(expert_in, (0, 2, 3, 1)))
    expert_out = in_hbm(expert_out)
    first_in, first_down = pl.pallas_call(
        load_kernel,
        out_shape=[
            pltpu.VMEM((2, expert_hidden, model_width), bf16),
            pltpu.VMEM((expert_hidden, model_width), bf16),
        ],
        in_specs=[pl.BlockSpec(memory_space=pl.ANY), hbm, hbm],
        out_specs=[whole()] * 2,
        scratch_shapes=[pltpu.SemaphoreType.DMA((2,))],
        compiler_params=params(1),
        cost_estimate=cost(1, 1),
        name="load",
    )(normed_mlp, expert_in, expert_out)

    send_rows = pl.pallas_call(
        dispatch_kernel,
        out_shape=shape((slots, column_share), bf16),
        in_specs=[pl.BlockSpec(memory_space=pl.ANY)] * 2 + [whole()] * 3,
        out_specs=whole(),
        compiler_params=params(8),
        name="dispatch",
    )(shared_pieces[0], first_down, send, own_columns, far_columns)

    arrived = exchange(send_rows, groups, halves=True)

    block = local_experts * capacity
    arrived_pieces = ring_get(arrived.reshape(groups, block, column_share), tensors)
    partial_pieces = pl.pallas_call(
        functools.partial(
            expert_kernel, tensors=tensors, experts=local_experts, capacity=capacity
        ),
        out_shape=[shape((groups, block, column_share), bf16)] * tensors,
        in_specs=[scalar()] + [whole()] * (tensors + 2) + [hbm, hbm],
        out_specs=[whole()] * tensors,
        scratch_shapes=[
            pltpu.VMEM((local_experts - 1, 2, expert_hidden, model_width), bf16),
            pltpu.VMEM((local_experts - 1, expert_hidden, model_width), bf16),
            pltpu.VMEM((local_experts, groups * capacity, model_width), bf16),
            pltpu.VMEM((tensors, groups, block, column_share), f32),
            pltpu.SemaphoreType.DMA((2, local_experts)),
        ],
        compiler_params=params(35),
        cost_estimate=cost(
            6 * slots * expert_hidden * model_width,
            6 * local_experts * expert_hidden * model_width,
        ),
        name="experts",
    )(
        index,
        *arrived_pieces,
        pltpu.with_memory_space_constraint(first_in, pltpu.VMEM),
        pltpu.with_memory_space_constraint(first_down, pltpu.VMEM),
        expert_in,
        expert_out,
    )
    partial_pieces = ring_send(partial_pieces)
    summed = pl.pallas_call(
        add_kernel,
        out_shape=shape((groups, block, column_share), bf16),
        in_specs=[whole()] * tensors,
        out_specs=whole(),
        compiler_params=params(12),
        name="add",
    )(*partial_pieces)

    shared_pieces = ring_send(shared_pieces)
    returned = exchange(summed.reshape(slots, column_share), groups, halves=True)

    final_send = pl.pallas_call(
        functools.partial(combine_kernel, tensors=tensors),
        out_shape=shape((slot_rows, column_share), bf16),
        in_specs=[whole()] * (5 + tensors),
        out_specs=whole(),
        compiler_params=params(24),
        name="combine",
    )(returned, gate_high, gate_low, resid_own, final, *shared_pieces)

    final_arrived = exchange(final_send, groups)

    places = requests * (leaf_len // tensors)
    settled = pl.pallas_call(
        functools.partial(
            settle_kernel, tensors=tensors, leaf_len=leaf_len, groups=groups
        ),
        grid=(1,),
        out_shape=[shape((places, column_share), bf16)] * tensors,
        in_specs=[
            scalar(),
            pl.BlockSpec((slot_rows, LANES), lambda i: (0, local_heads)),
            fixed(slot_rows, column_share),
        ],
        out_specs=[fixed(places, column_share)] * tensors,
        compiler_params=params(24, 1),
        name="settle",
    )(index, query_arrived, final_arrived)
    settled = ring_send(settled)
    if tensors == 2:
        first = index[0] == 0
        own, other = settled
        result = jnp.concatenate(
            [jnp.where(first, own, other), jnp.where(first, other, own)], axis=1
        )
    else:
        result = jnp.zeros((places, model_width), bf16)
        for at, piece in enumerate(settled):
            column = ((index[0] - at + tensors) % tensors) * column_share
            result = lax.dynamic_update_slice(result, piece, (0, column))
    return result.reshape(requests, leaf_len // tensors, model_width)


def solution(mesh):
    in_specs = (
        P(("dp", "tensor"), None, None),
        P(),
        P(None, "tensor"),
        P(None, "tensor"),
        P(None, "tensor"),
        P("tensor", None),
        P(None, "dp", "tensor"),
        P("dp", None),
        P("dp", None),
        P("dp", None),
        P(),
        P(None, None, "tensor"),
        P("tensor", None),
        P("dp", None, None, "tensor"),
        P("dp", "tensor", None),
        P("dp", None, None),
        P("dp", None, None),
        P("dp"),
    )
    out_specs = P("dp", "tensor", None)
    return jax.shard_map(
        on_device, mesh=mesh, in_specs=in_specs, out_specs=out_specs, check_vma=False
    )
```

```python
import functools
import math

import jax
import jax.numpy as jnp
from jax import lax
from jax.experimental import pallas as pl
from jax.experimental.pallas import tpu as pltpu
from jax.sharding import PartitionSpec as P

HEAD_DIM = 128
EPS = 1e-06
ROPE_BASE = 10000.0
LANES = 128
HIDE = -1e30
LOG2E = 1.4426950408889634
LN2 = 0.6931471805599453
LEVEL_KEYS = (512, 256, 128)
MIB = 1 << 20

f32 = jnp.float32
bf16 = jnp.bfloat16


def dot(a, b):
    return lax.dot_general(a, b, (((1,), (0,)), ((), ())), preferred_element_type=f32)


def dot_nt(a, b):
    return lax.dot_general(a, b, (((1,), (1,)), ((), ())), preferred_element_type=f32)


def iota(shape, dim):
    return lax.broadcasted_iota(jnp.int32, shape, dim).astype(f32)


def divided(index, by):
    quotient = jnp.floor((index + 0.5) * (1.0 / by))
    return quotient, index - by * quotient


def one_hot(condition):
    return jnp.where(condition, 1.0, 0.0).astype(bf16)


def rms(values, gain):
    mean_square = jnp.mean(values * values, axis=-1, keepdims=True)
    return (values * lax.rsqrt(mean_square + EPS) * gain).astype(bf16)


def ring_get(piece, count):
    pieces = [piece]
    for step in range(1, count):
        pieces.append(
            lax.ppermute(piece, "tensor", [((i + step) % count, i) for i in range(count)])
        )
    return pieces


def ring_send(pieces):
    count = len(pieces)
    arrived = [pieces[0]]
    for step in range(1, count):
        arrived.append(
            lax.ppermute(pieces[step], "tensor", [(i, (i + step) % count) for i in range(count)])
        )
    return arrived


def exchange(rows, groups, halves=False):
    size = groups // 2 if halves else groups
    blocks = rows.reshape(size, rows.shape[0] // size, rows.shape[1])
    parts = [list(range(size)), list(range(size, groups))] if halves else None
    return lax.all_to_all(
        blocks, "dp", split_axis=0, concat_axis=0, tiled=True, axis_index_groups=parts
    ).reshape(rows.shape)


def from_partner(array, groups):
    return lax.ppermute(array, "dp", [(i, (i + groups // 2) % groups) for i in range(groups)])


def in_hbm(array):
    return pltpu.with_memory_space_constraint(array, pltpu.HBM)


def whole():
    return pl.BlockSpec(memory_space=pltpu.VMEM)


def scalar():
    return pl.BlockSpec(memory_space=pltpu.SMEM)


def params(mib, grid=0):
    return pltpu.CompilerParams(
        vmem_limit_bytes=mib * MIB,
        dimension_semantics=("arbitrary",) * grid if grid else None,
    )


def cost(flops, nbytes):
    return pl.CostEstimate(flops=int(flops), bytes_accessed=int(nbytes), transcendentals=0)


def upright(row):
    size = row.shape[1]
    diagonal = iota((size, size), 0) == iota((size, size), 1)
    return jnp.sum(jnp.where(diagonal, row, 0.0), axis=1, keepdims=True)


def in_rows(values, leaf_len):
    choices, requests, _ = values.shape
    rows = requests * leaf_len
    request_of_row, token_of_row = divided(iota((1, rows), 1), leaf_len)
    flat = values.astype(f32).reshape(choices * requests, leaf_len).astype(bf16)
    spread = dot(flat, one_hot(iota((leaf_len, 1), 0) == token_of_row))
    _, request = divided(iota((choices * requests, 1), 0), requests)
    kept = jnp.where(request == request_of_row, spread, 0.0)
    return jnp.sum(kept.reshape(choices, requests, rows), axis=1)


def across_rows(column):
    size = column.shape[0]
    diagonal = iota((size, size), 0) == iota((size, size), 1)
    return jnp.sum(jnp.where(diagonal, column, 0.0), axis=0, keepdims=True)


def owner_slots(owner):
    rows = []
    for level in range(3):
        mine, repeated = owner[level : level + 1], 0.0
        for earlier in range(level):
            same = upright(owner[earlier : earlier + 1]) == mine
            repeated = repeated + jnp.max(jnp.where(same, 1.0, 0.0), axis=0, keepdims=True)
        rows.append(mine * 2.0 + repeated)
    return rows


def prelude_kernel(
    owner_ref, start_ref, length_ref, request_ref, ids_ref, gates_ref,
    place_ref, meta_ref, cos_ref, sin_ref, table_ref, pick_ref,
    *, leaf_len,
):
    requests = owner_ref.shape[1]
    slot_rows, rows = place_ref.shape
    start, length = start_ref[...].astype(f32), length_ref[...].astype(f32)
    row_slot, row_token = divided(iota((slot_rows, 1), 0), leaf_len)
    request_of_row, token_of_row = divided(iota((1, rows), 1), leaf_len)
    row_request, row_place = divided(iota((rows, 1), 0), leaf_len)
    mine = iota((1, requests), 1) == row_request
    slot_across, token_across = divided(iota((1, slot_rows), 1), leaf_len)
    named, first_key, key_count = 0.0, 0.0, 0.0
    for level, slot in enumerate(owner_slots(owner_ref[...].astype(f32))):
        slot_down = jnp.sum(jnp.where(mine, slot, 0.0), axis=1, keepdims=True)
        pick_ref[level] = one_hot((slot_down == slot_across) & (row_place == token_across))
        here = jnp.where(slot == row_slot, 1.0, 0.0)
        named = named + here
        first_key = first_key + here * start[level : level + 1]
        key_count = key_count + here * length[level : level + 1]
    placed = dot(named.astype(bf16), one_hot(iota((requests, 1), 0) == request_of_row))
    place_ref[...] = jnp.where(row_token == token_of_row, placed, 0.0).astype(bf16)

    first_key = jnp.sum(first_key, axis=1, keepdims=True)
    key_count = jnp.sum(key_count, axis=1, keepdims=True)
    dest, place = divided(request_ref[...].astype(f32), requests)
    row_group, _ = divided(row_slot, 2)
    tag = jnp.sum(jnp.where(dest == row_group, place + 1.0, 0.0), axis=1, keepdims=True)
    lane = iota((1, LANES), 1)
    meta = jnp.zeros((slot_rows, LANES), f32)
    for at, value in enumerate(divided(first_key, 32) + divided(key_count, 32) + (tag,)):
        meta = jnp.where(lane == at, value, meta)
    meta_ref[...] = meta.astype(bf16)

    offsets = length[0:1] + length[1:2] + length[2:3]
    position = jnp.sum(jnp.where(mine, offsets, 0.0), axis=1, keepdims=True) + row_place
    half = HEAD_DIM // 2
    pair = jnp.where(lane < half, lane, lane - half)
    angle = position * jnp.exp(pair * (-2.0 * math.log(ROPE_BASE) / HEAD_DIM))
    cos_ref[...] = jnp.cos(angle)
    sin_ref[...] = jnp.sin(angle) * jnp.where(lane < half, -1.0, 1.0)

    gates = gates_ref[...]
    gates_high = gates.astype(bf16).astype(f32)
    choices = gates.shape[0]
    for at, values in enumerate((ids_ref[...], gates_high, gates - gates_high)):
        table_ref[at * choices : (at + 1) * choices, :] = in_rows(values, leaf_len)
    dest_down = jnp.sum(jnp.where(mine, dest, 0.0), axis=1, keepdims=True)
    last = 3 * choices
    size = table_ref.shape[0] - last
    table_ref[last:, :] = jnp.broadcast_to(across_rows(dest_down), (size, rows))


def routing_kernel(
    half_ref, after_ref, table_ref, far_table_ref,
    send_ref, high_ref, low_ref, final_ref,
    *, tensors, leaf_len, groups, capacity, experts, choices,
):
    rows = table_ref.shape[1]
    final_rows = final_ref.shape[0]
    share = leaf_len // tensors
    _, token_of_row = divided(iota((1, rows), 1), leaf_len)

    slots = send_ref.shape[0]
    local = experts // groups
    block, slot_place = divided(iota((slots, 1), 0), capacity)
    block, local_expert = divided(block, local)
    device, slot_source = divided(block, 2)
    first_expert = (half_ref[0] * (experts // 2)).astype(f32)
    spread = one_hot(first_expert + device * local + local_expert == iota((1, experts), 1))
    expert_down = iota((experts, 1), 0)
    ahead = one_hot(iota((rows, rows), 0) < iota((rows, rows), 1))
    block, final_place = divided(iota((final_rows, 1), 0), share)
    block, final_source = divided(block, 2)
    final_group, final_half = divided(block, tensors)
    final_token = final_half * share + final_place
    send, high, low, final = [], [], [], []
    for source, table in enumerate((table_ref[...], far_table_ref[...])):
        member, gate_high, gate_low = 0.0, 0.0, 0.0
        for choice in range(choices):
            hit = jnp.where(table[choice : choice + 1] == expert_down, 1.0, 0.0)
            member = member + hit
            gate_high = gate_high + hit * table[choices + choice : choices + choice + 1]
            gate_low = gate_low + hit * table[2 * choices + choice : 2 * choices + choice + 1]
        member = member.astype(bf16)
        before = dot(member, ahead).astype(bf16)
        taken = (dot(spread, member) > 0.5) & (dot(spread, before) == slot_place)
        taken = taken & (slot_source == source)
        send.append(jnp.where(taken, 1.0, 0.0))
        high.append(jnp.where(taken, dot(spread, gate_high.astype(bf16)), 0.0))
        low.append(jnp.where(taken, dot(spread, gate_low.astype(bf16)), 0.0))
        going = (table[3 * choices : 3 * choices + 1] == final_group) & (final_source == source)
        final.append(jnp.where(going & (final_token == token_of_row), 1.0, 0.0))
    send_ref[...] = jnp.concatenate(send, axis=1).astype(bf16)
    high_ref[...] = jnp.transpose(jnp.concatenate(high, axis=1)).astype(bf16)
    low_ref[...] = jnp.transpose(jnp.concatenate(low, axis=1)).astype(bf16)
    final_ref[...] = jnp.concatenate(final, axis=1).astype(bf16)


def rotated(product, cosine, sine, heads):
    columns = []
    for head in range(heads):
        part = product[:, head * HEAD_DIM : (head + 1) * HEAD_DIM]
        columns.append(part * cosine + pltpu.roll(part, HEAD_DIM // 2, 1) * sine)
    return jnp.concatenate(columns, axis=1).astype(bf16)


def query_kernel(*refs, tensors, heads):
    index_ref, pieces, refs = refs[0], refs[1 : 1 + tensors], refs[1 + tensors :]
    (gain_ref, weight_ref, cos_ref, sin_ref, place_ref, meta_ref,
     raw_ref, normed_ref, query_ref, send_ref, buffer_ref, semaphores) = refs
    width = heads * HEAD_DIM
    copies = column_copies(weight_ref, buffer_ref, semaphores, width)
    shard = pieces[0].shape[0]
    for at, piece in enumerate(pieces):
        owner = lax.rem(index_ref[0] + at, tensors)
        raw_ref[pl.ds(pl.multiple_of(owner * shard, shard), shard), :] = piece[...]
    normed_ref[...] = rms(raw_ref[...].astype(f32), gain_ref[...])
    send_ref[:, send_ref.shape[1] - LANES :] = meta_ref[...]
    for at, copy in enumerate(copies):
        copy.wait()
        columns = slice(at * width, (at + 1) * width)
        product = dot(normed_ref[...], buffer_ref[:, columns])
        query = rotated(product, cos_ref[...], sin_ref[...], heads)
        query_ref[:, columns] = query
        send_ref[:, columns] = dot(place_ref[...], query).astype(bf16)


def leaf_kernel(
    normed_ref, query_ref, key_ref, value_ref, cos_ref, sin_ref, out_ref, lse_ref,
    *, heads, leaf_len, scale,
):
    step = pl.program_id(0)
    normed = normed_ref[...]
    rows = normed.shape[0]
    keys = rotated(dot(normed, key_ref[...]), cos_ref[...], sin_ref[...], heads)
    values = dot(normed, value_ref[...]).astype(bf16)
    down, across = iota((rows, 1), 0), iota((1, rows), 1)
    visible = (divided(down, leaf_len)[0] == divided(across, leaf_len)[0]) & (across <= down)
    lane = lax.broadcasted_iota(jnp.int32, (1, LANES), 1)

    @pl.when(step == 0)
    def _():
        lse_ref[...] = jnp.zeros_like(lse_ref)

    for head in range(heads):
        at = slice(head * HEAD_DIM, (head + 1) * HEAD_DIM)
        scores = jnp.where(visible, dot_nt(query_ref[:, at], keys[:, at]) * scale, HIDE)
        highest = jnp.max(scores, axis=1, keepdims=True)
        weights = jnp.exp(scores - highest)
        total = jnp.sum(weights, axis=1, keepdims=True)
        out_ref[:, at] = dot(weights.astype(bf16), values[:, at]) / total
        lse = highest + jnp.log(total)
        lse_ref[...] = jnp.where(lane == step * heads + head, lse, lse_ref[...])


def owner_kernel(
    arrived_ref, kv_ref, back_ref, query_ref, out_ref,
    *, heads, requests, leaf_len, scale,
):
    slot_rows = arrived_ref.shape[0]
    width = heads * HEAD_DIM
    count = requests * leaf_len
    packed = arrived_ref[:, width:]
    meta = packed.astype(f32)
    first = meta[:, 0:1] * 32.0 + meta[:, 1:2]
    used = meta[:, 2:3] + meta[:, 3:4] > 0.0
    begins = [sum(LEVEL_KEYS[:level]) for level in range(3)]
    level = jnp.where(first >= begins[1], 1.0, 0.0) + jnp.where(first >= begins[2], 1.0, 0.0)
    level = jnp.where(used, level, 3.0)
    lane = lax.broadcasted_iota(jnp.int32, (1, LANES), 1)
    of_level = level == lane.astype(f32)
    ahead = one_hot(iota((slot_rows, slot_rows), 1) < iota((slot_rows, slot_rows), 0))
    rank = dot(ahead, one_hot(of_level))
    rank = jnp.sum(jnp.where(of_level, rank, 0.0), axis=1, keepdims=True)
    target = jnp.where(used, level * count + rank, -1.0)
    spread = jnp.where(target == iota((1, 3 * count), 1), 1.0, 0.0)
    ordered = jnp.transpose(spread).astype(bf16)
    query_ref[...] = dot(ordered, arrived_ref[:, :width]).astype(bf16)
    meta = dot(ordered, packed)
    first = meta[:, 0:1] * 32.0 + meta[:, 1:2]
    last = first + meta[:, 2:3] * 32.0 + meta[:, 3:4]
    for level in range(3):
        size = LEVEL_KEYS[level]
        part = slice(level * count, (level + 1) * count)
        keys = slice(begins[level], begins[level] + size)
        key = iota((1, size), 1) + float(begins[level])
        bias = jnp.where((key >= first[part]) & (key < last[part]), 0.0, HIDE)
        ones = jnp.ones((size, HEAD_DIM), bf16)
        sums = jnp.zeros((count, LANES), f32)
        for head in range(heads):
            at = slice(head * HEAD_DIM, (head + 1) * HEAD_DIM)
            scores = dot_nt(query_ref[part, at], kv_ref[0, keys, at]) * (scale * LOG2E) + bias
            highest = jnp.max(scores, axis=1, keepdims=True)
            weights = jnp.exp2(scores - highest).astype(bf16)
            both = dot(weights, jnp.concatenate([kv_ref[1, keys, at], ones], axis=1))
            total = both[:, HEAD_DIM:]
            out_ref[part, at] = (both[:, :HEAD_DIM] / total).astype(bf16)
            lse = highest * LN2 + jnp.log(total)
            lse_high = lse.astype(bf16).astype(f32)
            sums = jnp.where(lane == head, lse_high, sums)
            sums = jnp.where(lane == head + heads, lse - lse_high, sums)
        out_ref[part, width:] = sums.astype(bf16)
    back_ref[...] = dot(spread.astype(bf16), out_ref[...]).astype(bf16)


def column_copies(source_ref, target_ref, semaphores, step):
    copies = []
    for at in range(source_ref.shape[1] // step):
        columns = pl.ds(at * step, step)
        copy = pltpu.make_async_copy(
            source_ref.at[:, columns], target_ref.at[:, columns], semaphores.at[at]
        )
        copy.start()
        copies.append(copy)
    return copies


def merge_kernel(
    after_ref, back_ref, pick_ref, leaf_ref, lse_ref, weight_ref, out_ref, buffer_ref, attended_ref, semaphores,
    *, heads, step,
):
    copies = column_copies(weight_ref, buffer_ref, semaphores, step)
    width = heads * HEAD_DIM
    back = back_ref[...]
    outputs, sums = [leaf_ref[...]], [lse_ref[...]]
    for level in range(3):
        rows = dot(pick_ref[level], back)
        outputs.append(rows[:, :width])
        tail = rows[:, width:]
        sums.append(tail + pltpu.roll(tail, LANES - heads, 1))
    highest = functools.reduce(jnp.maximum, sums)
    scales = [jnp.exp(one - highest) for one in sums]
    total = sum(scales[1:], scales[0])
    scales = [one / total for one in scales]
    for head in range(heads):
        at = slice(head * HEAD_DIM, (head + 1) * HEAD_DIM)
        mixed = sum(scales[i][:, head : head + 1] * outputs[i][:, at] for i in range(4))
        attended_ref[:, at] = mixed.astype(bf16)
    for at, copy in enumerate(copies):
        copy.wait()
        columns = slice(at * step, (at + 1) * step)
        out_ref[:, columns] = dot(attended_ref[...], buffer_ref[:, columns]).astype(bf16)


def middle_kernel(*refs, tensors):
    index_ref, _, raw_ref, gain_ref = refs[:4]
    pieces = refs[4 : 4 + tensors]
    normed_ref, own_ref, resid_own_ref, resid_ref = refs[4 + tensors :]
    width = own_ref.shape[1]
    own = pl.ds(pl.multiple_of(index_ref[0] * width, width), width)
    total = raw_ref[...].astype(f32)
    for piece in pieces:
        total = total + piece[...].astype(f32)
    resid_ref[...] = total
    resid_own_ref[...] = resid_ref[:, own]
    normed_ref[...] = rms(total, gain_ref[...])
    own_ref[...] = normed_ref[:, own]


def dispatch_kernel(after_ref, also_after_ref, send_ref, own_ref, far_ref, out_ref):
    both = jnp.concatenate([own_ref[...], far_ref[...]], axis=0)
    out_ref[...] = dot(send_ref[...], both).astype(bf16)


def shared_kernel(*refs, tensors):
    index_ref, rows_ref, in_hbm_ref, down_hbm_ref = refs[:4]
    pieces, refs = refs[4 : 4 + tensors], refs[4 + tensors :]
    in_ref, down_ref, total_ref, semaphores = refs
    copies = [
        pltpu.make_async_copy(in_hbm_ref.at[0], in_ref.at[0], semaphores.at[0]),
        pltpu.make_async_copy(in_hbm_ref.at[1], in_ref.at[1], semaphores.at[1]),
        pltpu.make_async_copy(down_hbm_ref, down_ref, semaphores.at[2]),
    ]
    for copy in copies:
        copy.start()
    rows = rows_ref[...]
    copies[0].wait()
    gate = dot_nt(rows, in_ref[0])
    copies[1].wait()
    up = dot_nt(rows, in_ref[1])
    hidden = (gate / (1.0 + jnp.exp(-gate)) * up).astype(bf16)
    copies[2].wait()
    total_ref[...] = dot(hidden, down_ref[...])
    width = pieces[0].shape[1]
    for at, piece in enumerate(pieces):
        column = lax.rem(index_ref[0] + at, tensors) * width
        piece[...] = total_ref[:, pl.ds(pl.multiple_of(column, width), width)].astype(bf16)


def load_kernel(after_ref, in_ref, down_ref, in_out_ref, down_out_ref, semaphores):
    copies = [
        pltpu.make_async_copy(in_ref.at[0], in_out_ref, semaphores.at[0]),
        pltpu.make_async_copy(down_ref.at[0], down_out_ref, semaphores.at[1]),
    ]
    for copy in copies:
        copy.start()
    for copy in copies:
        copy.wait()


def rows_of_experts(piece, experts, capacity):
    groups, _, width = piece.shape
    values = piece[...].astype(f32)
    for e in range(experts):
        mine = values[:, e * capacity : (e + 1) * capacity, :].reshape(groups * capacity, width)
        yield mine.astype(bf16)


def expert_kernel(*refs, tensors, experts, capacity):
    index_ref, arrived, refs = refs[0], refs[1 : 1 + tensors], refs[1 + tensors :]
    (first_in_ref, first_down_ref, in_hbm_ref, down_hbm_ref), refs = refs[:4], refs[4:]
    pieces, refs = refs[:tensors], refs[tensors:]
    in_ref, down_ref, rows_ref, total_ref, semaphores = refs
    copies = []
    for e in range(1, experts):
        copies.append(
            (
                pltpu.make_async_copy(in_hbm_ref.at[e], in_ref.at[e - 1], semaphores.at[0, e]),
                pltpu.make_async_copy(down_hbm_ref.at[e], down_ref.at[e - 1], semaphores.at[1, e]),
            )
        )
        for copy in copies[-1]:
            copy.start()
    groups, _, width = arrived[0].shape
    columns = [
        pl.ds(pl.multiple_of(lax.rem(index_ref[0] + at, tensors) * width, width), width)
        for at in range(tensors)
    ]
    for at, piece in enumerate(arrived):
        for e, rows in enumerate(rows_of_experts(piece, experts, capacity)):
            rows_ref[e, :, columns[at]] = rows
    for e in range(experts):
        if e == 0:
            gate_weight, up_weight, down = first_in_ref.at[0], first_in_ref.at[1], first_down_ref
        else:
            gate_weight, up_weight, down = in_ref.at[e - 1, 0], in_ref.at[e - 1, 1], down_ref.at[e - 1]
            copies[e - 1][0].wait()
        gate = dot_nt(rows_ref[e], gate_weight[...])
        up = dot_nt(rows_ref[e], up_weight[...])
        hidden = (gate / (1.0 + jnp.exp(-gate)) * up).astype(bf16)
        if e > 0:
            copies[e - 1][1].wait()
        mine = slice(e * capacity, (e + 1) * capacity)
        for at in range(tensors):
            value = dot(hidden, down[:, columns[at]])
            total_ref[at, :, mine, :] = value.reshape(groups, capacity, width)
    for at, piece in enumerate(pieces):
        piece[...] = total_ref[at].astype(bf16)


def add_kernel(after_ref, *refs):
    out_ref = refs[-1]
    out_ref[...] = sum(piece[...].astype(f32) for piece in refs[:-1]).astype(bf16)


def combine_kernel(*refs, tensors):
    returned_ref, high_ref, low_ref, resid_ref, final_ref = refs[:5]
    shared, out_ref = refs[5 : 5 + tensors], refs[5 + tensors]
    returned = returned_ref[...]
    routed = dot(high_ref[...], returned) + dot(low_ref[...], returned)
    rows = resid_ref.shape[0]
    total = resid_ref[...]
    for piece in shared:
        total = total + piece[...].astype(f32)
    both = jnp.concatenate([total + routed[:rows], routed[rows:]], axis=0).astype(bf16)
    out_ref[...] = dot(final_ref[...], both).astype(bf16)


def settle_kernel(meta_ref, rows_ref, out_ref, *, tensors, leaf_len, groups):
    slot_rows, final_rows = meta_ref.shape[0], rows_ref.shape[0]
    requests, share, _ = out_ref.shape
    width = rows_ref.shape[1]
    tag_down = meta_ref[...].astype(f32)[:, 4:5]
    block, place = divided(iota((1, final_rows), 1), share)
    block, source = divided(block, 2)
    group, half = divided(block, tensors)
    _, home = divided(group + source * (groups // 2), groups)
    tagged = iota((slot_rows, 1), 0) == home * (2.0 * leaf_len)
    tag = jnp.sum(jnp.where(tagged, tag_down, 0.0), axis=0, keepdims=True)
    request, position = divided(iota((requests * share, 1), 0), share)
    wanted = (tag == request + 1.0) & (place == position)
    for at in range(tensors):
        value = dot(one_hot(wanted & (half == at)), rows_ref[...])
        for r in range(requests):
            out_ref[r, :, at * width : (at + 1) * width] = value[
                r * share : (r + 1) * share
            ].astype(bf16)


def on_device(
    leaf_tokens,
    attn_gain,
    w_query,
    w_key,
    w_value,
    w_out,
    prefix_kv,
    prefix_owner,
    prefix_start,
    prefix_len,
    mlp_gain,
    shared_in,
    shared_out,
    expert_in,
    expert_out,
    expert_ids,
    gate_weights,
    request_of,
):
    groups = lax.axis_size("dp")
    tensors = lax.axis_size("tensor")
    index = lax.axis_index("tensor").astype(jnp.int32).reshape(1)
    shard_requests, leaf_len, model_width = leaf_tokens.shape
    requests = prefix_owner.shape[0]
    rows = requests * leaf_len
    local_width = w_query.shape[1]
    local_heads = local_width // HEAD_DIM
    scale = HEAD_DIM ** (-0.5)
    column_share = model_width // tensors
    top_count = expert_ids.shape[2]
    local_experts = expert_in.shape[0]
    experts = local_experts * groups
    assignments = rows * top_count
    capacity = tensors * max(1, assignments * 4 // (experts * 3 * tensors))
    slots = experts * capacity
    slot_rows = groups * 2 * leaf_len
    shape = jax.ShapeDtypeStruct

    raw_pieces = ring_get(leaf_tokens.reshape(shard_requests * leaf_len, model_width), tensors)

    owner_rows, request_row = prefix_owner.T, request_of.reshape(1, requests)
    table_rows = -(-(3 * top_count + 1) // 8) * 8
    place, meta, cosine, sine, table, pick = pl.pallas_call(
        functools.partial(prelude_kernel, leaf_len=leaf_len),
        out_shape=[
            shape((slot_rows, rows), bf16),
            shape((slot_rows, LANES), bf16),
            shape((rows, LANES), f32),
            shape((rows, LANES), f32),
            shape((table_rows, rows), f32),
            shape((3, rows, slot_rows), bf16),
        ],
        in_specs=[whole()] * 6,
        out_specs=[whole()] * 6,
        compiler_params=params(24),
        name="prelude",
    )(
        in_hbm(owner_rows), in_hbm(prefix_start.T), in_hbm(prefix_len.T), in_hbm(request_row),
        in_hbm(jnp.transpose(expert_ids, (2, 0, 1))),
        in_hbm(jnp.transpose(gate_weights, (2, 0, 1))),
    )
    far_table = from_partner(table, groups)

    step_heads = min(2, local_heads)
    step_width = step_heads * HEAD_DIM
    steps = local_heads // step_heads
    query_heads = min(4, local_heads)
    fixed = lambda *dims: pl.BlockSpec(dims, lambda i: (0,) * len(dims))
    columns = lambda *dims: pl.BlockSpec(dims, lambda i: (0,) * (len(dims) - 1) + (i,))
    send_width = local_width + LANES
    raw, normed, query, query_send = pl.pallas_call(
        functools.partial(query_kernel, tensors=tensors, heads=query_heads),
        out_shape=[
            shape((rows, model_width), bf16),
            shape((rows, model_width), bf16),
            shape((rows, local_width), bf16),
            shape((slot_rows, send_width), bf16),
        ],
        in_specs=[scalar()]
        + [whole()] * (tensors + 1)
        + [pl.BlockSpec(memory_space=pltpu.HBM)]
        + [whole()] * 4,
        out_specs=[whole()] * 4,
        scratch_shapes=[
            pltpu.VMEM((model_width, local_width), bf16),
            pltpu.SemaphoreType.DMA((local_heads // query_heads,)),
        ],
        compiler_params=params(24),
        cost_estimate=cost(2 * rows * model_width * local_width, 2 * model_width * local_width),
        name="queries",
    )(
        index, in_hbm(raw_pieces[0]), *raw_pieces[1:], in_hbm(attn_gain.reshape(1, -1)), in_hbm(w_query),
        cosine, sine, place, meta,
    )

    query_arrived = exchange(query_send, groups)

    leaf_out, leaf_lse = pl.pallas_call(
        functools.partial(leaf_kernel, heads=step_heads, leaf_len=leaf_len, scale=scale),
        grid=(steps,),
        out_shape=[shape((rows, local_width), f32), shape((rows, LANES), f32)],
        in_specs=[
            fixed(rows, model_width),
            columns(rows, step_width),
            columns(model_width, step_width),
            columns(model_width, step_width),
            fixed(rows, LANES),
            fixed(rows, LANES),
        ],
        out_specs=[columns(rows, step_width), fixed(rows, LANES)],
        compiler_params=params(24, 1),
        cost_estimate=cost(4 * rows * model_width * local_width, 4 * model_width * local_width),
        name="leaf",
    )(normed, query, in_hbm(w_key), in_hbm(w_value), cosine, sine)

    pool = prefix_kv.shape[1]
    back_send = pl.pallas_call(
        functools.partial(
            owner_kernel, heads=local_heads, requests=requests, leaf_len=leaf_len, scale=scale
        ),
        out_shape=shape((slot_rows, send_width), bf16),
        in_specs=[whole()] * 2,
        out_specs=whole(),
        scratch_shapes=[
            pltpu.VMEM((3 * rows, local_width), bf16),
            pltpu.VMEM((3 * rows, send_width), bf16),
        ],
        compiler_params=params(32),
        cost_estimate=cost(4 * slot_rows * pool * local_width, 4 * pool * local_width),
        name="owner",
    )(query_arrived, prefix_kv)

    back = exchange(back_send, groups)

    out_step = min(512, model_width)
    partial_out = pl.pallas_call(
        functools.partial(merge_kernel, heads=local_heads, step=out_step),
        out_shape=shape((rows, model_width), bf16),
        in_specs=[pl.BlockSpec(memory_space=pl.ANY)]
        + [whole()] * 4
        + [pl.BlockSpec(memory_space=pltpu.HBM)],
        out_specs=whole(),
        scratch_shapes=[
            pltpu.VMEM((local_width, model_width), bf16),
            pltpu.VMEM((rows, local_width), bf16),
            pltpu.SemaphoreType.DMA((model_width // out_step,)),
        ],
        compiler_params=params(24),
        cost_estimate=cost(2 * rows * local_width * model_width, 2 * local_width * model_width),
        name="merge",
    )(far_table, back, pick, leaf_out, leaf_lse, in_hbm(w_out))

    out_pieces = ring_get(partial_out, tensors)

    half = (lax.axis_index("dp") // (groups // 2)).astype(jnp.int32).reshape(1)
    send, gate_high, gate_low, final = pl.pallas_call(
        functools.partial(
            routing_kernel, tensors=tensors, leaf_len=leaf_len, groups=groups,
            capacity=capacity, experts=experts, choices=top_count,
        ),
        out_shape=[
            shape((slots, 2 * rows), bf16),
            shape((2 * rows, slots), bf16),
            shape((2 * rows, slots), bf16),
            shape((slot_rows, 2 * rows), bf16),
        ],
        in_specs=[scalar(), pl.BlockSpec(memory_space=pl.ANY)] + [whole()] * 2,
        out_specs=[whole()] * 4,
        compiler_params=params(16),
        cost_estimate=cost(1, 1),
        name="routing",
    )(half, partial_out, table, far_table)

    normed_mlp, own_columns, resid_own = pl.pallas_call(
        functools.partial(middle_kernel, tensors=tensors),
        out_shape=[
            shape((rows, model_width), bf16),
            shape((rows, column_share), bf16),
            shape((rows, column_share), f32),
        ],
        in_specs=[scalar(), pl.BlockSpec(memory_space=pl.ANY)] + [whole()] * (2 + tensors),
        out_specs=[whole()] * 3,
        scratch_shapes=[pltpu.VMEM((rows, model_width), f32)],
        compiler_params=params(24),
        name="middle",
    )(index, send, raw, mlp_gain.reshape(1, -1), *out_pieces)

    far_columns = from_partner(own_columns, groups)
    hbm = pl.BlockSpec(memory_space=pltpu.HBM)
    hidden = shared_out.shape[0]
    shared_pieces = pl.pallas_call(
        functools.partial(shared_kernel, tensors=tensors),
        out_shape=[shape((rows, column_share), bf16)] * tensors,
        in_specs=[scalar(), whole(), hbm, hbm],
        out_specs=[whole()] * tensors,
        scratch_shapes=[
            pltpu.VMEM((2, hidden, model_width), bf16),
            pltpu.VMEM((hidden, model_width), bf16),
            pltpu.VMEM((rows, model_width), f32),
            pltpu.SemaphoreType.DMA((3,)),
        ],
        compiler_params=params(16),
        cost_estimate=cost(1, 1),
        name="shared",
    )(index, normed_mlp, in_hbm(jnp.transpose(shared_in, (1, 2, 0))), in_hbm(shared_out))
    expert_hidden = expert_out.shape[1]
    expert_in = in_hbm(jnp.transpose(expert_in, (0, 2, 3, 1)))
    expert_out = in_hbm(expert_out)
    first_in, first_down = pl.pallas_call(
        load_kernel,
        out_shape=[
            pltpu.VMEM((2, expert_hidden, model_width), bf16),
            pltpu.VMEM((expert_hidden, model_width), bf16),
        ],
        in_specs=[pl.BlockSpec(memory_space=pl.ANY), hbm, hbm],
        out_specs=[whole()] * 2,
        scratch_shapes=[pltpu.SemaphoreType.DMA((2,))],
        compiler_params=params(1),
        cost_estimate=cost(1, 1),
        name="load",
    )(normed_mlp, expert_in, expert_out)

    send_rows = pl.pallas_call(
        dispatch_kernel,
        out_shape=shape((slots, column_share), bf16),
        in_specs=[pl.BlockSpec(memory_space=pl.ANY)] * 2 + [whole()] * 3,
        out_specs=whole(),
        compiler_params=params(8),
        name="dispatch",
    )(shared_pieces[0], first_down, send, own_columns, far_columns)

    arrived = exchange(send_rows, groups, halves=True)

    block = local_experts * capacity
    arrived_pieces = ring_get(arrived.reshape(groups, block, column_share), tensors)
    partial_pieces = pl.pallas_call(
        functools.partial(
            expert_kernel, tensors=tensors, experts=local_experts, capacity=capacity
        ),
        out_shape=[shape((groups, block, column_share), bf16)] * tensors,
        in_specs=[scalar()] + [whole()] * (tensors + 2) + [hbm, hbm],
        out_specs=[whole()] * tensors,
        scratch_shapes=[
            pltpu.VMEM((local_experts - 1, 2, expert_hidden, model_width), bf16),
            pltpu.VMEM((local_experts - 1, expert_hidden, model_width), bf16),
            pltpu.VMEM((local_experts, groups * capacity, model_width), bf16),
            pltpu.VMEM((tensors, groups, block, column_share), f32),
            pltpu.SemaphoreType.DMA((2, local_experts)),
        ],
        compiler_params=params(35),
        cost_estimate=cost(
            6 * slots * expert_hidden * model_width,
            6 * local_experts * expert_hidden * model_width,
        ),
        name="experts",
    )(
        index,
        *arrived_pieces,
        pltpu.with_memory_space_constraint(first_in, pltpu.VMEM),
        pltpu.with_memory_space_constraint(first_down, pltpu.VMEM),
        expert_in,
        expert_out,
    )
    partial_pieces, shared_pieces = lax.optimization_barrier((partial_pieces, shared_pieces))
    shared_pieces = ring_send(shared_pieces)
    partial_pieces = ring_send(partial_pieces)
    summed = pl.pallas_call(
        add_kernel,
        out_shape=shape((groups, block, column_share), bf16),
        in_specs=[pl.BlockSpec(memory_space=pl.ANY)] + [whole()] * tensors,
        out_specs=whole(),
        compiler_params=params(12),
        name="add",
    )(shared_pieces[-1], *partial_pieces)

    returned = exchange(summed.reshape(slots, column_share), groups, halves=True)

    final_send = pl.pallas_call(
        functools.partial(combine_kernel, tensors=tensors),
        out_shape=shape((slot_rows, column_share), bf16),
        in_specs=[whole()] * (5 + tensors),
        out_specs=whole(),
        compiler_params=params(24),
        name="combine",
    )(returned, gate_high, gate_low, resid_own, final, *shared_pieces)

    devices = groups * tensors
    blocks = final_send.reshape(devices, slot_rows // devices, column_share)
    final_arrived = lax.all_to_all(
        blocks, ("dp", "tensor"), split_axis=0, concat_axis=0, tiled=True
    ).reshape(slot_rows, column_share)

    return pl.pallas_call(
        functools.partial(settle_kernel, tensors=tensors, leaf_len=leaf_len, groups=groups),
        grid=(1,),
        out_shape=shape((requests, leaf_len // tensors, model_width), bf16),
        in_specs=[
            pl.BlockSpec((slot_rows, LANES), lambda i: (0, local_heads)),
            fixed(slot_rows, column_share),
        ],
        out_specs=fixed(requests, leaf_len // tensors, model_width),
        compiler_params=params(16, 1),
        name="settle",
    )(query_arrived, final_arrived)


def solution(mesh):
    in_specs = (
        P(("dp", "tensor"), None, None),
        P(),
        P(None, "tensor"),
        P(None, "tensor"),
        P(None, "tensor"),
        P("tensor", None),
        P(None, "dp", "tensor"),
        P("dp", None),
        P("dp", None),
        P("dp", None),
        P(),
        P(None, None, "tensor"),
        P("tensor", None),
        P("dp", None, None, "tensor"),
        P("dp", "tensor", None),
        P("dp", None, None),
        P("dp", None, None),
        P("dp"),
    )
    out_specs = P("dp", "tensor", None)
    return jax.shard_map(
        on_device, mesh=mesh, in_specs=in_specs, out_specs=out_specs, check_vma=False
    )
```

```python
import functools
import math

import jax
import jax.numpy as jnp
from jax import lax
from jax.experimental import pallas as pl
from jax.experimental.pallas import tpu as pltpu
from jax.sharding import PartitionSpec as P

HEAD_DIM = 128
EPS = 1e-06
ROPE_BASE = 10000.0
LANES = 128
HIDE = -1e30
LOG2E = 1.4426950408889634
LN2 = 0.6931471805599453
LEVEL_KEYS = (512, 256, 128)
MIB = 1 << 20

f32 = jnp.float32
bf16 = jnp.bfloat16


def dot(a, b):
    return lax.dot_general(a, b, (((1,), (0,)), ((), ())), preferred_element_type=f32)


def dot_nt(a, b):
    return lax.dot_general(a, b, (((1,), (1,)), ((), ())), preferred_element_type=f32)


def iota(shape, dim):
    return lax.broadcasted_iota(jnp.int32, shape, dim).astype(f32)


def divided(index, by):
    quotient = jnp.floor((index + 0.5) * (1.0 / by))
    return quotient, index - by * quotient


def one_hot(condition):
    return jnp.where(condition, 1.0, 0.0).astype(bf16)


def rms(values, gain):
    mean_square = jnp.mean(values * values, axis=-1, keepdims=True)
    return (values * lax.rsqrt(mean_square + EPS) * gain).astype(bf16)


def ring_get(piece, count):
    pieces = [piece]
    for step in range(1, count):
        pieces.append(
            lax.ppermute(piece, "tensor", [((i + step) % count, i) for i in range(count)])
        )
    return pieces


def ring_send(pieces):
    count = len(pieces)
    arrived = [pieces[0]]
    for step in range(1, count):
        arrived.append(
            lax.ppermute(pieces[step], "tensor", [(i, (i + step) % count) for i in range(count)])
        )
    return arrived


def exchange(rows, groups, halves=False):
    size = groups // 2 if halves else groups
    blocks = rows.reshape(size, rows.shape[0] // size, rows.shape[1])
    parts = [list(range(size)), list(range(size, groups))] if halves else None
    return lax.all_to_all(
        blocks, "dp", split_axis=0, concat_axis=0, tiled=True, axis_index_groups=parts
    ).reshape(rows.shape)


def from_partner(array, groups):
    return lax.ppermute(array, "dp", [(i, (i + groups // 2) % groups) for i in range(groups)])


def in_hbm(array):
    return pltpu.with_memory_space_constraint(array, pltpu.HBM)


def whole():
    return pl.BlockSpec(memory_space=pltpu.VMEM)


def scalar():
    return pl.BlockSpec(memory_space=pltpu.SMEM)


def params(mib, grid=0):
    return pltpu.CompilerParams(
        vmem_limit_bytes=mib * MIB,
        dimension_semantics=("arbitrary",) * grid if grid else None,
    )


def cost(flops, nbytes):
    return pl.CostEstimate(flops=int(flops), bytes_accessed=int(nbytes), transcendentals=0)


def upright(row):
    size = row.shape[1]
    diagonal = iota((size, size), 0) == iota((size, size), 1)
    return jnp.sum(jnp.where(diagonal, row, 0.0), axis=1, keepdims=True)


def in_rows(values, leaf_len):
    choices, requests, _ = values.shape
    rows = requests * leaf_len
    request_of_row, token_of_row = divided(iota((1, rows), 1), leaf_len)
    flat = values.astype(f32).reshape(choices * requests, leaf_len).astype(bf16)
    spread = dot(flat, one_hot(iota((leaf_len, 1), 0) == token_of_row))
    _, request = divided(iota((choices * requests, 1), 0), requests)
    kept = jnp.where(request == request_of_row, spread, 0.0)
    return jnp.sum(kept.reshape(choices, requests, rows), axis=1)


def across_rows(column):
    size = column.shape[0]
    diagonal = iota((size, size), 0) == iota((size, size), 1)
    return jnp.sum(jnp.where(diagonal, column, 0.0), axis=0, keepdims=True)


def owner_slots(owner):
    rows = []
    for level in range(3):
        mine, repeated = owner[level : level + 1], 0.0
        for earlier in range(level):
            same = upright(owner[earlier : earlier + 1]) == mine
            repeated = repeated + jnp.max(jnp.where(same, 1.0, 0.0), axis=0, keepdims=True)
        rows.append(mine * 2.0 + repeated)
    return rows


def prelude_kernel(
    owner_ref, start_ref, length_ref, request_ref, ids_ref, gates_ref,
    place_ref, meta_ref, cos_ref, sin_ref, table_ref, pick_ref,
    *, leaf_len,
):
    requests = owner_ref.shape[1]
    slot_rows, rows = place_ref.shape
    start, length = start_ref[...].astype(f32), length_ref[...].astype(f32)
    row_slot, row_token = divided(iota((slot_rows, 1), 0), leaf_len)
    request_of_row, token_of_row = divided(iota((1, rows), 1), leaf_len)
    row_request, row_place = divided(iota((rows, 1), 0), leaf_len)
    mine = iota((1, requests), 1) == row_request
    slot_across, token_across = divided(iota((1, slot_rows), 1), leaf_len)
    named, first_key, key_count = 0.0, 0.0, 0.0
    for level, slot in enumerate(owner_slots(owner_ref[...].astype(f32))):
        slot_down = jnp.sum(jnp.where(mine, slot, 0.0), axis=1, keepdims=True)
        pick_ref[level] = one_hot((slot_down == slot_across) & (row_place == token_across))
        here = jnp.where(slot == row_slot, 1.0, 0.0)
        named = named + here
        first_key = first_key + here * start[level : level + 1]
        key_count = key_count + here * length[level : level + 1]
    placed = dot(named.astype(bf16), one_hot(iota((requests, 1), 0) == request_of_row))
    place_ref[...] = jnp.where(row_token == token_of_row, placed, 0.0).astype(bf16)

    first_key = jnp.sum(first_key, axis=1, keepdims=True)
    key_count = jnp.sum(key_count, axis=1, keepdims=True)
    dest, place = divided(request_ref[...].astype(f32), requests)
    row_group, _ = divided(row_slot, 2)
    tag = jnp.sum(jnp.where(dest == row_group, place + 1.0, 0.0), axis=1, keepdims=True)
    lane = iota((1, LANES), 1)
    meta = jnp.zeros((slot_rows, LANES), f32)
    for at, value in enumerate(divided(first_key, 32) + divided(key_count, 32) + (tag,)):
        meta = jnp.where(lane == at, value, meta)
    meta_ref[...] = meta.astype(bf16)

    offsets = length[0:1] + length[1:2] + length[2:3]
    position = jnp.sum(jnp.where(mine, offsets, 0.0), axis=1, keepdims=True) + row_place
    half = HEAD_DIM // 2
    pair = jnp.where(lane < half, lane, lane - half)
    angle = position * jnp.exp(pair * (-2.0 * math.log(ROPE_BASE) / HEAD_DIM))
    cos_ref[...] = jnp.cos(angle)
    sin_ref[...] = jnp.sin(angle) * jnp.where(lane < half, -1.0, 1.0)

    gates = gates_ref[...]
    gates_high = gates.astype(bf16).astype(f32)
    choices = gates.shape[0]
    for at, values in enumerate((ids_ref[...], gates_high, gates - gates_high)):
        table_ref[at * choices : (at + 1) * choices, :] = in_rows(values, leaf_len)
    dest_down = jnp.sum(jnp.where(mine, dest, 0.0), axis=1, keepdims=True)
    last = 3 * choices
    size = table_ref.shape[0] - last
    table_ref[last:, :] = jnp.broadcast_to(across_rows(dest_down), (size, rows))


def routing_kernel(
    half_ref, after_ref, table_ref, far_table_ref,
    send_ref, high_ref, low_ref, final_ref,
    *, tensors, leaf_len, groups, capacity, experts, choices,
):
    rows = table_ref.shape[1]
    final_rows = final_ref.shape[0]
    share = leaf_len // tensors
    _, token_of_row = divided(iota((1, rows), 1), leaf_len)

    slots = send_ref.shape[0]
    local = experts // groups
    block, slot_place = divided(iota((slots, 1), 0), capacity)
    block, local_expert = divided(block, local)
    device, slot_source = divided(block, 2)
    first_expert = (half_ref[0] * (experts // 2)).astype(f32)
    spread = one_hot(first_expert + device * local + local_expert == iota((1, experts), 1))
    expert_down = iota((experts, 1), 0)
    ahead = one_hot(iota((rows, rows), 0) < iota((rows, rows), 1))
    block, final_place = divided(iota((final_rows, 1), 0), share)
    block, final_source = divided(block, 2)
    final_group, final_half = divided(block, tensors)
    final_token = final_half * share + final_place
    send, high, low, final = [], [], [], []
    for source, table in enumerate((table_ref[...], far_table_ref[...])):
        member, gate_high, gate_low = 0.0, 0.0, 0.0
        for choice in range(choices):
            hit = jnp.where(table[choice : choice + 1] == expert_down, 1.0, 0.0)
            member = member + hit
            gate_high = gate_high + hit * table[choices + choice : choices + choice + 1]
            gate_low = gate_low + hit * table[2 * choices + choice : 2 * choices + choice + 1]
        member = member.astype(bf16)
        before = dot(member, ahead).astype(bf16)
        taken = (dot(spread, member) > 0.5) & (dot(spread, before) == slot_place)
        taken = taken & (slot_source == source)
        send.append(jnp.where(taken, 1.0, 0.0))
        high.append(jnp.where(taken, dot(spread, gate_high.astype(bf16)), 0.0))
        low.append(jnp.where(taken, dot(spread, gate_low.astype(bf16)), 0.0))
        going = (table[3 * choices : 3 * choices + 1] == final_group) & (final_source == source)
        final.append(jnp.where(going & (final_token == token_of_row), 1.0, 0.0))
    send_ref[...] = jnp.concatenate(send, axis=1).astype(bf16)
    high_ref[...] = jnp.transpose(jnp.concatenate(high, axis=1)).astype(bf16)
    low_ref[...] = jnp.transpose(jnp.concatenate(low, axis=1)).astype(bf16)
    final_ref[...] = jnp.concatenate(final, axis=1).astype(bf16)


def rotated(product, cosine, sine, heads):
    columns = []
    for head in range(heads):
        part = product[:, head * HEAD_DIM : (head + 1) * HEAD_DIM]
        columns.append(part * cosine + pltpu.roll(part, HEAD_DIM // 2, 1) * sine)
    return jnp.concatenate(columns, axis=1).astype(bf16)


def query_kernel(*refs, tensors, heads):
    index_ref, pieces, refs = refs[0], refs[1 : 1 + tensors], refs[1 + tensors :]
    (gain_ref, weight_ref, cos_ref, sin_ref, place_ref, meta_ref,
     raw_ref, normed_ref, query_ref, send_ref, buffer_ref, semaphores) = refs
    width = heads * HEAD_DIM
    copies = column_copies(weight_ref, buffer_ref, semaphores, width)
    shard = pieces[0].shape[0]
    for at, piece in enumerate(pieces):
        owner = lax.rem(index_ref[0] + at, tensors)
        raw_ref[pl.ds(pl.multiple_of(owner * shard, shard), shard), :] = piece[...]
    normed_ref[...] = rms(raw_ref[...].astype(f32), gain_ref[...])
    send_ref[:, send_ref.shape[1] - LANES :] = meta_ref[...]
    for at, copy in enumerate(copies):
        copy.wait()
        columns = slice(at * width, (at + 1) * width)
        product = dot(normed_ref[...], buffer_ref[:, columns])
        query = rotated(product, cos_ref[...], sin_ref[...], heads)
        query_ref[:, columns] = query
        send_ref[:, columns] = dot(place_ref[...], query).astype(bf16)


def leaf_kernel(
    normed_ref, query_ref, key_ref, value_ref, cos_ref, sin_ref, out_ref, lse_ref,
    *, heads, leaf_len, scale,
):
    step = pl.program_id(0)
    normed = normed_ref[...]
    rows = normed.shape[0]
    keys = rotated(dot(normed, key_ref[...]), cos_ref[...], sin_ref[...], heads)
    values = dot(normed, value_ref[...]).astype(bf16)
    down, across = iota((rows, 1), 0), iota((1, rows), 1)
    visible = (divided(down, leaf_len)[0] == divided(across, leaf_len)[0]) & (across <= down)
    lane = lax.broadcasted_iota(jnp.int32, (1, LANES), 1)

    @pl.when(step == 0)
    def _():
        lse_ref[...] = jnp.zeros_like(lse_ref)

    for head in range(heads):
        at = slice(head * HEAD_DIM, (head + 1) * HEAD_DIM)
        scores = jnp.where(visible, dot_nt(query_ref[:, at], keys[:, at]) * scale, HIDE)
        highest = jnp.max(scores, axis=1, keepdims=True)
        weights = jnp.exp(scores - highest)
        total = jnp.sum(weights, axis=1, keepdims=True)
        out_ref[:, at] = dot(weights.astype(bf16), values[:, at]) / total
        lse = highest + jnp.log(total)
        lse_ref[...] = jnp.where(lane == step * heads + head, lse, lse_ref[...])


def owner_kernel(
    arrived_ref, kv_ref, back_ref, query_ref, out_ref,
    *, heads, requests, leaf_len, scale,
):
    slot_rows = arrived_ref.shape[0]
    width = heads * HEAD_DIM
    count = requests * leaf_len
    packed = arrived_ref[:, width:]
    meta = packed.astype(f32)
    first = meta[:, 0:1] * 32.0 + meta[:, 1:2]
    used = meta[:, 2:3] + meta[:, 3:4] > 0.0
    begins = [sum(LEVEL_KEYS[:level]) for level in range(3)]
    level = jnp.where(first >= begins[1], 1.0, 0.0) + jnp.where(first >= begins[2], 1.0, 0.0)
    level = jnp.where(used, level, 3.0)
    lane = lax.broadcasted_iota(jnp.int32, (1, LANES), 1)
    of_level = level == lane.astype(f32)
    ahead = one_hot(iota((slot_rows, slot_rows), 1) < iota((slot_rows, slot_rows), 0))
    rank = dot(ahead, one_hot(of_level))
    rank = jnp.sum(jnp.where(of_level, rank, 0.0), axis=1, keepdims=True)
    target = jnp.where(used, level * count + rank, -1.0)
    spread = jnp.where(target == iota((1, 3 * count), 1), 1.0, 0.0)
    ordered = jnp.transpose(spread).astype(bf16)
    query_ref[...] = dot(ordered, arrived_ref[:, :width]).astype(bf16)
    meta = dot(ordered, packed)
    first = meta[:, 0:1] * 32.0 + meta[:, 1:2]
    last = first + meta[:, 2:3] * 32.0 + meta[:, 3:4]
    for level in range(3):
        size = LEVEL_KEYS[level]
        part = slice(level * count, (level + 1) * count)
        keys = slice(begins[level], begins[level] + size)
        key = iota((1, size), 1) + float(begins[level])
        bias = jnp.where((key >= first[part]) & (key < last[part]), 0.0, HIDE)
        ones = jnp.ones((size, HEAD_DIM), bf16)
        sums = jnp.zeros((count, LANES), f32)
        for head in range(heads):
            at = slice(head * HEAD_DIM, (head + 1) * HEAD_DIM)
            scores = dot_nt(query_ref[part, at], kv_ref[0, keys, at]) * (scale * LOG2E) + bias
            highest = jnp.max(scores, axis=1, keepdims=True)
            weights = jnp.exp2(scores - highest).astype(bf16)
            both = dot(weights, jnp.concatenate([kv_ref[1, keys, at], ones], axis=1))
            total = both[:, HEAD_DIM:]
            out_ref[part, at] = (both[:, :HEAD_DIM] / total).astype(bf16)
            lse = highest * LN2 + jnp.log(total)
            lse_high = lse.astype(bf16).astype(f32)
            sums = jnp.where(lane == head, lse_high, sums)
            sums = jnp.where(lane == head + heads, lse - lse_high, sums)
        out_ref[part, width:] = sums.astype(bf16)
    back_ref[...] = dot(spread.astype(bf16), out_ref[...]).astype(bf16)


def column_copies(source_ref, target_ref, semaphores, step):
    copies = []
    for at in range(source_ref.shape[1] // step):
        columns = pl.ds(at * step, step)
        copy = pltpu.make_async_copy(
            source_ref.at[:, columns], target_ref.at[:, columns], semaphores.at[at]
        )
        copy.start()
        copies.append(copy)
    return copies


def merge_kernel(
    after_ref, back_ref, pick_ref, leaf_ref, lse_ref, weight_ref, out_ref, buffer_ref, attended_ref, semaphores,
    *, heads, step,
):
    copies = column_copies(weight_ref, buffer_ref, semaphores, step)
    width = heads * HEAD_DIM
    back = back_ref[...]
    outputs, sums = [leaf_ref[...]], [lse_ref[...]]
    for level in range(3):
        rows = dot(pick_ref[level], back)
        outputs.append(rows[:, :width])
        tail = rows[:, width:]
        sums.append(tail + pltpu.roll(tail, LANES - heads, 1))
    highest = functools.reduce(jnp.maximum, sums)
    scales = [jnp.exp(one - highest) for one in sums]
    total = sum(scales[1:], scales[0])
    scales = [one / total for one in scales]
    for head in range(heads):
        at = slice(head * HEAD_DIM, (head + 1) * HEAD_DIM)
        mixed = sum(scales[i][:, head : head + 1] * outputs[i][:, at] for i in range(4))
        attended_ref[:, at] = mixed.astype(bf16)
    for at, copy in enumerate(copies):
        copy.wait()
        columns = slice(at * step, (at + 1) * step)
        out_ref[:, columns] = dot(attended_ref[...], buffer_ref[:, columns]).astype(bf16)


def middle_kernel(*refs, tensors):
    index_ref, _, raw_ref, gain_ref = refs[:4]
    pieces = refs[4 : 4 + tensors]
    normed_ref, own_ref, resid_own_ref, resid_ref = refs[4 + tensors :]
    width = own_ref.shape[1]
    own = pl.ds(pl.multiple_of(index_ref[0] * width, width), width)
    total = raw_ref[...].astype(f32)
    for piece in pieces:
        total = total + piece[...].astype(f32)
    resid_ref[...] = total
    resid_own_ref[...] = resid_ref[:, own]
    normed_ref[...] = rms(total, gain_ref[...])
    own_ref[...] = normed_ref[:, own]


def dispatch_kernel(after_ref, also_after_ref, send_ref, own_ref, far_ref, out_ref):
    both = jnp.concatenate([own_ref[...], far_ref[...]], axis=0)
    out_ref[...] = dot(send_ref[...], both).astype(bf16)


def shared_kernel(*refs, tensors):
    index_ref, rows_ref, in_hbm_ref, down_hbm_ref, expert_in_ref, expert_down_ref = refs[:6]
    pieces, refs = refs[6 : 6 + tensors], refs[6 + tensors :]
    early_in_ref, early_down_ref, in_ref, down_ref, total_ref, semaphores = refs
    early = early_in_ref.shape[0]
    copies = [
        pltpu.make_async_copy(in_hbm_ref.at[0], in_ref.at[0], semaphores.at[0]),
        pltpu.make_async_copy(in_hbm_ref.at[1], in_ref.at[1], semaphores.at[1]),
        pltpu.make_async_copy(down_hbm_ref, down_ref, semaphores.at[2]),
        pltpu.make_async_copy(expert_in_ref.at[0:early], early_in_ref, semaphores.at[3]),
        pltpu.make_async_copy(expert_down_ref.at[0], early_down_ref, semaphores.at[4]),
    ]
    for copy in copies:
        copy.start()
    rows = rows_ref[...]
    copies[0].wait()
    gate = dot_nt(rows, in_ref[0])
    copies[1].wait()
    up = dot_nt(rows, in_ref[1])
    hidden = (gate / (1.0 + jnp.exp(-gate)) * up).astype(bf16)
    copies[2].wait()
    total_ref[...] = dot(hidden, down_ref[...])
    width = pieces[0].shape[1]
    for at, piece in enumerate(pieces):
        column = lax.rem(index_ref[0] + at, tensors) * width
        piece[...] = total_ref[:, pl.ds(pl.multiple_of(column, width), width)].astype(bf16)
    copies[3].wait()
    copies[4].wait()


def rows_of_experts(piece, experts, capacity):
    groups, _, width = piece.shape
    values = piece[...].astype(f32)
    for e in range(experts):
        mine = values[:, e * capacity : (e + 1) * capacity, :].reshape(groups * capacity, width)
        yield mine.astype(bf16)


def expert_kernel(*refs, tensors, experts, capacity):
    index_ref, arrived, refs = refs[0], refs[1 : 1 + tensors], refs[1 + tensors :]
    (early_in_ref, early_down_ref, in_hbm_ref, down_hbm_ref), refs = refs[:4], refs[4:]
    pieces, refs = refs[:tensors], refs[tensors:]
    in_ref, down_ref, rows_ref, semaphores = refs
    early = early_in_ref.shape[0]
    in_copies, down_copies = {}, {}
    for e in range(1, experts):
        down_copies[e] = pltpu.make_async_copy(
            down_hbm_ref.at[e], down_ref.at[e - 1], semaphores.at[0, e]
        )
        if e >= early:
            in_copies[e] = pltpu.make_async_copy(
                in_hbm_ref.at[e], in_ref.at[e - early], semaphores.at[1, e]
            )
            in_copies[e].start()
        down_copies[e].start()
    groups, _, width = arrived[0].shape
    columns = [
        pl.ds(pl.multiple_of(lax.rem(index_ref[0] + at, tensors) * width, width), width)
        for at in range(tensors)
    ]
    for at, piece in enumerate(arrived):
        for e, rows in enumerate(rows_of_experts(piece, experts, capacity)):
            rows_ref[e, :, columns[at]] = rows
    together = max(1, 16 // capacity)
    values = []
    for e in range(experts):
        if e < early:
            weights = early_in_ref.at[e]
        else:
            weights = in_ref.at[e - early]
            in_copies[e].wait()
        down = early_down_ref if e == 0 else down_ref.at[e - 1]
        gate = dot_nt(rows_ref[e], weights[0])
        up = dot_nt(rows_ref[e], weights[1])
        hidden = (gate / (1.0 + jnp.exp(-gate)) * up).astype(bf16)
        if e > 0:
            down_copies[e].wait()
        values.append(
            [
                dot(hidden, down[:, columns[at]]).reshape(groups, capacity, width)
                for at in range(tensors)
            ]
        )
        if len(values) == together or e == experts - 1:
            mine = slice((e + 1 - len(values)) * capacity, (e + 1) * capacity)
            for at, piece in enumerate(pieces):
                parts = [value[at] for value in values]
                piece[:, mine, :] = jnp.concatenate(parts, axis=1).astype(bf16)
            values = []


def add_kernel(after_ref, *refs):
    out_ref = refs[-1]
    out_ref[...] = sum(piece[...].astype(f32) for piece in refs[:-1]).astype(bf16)


def combine_kernel(*refs, tensors):
    returned_ref, high_ref, low_ref, resid_ref, final_ref = refs[:5]
    shared, out_ref = refs[5 : 5 + tensors], refs[5 + tensors]
    returned = returned_ref[...]
    routed = dot(high_ref[...], returned) + dot(low_ref[...], returned)
    rows = resid_ref.shape[0]
    total = resid_ref[...]
    for piece in shared:
        total = total + piece[...].astype(f32)
    both = jnp.concatenate([total + routed[:rows], routed[rows:]], axis=0).astype(bf16)
    out_ref[...] = dot(final_ref[...], both).astype(bf16)


def settle_kernel(meta_ref, rows_ref, out_ref, *, tensors, leaf_len, groups):
    slot_rows, final_rows = meta_ref.shape[0], rows_ref.shape[0]
    requests, share, _ = out_ref.shape
    width = rows_ref.shape[1]
    tag_down = meta_ref[...].astype(f32)[:, 4:5]
    block, place = divided(iota((1, final_rows), 1), share)
    block, source = divided(block, 2)
    group, half = divided(block, tensors)
    _, home = divided(group + source * (groups // 2), groups)
    tagged = iota((slot_rows, 1), 0) == home * (2.0 * leaf_len)
    tag = jnp.sum(jnp.where(tagged, tag_down, 0.0), axis=0, keepdims=True)
    request, position = divided(iota((requests * share, 1), 0), share)
    wanted = (tag == request + 1.0) & (place == position)
    for at in range(tensors):
        value = dot(one_hot(wanted & (half == at)), rows_ref[...])
        for r in range(requests):
            out_ref[r, :, at * width : (at + 1) * width] = value[
                r * share : (r + 1) * share
            ].astype(bf16)


def on_device(
    leaf_tokens,
    attn_gain,
    w_query,
    w_key,
    w_value,
    w_out,
    prefix_kv,
    prefix_owner,
    prefix_start,
    prefix_len,
    mlp_gain,
    shared_in,
    shared_out,
    expert_in,
    expert_out,
    expert_ids,
    gate_weights,
    request_of,
):
    groups = lax.axis_size("dp")
    tensors = lax.axis_size("tensor")
    index = lax.axis_index("tensor").astype(jnp.int32).reshape(1)
    shard_requests, leaf_len, model_width = leaf_tokens.shape
    requests = prefix_owner.shape[0]
    rows = requests * leaf_len
    local_width = w_query.shape[1]
    local_heads = local_width // HEAD_DIM
    scale = HEAD_DIM ** (-0.5)
    column_share = model_width // tensors
    top_count = expert_ids.shape[2]
    local_experts = expert_in.shape[0]
    experts = local_experts * groups
    assignments = rows * top_count
    capacity = tensors * max(1, assignments * 4 // (experts * 3 * tensors))
    slots = experts * capacity
    slot_rows = groups * 2 * leaf_len
    shape = jax.ShapeDtypeStruct

    raw_pieces = ring_get(leaf_tokens.reshape(shard_requests * leaf_len, model_width), tensors)

    owner_rows, request_row = prefix_owner.T, request_of.reshape(1, requests)
    table_rows = -(-(3 * top_count + 1) // 8) * 8
    place, meta, cosine, sine, table, pick = pl.pallas_call(
        functools.partial(prelude_kernel, leaf_len=leaf_len),
        out_shape=[
            shape((slot_rows, rows), bf16),
            shape((slot_rows, LANES), bf16),
            shape((rows, LANES), f32),
            shape((rows, LANES), f32),
            shape((table_rows, rows), f32),
            shape((3, rows, slot_rows), bf16),
        ],
        in_specs=[whole()] * 6,
        out_specs=[whole()] * 6,
        compiler_params=params(4),
        name="prelude",
    )(
        in_hbm(owner_rows), in_hbm(prefix_start.T), in_hbm(prefix_len.T), in_hbm(request_row),
        in_hbm(jnp.transpose(expert_ids, (2, 0, 1))),
        in_hbm(jnp.transpose(gate_weights, (2, 0, 1))),
    )
    far_table = from_partner(table, groups)

    step_heads = min(2, local_heads)
    step_width = step_heads * HEAD_DIM
    steps = local_heads // step_heads
    query_heads = min(4, local_heads)
    fixed = lambda *dims: pl.BlockSpec(dims, lambda i: (0,) * len(dims))
    columns = lambda *dims: pl.BlockSpec(dims, lambda i: (0,) * (len(dims) - 1) + (i,))
    send_width = local_width + LANES
    raw, normed, query, query_send = pl.pallas_call(
        functools.partial(query_kernel, tensors=tensors, heads=query_heads),
        out_shape=[
            shape((rows, model_width), bf16),
            shape((rows, model_width), bf16),
            shape((rows, local_width), bf16),
            shape((slot_rows, send_width), bf16),
        ],
        in_specs=[scalar()]
        + [whole()] * (tensors + 1)
        + [pl.BlockSpec(memory_space=pltpu.HBM)]
        + [whole()] * 4,
        out_specs=[whole()] * 4,
        scratch_shapes=[
            pltpu.VMEM((model_width, local_width), bf16),
            pltpu.SemaphoreType.DMA((local_heads // query_heads,)),
        ],
        compiler_params=params(10),
        cost_estimate=cost(2 * rows * model_width * local_width, 2 * model_width * local_width),
        name="queries",
    )(
        index, in_hbm(raw_pieces[0]), *raw_pieces[1:], in_hbm(attn_gain.reshape(1, -1)), in_hbm(w_query),
        cosine, sine, place, meta,
    )

    query_arrived = exchange(query_send, groups)

    leaf_out, leaf_lse = pl.pallas_call(
        functools.partial(leaf_kernel, heads=step_heads, leaf_len=leaf_len, scale=scale),
        grid=(steps,),
        out_shape=[shape((rows, local_width), f32), shape((rows, LANES), f32)],
        in_specs=[
            fixed(rows, model_width),
            columns(rows, step_width),
            columns(model_width, step_width),
            columns(model_width, step_width),
            fixed(rows, LANES),
            fixed(rows, LANES),
        ],
        out_specs=[columns(rows, step_width), fixed(rows, LANES)],
        compiler_params=params(10, 1),
        cost_estimate=cost(4 * rows * model_width * local_width, 4 * model_width * local_width),
        name="leaf",
    )(normed, query, in_hbm(w_key), in_hbm(w_value), cosine, sine)

    pool = prefix_kv.shape[1]
    back_send = pl.pallas_call(
        functools.partial(
            owner_kernel, heads=local_heads, requests=requests, leaf_len=leaf_len, scale=scale
        ),
        out_shape=shape((slot_rows, send_width), bf16),
        in_specs=[whole()] * 2,
        out_specs=whole(),
        scratch_shapes=[
            pltpu.VMEM((3 * rows, local_width), bf16),
            pltpu.VMEM((3 * rows, send_width), bf16),
        ],
        compiler_params=params(16),
        cost_estimate=cost(4 * slot_rows * pool * local_width, 4 * pool * local_width),
        name="owner",
    )(query_arrived, prefix_kv)

    back = exchange(back_send, groups)

    out_step = min(512, model_width)
    partial_out = pl.pallas_call(
        functools.partial(merge_kernel, heads=local_heads, step=out_step),
        out_shape=shape((rows, model_width), bf16),
        in_specs=[pl.BlockSpec(memory_space=pl.ANY)]
        + [whole()] * 4
        + [pl.BlockSpec(memory_space=pltpu.HBM)],
        out_specs=whole(),
        scratch_shapes=[
            pltpu.VMEM((local_width, model_width), bf16),
            pltpu.VMEM((rows, local_width), bf16),
            pltpu.SemaphoreType.DMA((model_width // out_step,)),
        ],
        compiler_params=params(10),
        cost_estimate=cost(2 * rows * local_width * model_width, 2 * local_width * model_width),
        name="merge",
    )(far_table, back, pick, leaf_out, leaf_lse, in_hbm(w_out))

    out_pieces = ring_get(partial_out, tensors)

    half = (lax.axis_index("dp") // (groups // 2)).astype(jnp.int32).reshape(1)
    send, gate_high, gate_low, final = pl.pallas_call(
        functools.partial(
            routing_kernel, tensors=tensors, leaf_len=leaf_len, groups=groups,
            capacity=capacity, experts=experts, choices=top_count,
        ),
        out_shape=[
            shape((slots, 2 * rows), bf16),
            shape((2 * rows, slots), bf16),
            shape((2 * rows, slots), bf16),
            shape((slot_rows, 2 * rows), bf16),
        ],
        in_specs=[scalar(), pl.BlockSpec(memory_space=pl.ANY)] + [whole()] * 2,
        out_specs=[whole()] * 4,
        compiler_params=params(6),
        cost_estimate=cost(1, 1),
        name="routing",
    )(half, partial_out, table, far_table)

    normed_mlp, own_columns, resid_own = pl.pallas_call(
        functools.partial(middle_kernel, tensors=tensors),
        out_shape=[
            shape((rows, model_width), bf16),
            shape((rows, column_share), bf16),
            shape((rows, column_share), f32),
        ],
        in_specs=[scalar(), pl.BlockSpec(memory_space=pl.ANY)] + [whole()] * (2 + tensors),
        out_specs=[whole()] * 3,
        scratch_shapes=[pltpu.VMEM((rows, model_width), f32)],
        compiler_params=params(4),
        name="middle",
    )(index, send, raw, mlp_gain.reshape(1, -1), *out_pieces)

    far_columns = from_partner(own_columns, groups)
    hbm = pl.BlockSpec(memory_space=pltpu.HBM)
    hidden = shared_out.shape[0]
    expert_hidden = expert_out.shape[1]
    expert_in = in_hbm(jnp.transpose(expert_in, (0, 2, 3, 1)))
    expert_out = in_hbm(expert_out)
    early = max(1, local_experts // 2)
    *shared_pieces, early_in, early_down = pl.pallas_call(
        functools.partial(shared_kernel, tensors=tensors),
        out_shape=[shape((rows, column_share), bf16)] * tensors
        + [
            pltpu.VMEM((early, 2, expert_hidden, model_width), bf16),
            pltpu.VMEM((expert_hidden, model_width), bf16),
        ],
        in_specs=[scalar(), whole()] + [hbm] * 4,
        out_specs=[whole()] * (tensors + 2),
        scratch_shapes=[
            pltpu.VMEM((2, hidden, model_width), bf16),
            pltpu.VMEM((hidden, model_width), bf16),
            pltpu.VMEM((rows, model_width), f32),
            pltpu.SemaphoreType.DMA((5,)),
        ],
        compiler_params=params(11),
        cost_estimate=cost(1, 1),
        name="shared",
    )(
        index, normed_mlp, in_hbm(jnp.transpose(shared_in, (1, 2, 0))), in_hbm(shared_out),
        expert_in, expert_out,
    )

    send_rows = pl.pallas_call(
        dispatch_kernel,
        out_shape=shape((slots, column_share), bf16),
        in_specs=[pl.BlockSpec(memory_space=pl.ANY)] * 2 + [whole()] * 3,
        out_specs=whole(),
        compiler_params=params(3),
        name="dispatch",
    )(shared_pieces[0], early_down, send, own_columns, far_columns)

    arrived = exchange(send_rows, groups, halves=True)

    block = local_experts * capacity
    arrived_pieces = ring_get(arrived.reshape(groups, block, column_share), tensors)
    partial_pieces = pl.pallas_call(
        functools.partial(
            expert_kernel, tensors=tensors, experts=local_experts, capacity=capacity
        ),
        out_shape=[shape((groups, block, column_share), bf16)] * tensors,
        in_specs=[scalar()] + [whole()] * (tensors + 2) + [hbm, hbm],
        out_specs=[whole()] * tensors,
        scratch_shapes=[
            pltpu.VMEM((local_experts - early, 2, expert_hidden, model_width), bf16),
            pltpu.VMEM((local_experts - 1, expert_hidden, model_width), bf16),
            pltpu.VMEM((local_experts, groups * capacity, model_width), bf16),
            pltpu.SemaphoreType.DMA((2, local_experts)),
        ],
        compiler_params=params(28),
        cost_estimate=cost(
            6 * slots * expert_hidden * model_width,
            6 * local_experts * expert_hidden * model_width,
        ),
        name="experts",
    )(
        index,
        *arrived_pieces,
        pltpu.with_memory_space_constraint(early_in, pltpu.VMEM),
        pltpu.with_memory_space_constraint(early_down, pltpu.VMEM),
        expert_in,
        expert_out,
    )
    partial_pieces, shared_pieces = lax.optimization_barrier((partial_pieces, shared_pieces))
    shared_pieces = ring_send(shared_pieces)
    partial_pieces = ring_send(partial_pieces)
    summed = pl.pallas_call(
        add_kernel,
        out_shape=shape((groups, block, column_share), bf16),
        in_specs=[pl.BlockSpec(memory_space=pl.ANY)] + [whole()] * tensors,
        out_specs=whole(),
        compiler_params=params(6),
        name="add",
    )(shared_pieces[-1], *partial_pieces)

    returned = exchange(summed.reshape(slots, column_share), groups, halves=True)

    final_send = pl.pallas_call(
        functools.partial(combine_kernel, tensors=tensors),
        out_shape=shape((slot_rows, column_share), bf16),
        in_specs=[whole()] * (5 + tensors),
        out_specs=whole(),
        compiler_params=params(6),
        name="combine",
    )(returned, gate_high, gate_low, resid_own, final, *shared_pieces)

    devices = groups * tensors
    blocks = final_send.reshape(devices, slot_rows // devices, column_share)
    final_arrived = lax.all_to_all(
        blocks, ("dp", "tensor"), split_axis=0, concat_axis=0, tiled=True
    ).reshape(slot_rows, column_share)

    return pl.pallas_call(
        functools.partial(settle_kernel, tensors=tensors, leaf_len=leaf_len, groups=groups),
        grid=(1,),
        out_shape=shape((requests, leaf_len // tensors, model_width), bf16),
        in_specs=[
            pl.BlockSpec((slot_rows, LANES), lambda i: (0, local_heads)),
            fixed(slot_rows, column_share),
        ],
        out_specs=fixed(requests, leaf_len // tensors, model_width),
        compiler_params=params(4, 1),
        name="settle",
    )(query_arrived, final_arrived)


def solution(mesh):
    in_specs = (
        P(("dp", "tensor"), None, None),
        P(),
        P(None, "tensor"),
        P(None, "tensor"),
        P(None, "tensor"),
        P("tensor", None),
        P(None, "dp", "tensor"),
        P("dp", None),
        P("dp", None),
        P("dp", None),
        P(),
        P(None, None, "tensor"),
        P("tensor", None),
        P("dp", None, None, "tensor"),
        P("dp", "tensor", None),
        P("dp", None, None),
        P("dp", None, None),
        P("dp"),
    )
    out_specs = P("dp", "tensor", None)
    return jax.shard_map(
        on_device, mesh=mesh, in_specs=in_specs, out_specs=out_specs, check_vma=False
    )
```

```python
import functools
import math

import jax
import jax.numpy as jnp
from jax import lax
from jax.experimental import pallas as pl
from jax.experimental.pallas import tpu as pltpu
from jax.sharding import PartitionSpec as P

HEAD_DIM = 128
EPS = 1e-06
ROPE_BASE = 10000.0
LANES = 128
HIDE = -1e30
LOG2E = 1.4426950408889634
LN2 = 0.6931471805599453
LEVEL_KEYS = (512, 256, 128)
MIB = 1 << 20

f32 = jnp.float32
bf16 = jnp.bfloat16


def dot(a, b):
    return lax.dot_general(a, b, (((1,), (0,)), ((), ())), preferred_element_type=f32)


def dot_nt(a, b):
    return lax.dot_general(a, b, (((1,), (1,)), ((), ())), preferred_element_type=f32)


def iota(shape, dim):
    return lax.broadcasted_iota(jnp.int32, shape, dim).astype(f32)


def divided(index, by):
    quotient = jnp.floor((index + 0.5) * (1.0 / by))
    return quotient, index - by * quotient


def one_hot(condition):
    return jnp.where(condition, 1.0, 0.0).astype(bf16)


def rms(values, gain):
    mean_square = jnp.mean(values * values, axis=-1, keepdims=True)
    return (values * lax.rsqrt(mean_square + EPS) * gain).astype(bf16)


def ring_get(piece, count):
    pieces = [piece]
    for step in range(1, count):
        pieces.append(
            lax.ppermute(piece, "tensor", [((i + step) % count, i) for i in range(count)])
        )
    return pieces


def ring_send(pieces):
    count = len(pieces)
    arrived = [pieces[0]]
    for step in range(1, count):
        arrived.append(
            lax.ppermute(pieces[step], "tensor", [(i, (i + step) % count) for i in range(count)])
        )
    return arrived


def exchange(rows, groups, halves=False):
    size = groups // 2 if halves else groups
    blocks = rows.reshape(size, rows.shape[0] // size, rows.shape[1])
    parts = [list(range(size)), list(range(size, groups))] if halves else None
    return lax.all_to_all(
        blocks, "dp", split_axis=0, concat_axis=0, tiled=True, axis_index_groups=parts
    ).reshape(rows.shape)


def from_partner(array, groups):
    return lax.ppermute(array, "dp", [(i, (i + groups // 2) % groups) for i in range(groups)])


def in_hbm(array):
    return pltpu.with_memory_space_constraint(array, pltpu.HBM)


def whole():
    return pl.BlockSpec(memory_space=pltpu.VMEM)


def scalar():
    return pl.BlockSpec(memory_space=pltpu.SMEM)


def params(mib, grid=0):
    return pltpu.CompilerParams(
        vmem_limit_bytes=mib * MIB,
        dimension_semantics=("arbitrary",) * grid if grid else None,
    )


def cost(flops, nbytes):
    return pl.CostEstimate(flops=int(flops), bytes_accessed=int(nbytes), transcendentals=0)


def upright(row):
    size = row.shape[1]
    diagonal = iota((size, size), 0) == iota((size, size), 1)
    return jnp.sum(jnp.where(diagonal, row, 0.0), axis=1, keepdims=True)


def in_rows(values, leaf_len):
    choices, requests, _ = values.shape
    rows = requests * leaf_len
    request_of_row, token_of_row = divided(iota((1, rows), 1), leaf_len)
    flat = values.astype(f32).reshape(choices * requests, leaf_len).astype(bf16)
    spread = dot(flat, one_hot(iota((leaf_len, 1), 0) == token_of_row))
    _, request = divided(iota((choices * requests, 1), 0), requests)
    kept = jnp.where(request == request_of_row, spread, 0.0)
    return jnp.sum(kept.reshape(choices, requests, rows), axis=1)


def across_rows(column):
    size = column.shape[0]
    diagonal = iota((size, size), 0) == iota((size, size), 1)
    return jnp.sum(jnp.where(diagonal, column, 0.0), axis=0, keepdims=True)


def owner_slots(owner):
    rows = []
    for level in range(3):
        mine, repeated = owner[level : level + 1], 0.0
        for earlier in range(level):
            same = upright(owner[earlier : earlier + 1]) == mine
            repeated = repeated + jnp.max(jnp.where(same, 1.0, 0.0), axis=0, keepdims=True)
        rows.append(mine * 2.0 + repeated)
    return rows


def prelude_kernel(
    owner_ref, start_ref, length_ref, request_ref, ids_ref, gates_ref,
    place_ref, meta_ref, cos_ref, sin_ref, table_ref, pick_ref,
    *, leaf_len,
):
    requests = owner_ref.shape[1]
    slot_rows, rows = place_ref.shape
    start, length = start_ref[...].astype(f32), length_ref[...].astype(f32)
    row_slot, row_token = divided(iota((slot_rows, 1), 0), leaf_len)
    request_of_row, token_of_row = divided(iota((1, rows), 1), leaf_len)
    row_request, row_place = divided(iota((rows, 1), 0), leaf_len)
    mine = iota((1, requests), 1) == row_request
    slot_across, token_across = divided(iota((1, slot_rows), 1), leaf_len)
    named, first_key, key_count = 0.0, 0.0, 0.0
    for level, slot in enumerate(owner_slots(owner_ref[...].astype(f32))):
        slot_down = jnp.sum(jnp.where(mine, slot, 0.0), axis=1, keepdims=True)
        pick_ref[level] = one_hot((slot_down == slot_across) & (row_place == token_across))
        here = jnp.where(slot == row_slot, 1.0, 0.0)
        named = named + here
        first_key = first_key + here * start[level : level + 1]
        key_count = key_count + here * length[level : level + 1]
    placed = dot(named.astype(bf16), one_hot(iota((requests, 1), 0) == request_of_row))
    place_ref[...] = jnp.where(row_token == token_of_row, placed, 0.0).astype(bf16)

    first_key = jnp.sum(first_key, axis=1, keepdims=True)
    key_count = jnp.sum(key_count, axis=1, keepdims=True)
    dest, place = divided(request_ref[...].astype(f32), requests)
    row_group, _ = divided(row_slot, 2)
    tag = jnp.sum(jnp.where(dest == row_group, place + 1.0, 0.0), axis=1, keepdims=True)
    lane = iota((1, LANES), 1)
    meta = jnp.zeros((slot_rows, LANES), f32)
    for at, value in enumerate(divided(first_key, 32) + divided(key_count, 32) + (tag,)):
        meta = jnp.where(lane == at, value, meta)
    meta_ref[...] = meta.astype(bf16)

    offsets = length[0:1] + length[1:2] + length[2:3]
    position = jnp.sum(jnp.where(mine, offsets, 0.0), axis=1, keepdims=True) + row_place
    half = HEAD_DIM // 2
    pair = jnp.where(lane < half, lane, lane - half)
    angle = position * jnp.exp(pair * (-2.0 * math.log(ROPE_BASE) / HEAD_DIM))
    cos_ref[...] = jnp.cos(angle)
    sin_ref[...] = jnp.sin(angle) * jnp.where(lane < half, -1.0, 1.0)

    gates = gates_ref[...]
    gates_high = gates.astype(bf16).astype(f32)
    choices = gates.shape[0]
    for at, values in enumerate((ids_ref[...], gates_high, gates - gates_high)):
        table_ref[at * choices : (at + 1) * choices, :] = in_rows(values, leaf_len)
    dest_down = jnp.sum(jnp.where(mine, dest, 0.0), axis=1, keepdims=True)
    last = 3 * choices
    size = table_ref.shape[0] - last
    table_ref[last:, :] = jnp.broadcast_to(across_rows(dest_down), (size, rows))


def routing_kernel(
    half_ref, after_ref, table_ref, far_table_ref,
    send_ref, high_ref, low_ref, final_ref,
    *, tensors, leaf_len, groups, capacity, experts, choices,
):
    rows = table_ref.shape[1]
    final_rows = final_ref.shape[0]
    share = leaf_len // tensors
    _, token_of_row = divided(iota((1, rows), 1), leaf_len)

    slots = send_ref.shape[0]
    local = experts // groups
    block, slot_place = divided(iota((slots, 1), 0), capacity)
    block, local_expert = divided(block, local)
    device, slot_source = divided(block, 2)
    first_expert = (half_ref[0] * (experts // 2)).astype(f32)
    spread = one_hot(first_expert + device * local + local_expert == iota((1, experts), 1))
    expert_down = iota((experts, 1), 0)
    ahead = one_hot(iota((rows, rows), 0) < iota((rows, rows), 1))
    block, final_place = divided(iota((final_rows, 1), 0), share)
    block, final_source = divided(block, 2)
    final_group, final_half = divided(block, tensors)
    final_token = final_half * share + final_place
    send, high, low, final = [], [], [], []
    for source, table in enumerate((table_ref[...], far_table_ref[...])):
        member, gate_high, gate_low = 0.0, 0.0, 0.0
        for choice in range(choices):
            hit = jnp.where(table[choice : choice + 1] == expert_down, 1.0, 0.0)
            member = member + hit
            gate_high = gate_high + hit * table[choices + choice : choices + choice + 1]
            gate_low = gate_low + hit * table[2 * choices + choice : 2 * choices + choice + 1]
        member = member.astype(bf16)
        before = dot(member, ahead).astype(bf16)
        taken = (dot(spread, member) > 0.5) & (dot(spread, before) == slot_place)
        taken = taken & (slot_source == source)
        send.append(jnp.where(taken, 1.0, 0.0))
        high.append(jnp.where(taken, dot(spread, gate_high.astype(bf16)), 0.0))
        low.append(jnp.where(taken, dot(spread, gate_low.astype(bf16)), 0.0))
        going = (table[3 * choices : 3 * choices + 1] == final_group) & (final_source == source)
        final.append(jnp.where(going & (final_token == token_of_row), 1.0, 0.0))
    send_ref[...] = jnp.concatenate(send, axis=1).astype(bf16)
    high_ref[...] = jnp.transpose(jnp.concatenate(high, axis=1)).astype(bf16)
    low_ref[...] = jnp.transpose(jnp.concatenate(low, axis=1)).astype(bf16)
    final_ref[...] = jnp.concatenate(final, axis=1).astype(bf16)


def rotated(product, cosine, sine, heads):
    columns = []
    for head in range(heads):
        part = product[:, head * HEAD_DIM : (head + 1) * HEAD_DIM]
        columns.append(part * cosine + pltpu.roll(part, HEAD_DIM // 2, 1) * sine)
    return jnp.concatenate(columns, axis=1).astype(bf16)


def query_kernel(*refs, tensors, heads):
    index_ref, pieces, refs = refs[0], refs[1 : 1 + tensors], refs[1 + tensors :]
    (gain_ref, weight_ref, cos_ref, sin_ref, place_ref, meta_ref,
     raw_ref, normed_ref, query_ref, send_ref, buffer_ref, semaphores) = refs
    width = heads * HEAD_DIM
    copies = column_copies(weight_ref, buffer_ref, semaphores, width)
    shard = pieces[0].shape[0]
    for at, piece in enumerate(pieces):
        owner = lax.rem(index_ref[0] + at, tensors)
        raw_ref[pl.ds(pl.multiple_of(owner * shard, shard), shard), :] = piece[...]
    normed_ref[...] = rms(raw_ref[...].astype(f32), gain_ref[...])
    send_ref[:, send_ref.shape[1] - LANES :] = meta_ref[...]
    for at, copy in enumerate(copies):
        copy.wait()
        columns = slice(at * width, (at + 1) * width)
        product = dot(normed_ref[...], buffer_ref[:, columns])
        query = rotated(product, cos_ref[...], sin_ref[...], heads)
        query_ref[:, columns] = query
        send_ref[:, columns] = dot(place_ref[...], query).astype(bf16)


def leaf_kernel(
    normed_ref, query_ref, key_ref, value_ref, cos_ref, sin_ref, out_ref, lse_ref,
    *, heads, leaf_len, scale,
):
    step = pl.program_id(0)
    normed = normed_ref[...]
    rows = normed.shape[0]
    keys = rotated(dot(normed, key_ref[...]), cos_ref[...], sin_ref[...], heads)
    values = dot(normed, value_ref[...]).astype(bf16)
    down, across = iota((rows, 1), 0), iota((1, rows), 1)
    visible = (divided(down, leaf_len)[0] == divided(across, leaf_len)[0]) & (across <= down)
    lane = lax.broadcasted_iota(jnp.int32, (1, LANES), 1)

    @pl.when(step == 0)
    def _():
        lse_ref[...] = jnp.zeros_like(lse_ref)

    for head in range(heads):
        at = slice(head * HEAD_DIM, (head + 1) * HEAD_DIM)
        scores = jnp.where(visible, dot_nt(query_ref[:, at], keys[:, at]) * scale, HIDE)
        highest = jnp.max(scores, axis=1, keepdims=True)
        weights = jnp.exp(scores - highest)
        total = jnp.sum(weights, axis=1, keepdims=True)
        out_ref[:, at] = dot(weights.astype(bf16), values[:, at]) / total
        lse = highest + jnp.log(total)
        lse_ref[...] = jnp.where(lane == step * heads + head, lse, lse_ref[...])


def owner_kernel(
    arrived_ref, kv_ref, back_ref, query_ref, out_ref,
    *, heads, requests, leaf_len, scale,
):
    slot_rows = arrived_ref.shape[0]
    width = heads * HEAD_DIM
    count = requests * leaf_len
    packed = arrived_ref[:, width:]
    meta = packed.astype(f32)
    first = meta[:, 0:1] * 32.0 + meta[:, 1:2]
    used = meta[:, 2:3] + meta[:, 3:4] > 0.0
    begins = [sum(LEVEL_KEYS[:level]) for level in range(3)]
    level = jnp.where(first >= begins[1], 1.0, 0.0) + jnp.where(first >= begins[2], 1.0, 0.0)
    level = jnp.where(used, level, 3.0)
    lane = lax.broadcasted_iota(jnp.int32, (1, LANES), 1)
    of_level = level == lane.astype(f32)
    ahead = one_hot(iota((slot_rows, slot_rows), 1) < iota((slot_rows, slot_rows), 0))
    rank = dot(ahead, one_hot(of_level))
    rank = jnp.sum(jnp.where(of_level, rank, 0.0), axis=1, keepdims=True)
    target = jnp.where(used, level * count + rank, -1.0)
    spread = jnp.where(target == iota((1, 3 * count), 1), 1.0, 0.0)
    ordered = jnp.transpose(spread).astype(bf16)
    query_ref[...] = dot(ordered, arrived_ref[:, :width]).astype(bf16)
    meta = dot(ordered, packed)
    first = meta[:, 0:1] * 32.0 + meta[:, 1:2]
    last = first + meta[:, 2:3] * 32.0 + meta[:, 3:4]
    for level in range(3):
        size = LEVEL_KEYS[level]
        part = slice(level * count, (level + 1) * count)
        keys = slice(begins[level], begins[level] + size)
        key = iota((1, size), 1) + float(begins[level])
        bias = jnp.where((key >= first[part]) & (key < last[part]), 0.0, HIDE)
        ones = jnp.ones((size, HEAD_DIM), bf16)
        sums = jnp.zeros((count, LANES), f32)
        for head in range(heads):
            at = slice(head * HEAD_DIM, (head + 1) * HEAD_DIM)
            scores = dot_nt(query_ref[part, at], kv_ref[0, keys, at]) * (scale * LOG2E) + bias
            highest = jnp.max(scores, axis=1, keepdims=True)
            weights = jnp.exp2(scores - highest).astype(bf16)
            both = dot(weights, jnp.concatenate([kv_ref[1, keys, at], ones], axis=1))
            total = both[:, HEAD_DIM:]
            out_ref[part, at] = (both[:, :HEAD_DIM] / total).astype(bf16)
            lse = highest * LN2 + jnp.log(total)
            lse_high = lse.astype(bf16).astype(f32)
            sums = jnp.where(lane == head, lse_high, sums)
            sums = jnp.where(lane == head + heads, lse - lse_high, sums)
        out_ref[part, width:] = sums.astype(bf16)
    back_ref[...] = dot(spread.astype(bf16), out_ref[...]).astype(bf16)


def column_copies(source_ref, target_ref, semaphores, step):
    copies = []
    for at in range(source_ref.shape[1] // step):
        columns = pl.ds(at * step, step)
        copy = pltpu.make_async_copy(
            source_ref.at[:, columns], target_ref.at[:, columns], semaphores.at[at]
        )
        copy.start()
        copies.append(copy)
    return copies


def merge_kernel(
    after_ref, back_ref, pick_ref, leaf_ref, lse_ref, weight_ref, out_ref, buffer_ref, attended_ref, semaphores,
    *, heads, step,
):
    copies = column_copies(weight_ref, buffer_ref, semaphores, step)
    width = heads * HEAD_DIM
    back = back_ref[...]
    outputs, sums = [leaf_ref[...]], [lse_ref[...]]
    for level in range(3):
        rows = dot(pick_ref[level], back)
        outputs.append(rows[:, :width])
        tail = rows[:, width:]
        sums.append(tail + pltpu.roll(tail, LANES - heads, 1))
    highest = functools.reduce(jnp.maximum, sums)
    scales = [jnp.exp(one - highest) for one in sums]
    total = sum(scales[1:], scales[0])
    scales = [one / total for one in scales]
    for head in range(heads):
        at = slice(head * HEAD_DIM, (head + 1) * HEAD_DIM)
        mixed = sum(scales[i][:, head : head + 1] * outputs[i][:, at] for i in range(4))
        attended_ref[:, at] = mixed.astype(bf16)
    for at, copy in enumerate(copies):
        copy.wait()
        columns = slice(at * step, (at + 1) * step)
        out_ref[:, columns] = dot(attended_ref[...], buffer_ref[:, columns]).astype(bf16)


def middle_kernel(*refs, tensors):
    index_ref, _, raw_ref, gain_ref = refs[:4]
    pieces = refs[4 : 4 + tensors]
    normed_ref, own_ref, resid_own_ref, resid_ref = refs[4 + tensors :]
    width = own_ref.shape[1]
    own = pl.ds(pl.multiple_of(index_ref[0] * width, width), width)
    total = raw_ref[...].astype(f32)
    for piece in pieces:
        total = total + piece[...].astype(f32)
    resid_ref[...] = total
    resid_own_ref[...] = resid_ref[:, own]
    normed_ref[...] = rms(total, gain_ref[...])
    own_ref[...] = normed_ref[:, own]


def dispatch_kernel(after_ref, also_after_ref, send_ref, own_ref, far_ref, out_ref):
    both = jnp.concatenate([own_ref[...], far_ref[...]], axis=0)
    out_ref[...] = dot(send_ref[...], both).astype(bf16)


def shared_kernel(*refs, tensors):
    index_ref, rows_ref, in_hbm_ref, down_hbm_ref, expert_in_ref, expert_down_ref = refs[:6]
    pieces, refs = refs[6 : 6 + tensors], refs[6 + tensors :]
    early_in_ref, early_down_ref, in_ref, down_ref, total_ref, semaphores = refs
    early = early_in_ref.shape[0]
    copies = [
        pltpu.make_async_copy(in_hbm_ref.at[0], in_ref.at[0], semaphores.at[0]),
        pltpu.make_async_copy(in_hbm_ref.at[1], in_ref.at[1], semaphores.at[1]),
        pltpu.make_async_copy(down_hbm_ref, down_ref, semaphores.at[2]),
        pltpu.make_async_copy(expert_in_ref.at[0:early], early_in_ref, semaphores.at[3]),
        pltpu.make_async_copy(expert_down_ref.at[0], early_down_ref, semaphores.at[4]),
    ]
    for copy in copies:
        copy.start()
    rows = rows_ref[...]
    copies[0].wait()
    gate = dot_nt(rows, in_ref[0])
    copies[1].wait()
    up = dot_nt(rows, in_ref[1])
    hidden = (gate / (1.0 + jnp.exp(-gate)) * up).astype(bf16)
    copies[2].wait()
    total_ref[...] = dot(hidden, down_ref[...])
    width = pieces[0].shape[1]
    for at, piece in enumerate(pieces):
        column = lax.rem(index_ref[0] + at, tensors) * width
        piece[...] = total_ref[:, pl.ds(pl.multiple_of(column, width), width)].astype(bf16)
    copies[3].wait()
    copies[4].wait()


def rows_of_experts(piece, experts, capacity):
    groups, _, width = piece.shape
    values = piece[...].astype(f32)
    for e in range(experts):
        mine = values[:, e * capacity : (e + 1) * capacity, :].reshape(groups * capacity, width)
        yield mine.astype(bf16)


def own_half_kernel(index_ref, piece, early_in_ref, out_ref, *, experts, capacity):
    width = piece.shape[2]
    columns = pl.ds(pl.multiple_of(index_ref[0] * width, width), width)
    rows = list(rows_of_experts(piece, experts, capacity))
    for e in range(early_in_ref.shape[0]):
        for part in range(2):
            out_ref[e, part] = dot_nt(rows[e], early_in_ref[e, part, :, columns])


def expert_kernel(*refs, tensors, experts, capacity):
    index_ref, arrived, refs = refs[0], refs[1 : 1 + tensors], refs[1 + tensors :]
    (half_ref, early_in_ref, early_down_ref, in_hbm_ref, down_hbm_ref), refs = refs[:5], refs[5:]
    pieces, refs = refs[:tensors], refs[tensors:]
    in_ref, down_ref, rows_ref, semaphores = refs
    early = early_in_ref.shape[0]
    in_copies, down_copies = {}, {}
    for e in range(1, experts):
        down_copies[e] = pltpu.make_async_copy(
            down_hbm_ref.at[e], down_ref.at[e - 1], semaphores.at[0, e]
        )
        if e >= early:
            in_copies[e] = pltpu.make_async_copy(
                in_hbm_ref.at[e], in_ref.at[e - early], semaphores.at[1, e]
            )
            in_copies[e].start()
        down_copies[e].start()
    groups, _, width = arrived[0].shape
    columns = [
        pl.ds(pl.multiple_of(lax.rem(index_ref[0] + at, tensors) * width, width), width)
        for at in range(tensors)
    ]
    for at, piece in enumerate(arrived):
        for e, rows in enumerate(rows_of_experts(piece, experts, capacity)):
            rows_ref[e, :, columns[at]] = rows
    together = max(1, 16 // capacity)
    values = []
    for e in range(experts):
        if e < early:
            weights = early_in_ref.at[e]
        else:
            weights = in_ref.at[e - early]
            in_copies[e].wait()
        down = early_down_ref if e == 0 else down_ref.at[e - 1]
        if e < early:
            gate, up = half_ref[e, 0], half_ref[e, 1]
            for at in range(1, tensors):
                other = rows_ref[e, :, columns[at]]
                gate = gate + dot_nt(other, weights[0, :, columns[at]])
                up = up + dot_nt(other, weights[1, :, columns[at]])
        else:
            gate = dot_nt(rows_ref[e], weights[0])
            up = dot_nt(rows_ref[e], weights[1])
        hidden = (gate / (1.0 + jnp.exp(-gate)) * up).astype(bf16)
        if e > 0:
            down_copies[e].wait()
        values.append(
            [
                dot(hidden, down[:, columns[at]]).reshape(groups, capacity, width)
                for at in range(tensors)
            ]
        )
        if len(values) == together or e == experts - 1:
            mine = slice((e + 1 - len(values)) * capacity, (e + 1) * capacity)
            for at, piece in enumerate(pieces):
                parts = [value[at] for value in values]
                piece[:, mine, :] = jnp.concatenate(parts, axis=1).astype(bf16)
            values = []


def add_kernel(after_ref, *refs):
    out_ref = refs[-1]
    out_ref[...] = sum(piece[...].astype(f32) for piece in refs[:-1]).astype(bf16)


def combine_kernel(*refs, tensors):
    returned_ref, high_ref, low_ref, resid_ref, final_ref = refs[:5]
    shared, out_ref = refs[5 : 5 + tensors], refs[5 + tensors]
    returned = returned_ref[...]
    routed = dot(high_ref[...], returned) + dot(low_ref[...], returned)
    rows = resid_ref.shape[0]
    total = resid_ref[...]
    for piece in shared:
        total = total + piece[...].astype(f32)
    both = jnp.concatenate([total + routed[:rows], routed[rows:]], axis=0).astype(bf16)
    out_ref[...] = dot(final_ref[...], both).astype(bf16)


def settle_kernel(meta_ref, rows_ref, out_ref, *, tensors, leaf_len, groups):
    slot_rows, final_rows = meta_ref.shape[0], rows_ref.shape[0]
    requests, share, _ = out_ref.shape
    width = rows_ref.shape[1]
    tag_down = meta_ref[...].astype(f32)[:, 4:5]
    block, place = divided(iota((1, final_rows), 1), share)
    block, source = divided(block, 2)
    group, half = divided(block, tensors)
    _, home = divided(group + source * (groups // 2), groups)
    tagged = iota((slot_rows, 1), 0) == home * (2.0 * leaf_len)
    tag = jnp.sum(jnp.where(tagged, tag_down, 0.0), axis=0, keepdims=True)
    request, position = divided(iota((requests * share, 1), 0), share)
    wanted = (tag == request + 1.0) & (place == position)
    for at in range(tensors):
        value = dot(one_hot(wanted & (half == at)), rows_ref[...])
        for r in range(requests):
            out_ref[r, :, at * width : (at + 1) * width] = value[
                r * share : (r + 1) * share
            ].astype(bf16)


def on_device(
    leaf_tokens,
    attn_gain,
    w_query,
    w_key,
    w_value,
    w_out,
    prefix_kv,
    prefix_owner,
    prefix_start,
    prefix_len,
    mlp_gain,
    shared_in,
    shared_out,
    expert_in,
    expert_out,
    expert_ids,
    gate_weights,
    request_of,
):
    groups = lax.axis_size("dp")
    tensors = lax.axis_size("tensor")
    index = lax.axis_index("tensor").astype(jnp.int32).reshape(1)
    shard_requests, leaf_len, model_width = leaf_tokens.shape
    requests = prefix_owner.shape[0]
    rows = requests * leaf_len
    local_width = w_query.shape[1]
    local_heads = local_width // HEAD_DIM
    scale = HEAD_DIM ** (-0.5)
    column_share = model_width // tensors
    top_count = expert_ids.shape[2]
    local_experts = expert_in.shape[0]
    experts = local_experts * groups
    assignments = rows * top_count
    capacity = tensors * max(1, assignments * 4 // (experts * 3 * tensors))
    slots = experts * capacity
    slot_rows = groups * 2 * leaf_len
    shape = jax.ShapeDtypeStruct

    raw_pieces = ring_get(leaf_tokens.reshape(shard_requests * leaf_len, model_width), tensors)

    owner_rows, request_row = prefix_owner.T, request_of.reshape(1, requests)
    table_rows = -(-(3 * top_count + 1) // 8) * 8
    place, meta, cosine, sine, table, pick = pl.pallas_call(
        functools.partial(prelude_kernel, leaf_len=leaf_len),
        out_shape=[
            shape((slot_rows, rows), bf16),
            shape((slot_rows, LANES), bf16),
            shape((rows, LANES), f32),
            shape((rows, LANES), f32),
            shape((table_rows, rows), f32),
            shape((3, rows, slot_rows), bf16),
        ],
        in_specs=[whole()] * 6,
        out_specs=[whole()] * 6,
        compiler_params=params(4),
        name="prelude",
    )(
        in_hbm(owner_rows), in_hbm(prefix_start.T), in_hbm(prefix_len.T), in_hbm(request_row),
        in_hbm(jnp.transpose(expert_ids, (2, 0, 1))),
        in_hbm(jnp.transpose(gate_weights, (2, 0, 1))),
    )
    far_table = from_partner(table, groups)

    step_heads = min(2, local_heads)
    step_width = step_heads * HEAD_DIM
    steps = local_heads // step_heads
    query_heads = min(4, local_heads)
    fixed = lambda *dims: pl.BlockSpec(dims, lambda i: (0,) * len(dims))
    columns = lambda *dims: pl.BlockSpec(dims, lambda i: (0,) * (len(dims) - 1) + (i,))
    send_width = local_width + LANES
    raw, normed, query, query_send = pl.pallas_call(
        functools.partial(query_kernel, tensors=tensors, heads=query_heads),
        out_shape=[
            shape((rows, model_width), bf16),
            shape((rows, model_width), bf16),
            shape((rows, local_width), bf16),
            shape((slot_rows, send_width), bf16),
        ],
        in_specs=[scalar()]
        + [whole()] * (tensors + 1)
        + [pl.BlockSpec(memory_space=pltpu.HBM)]
        + [whole()] * 4,
        out_specs=[whole()] * 4,
        scratch_shapes=[
            pltpu.VMEM((model_width, local_width), bf16),
            pltpu.SemaphoreType.DMA((local_heads // query_heads,)),
        ],
        compiler_params=params(10),
        cost_estimate=cost(2 * rows * model_width * local_width, 2 * model_width * local_width),
        name="queries",
    )(
        index, in_hbm(raw_pieces[0]), *raw_pieces[1:], in_hbm(attn_gain.reshape(1, -1)), in_hbm(w_query),
        cosine, sine, place, meta,
    )

    query_arrived = exchange(query_send, groups)

    leaf_out, leaf_lse = pl.pallas_call(
        functools.partial(leaf_kernel, heads=step_heads, leaf_len=leaf_len, scale=scale),
        grid=(steps,),
        out_shape=[shape((rows, local_width), f32), shape((rows, LANES), f32)],
        in_specs=[
            fixed(rows, model_width),
            columns(rows, step_width),
            columns(model_width, step_width),
            columns(model_width, step_width),
            fixed(rows, LANES),
            fixed(rows, LANES),
        ],
        out_specs=[columns(rows, step_width), fixed(rows, LANES)],
        compiler_params=params(10, 1),
        cost_estimate=cost(4 * rows * model_width * local_width, 4 * model_width * local_width),
        name="leaf",
    )(normed, query, in_hbm(w_key), in_hbm(w_value), cosine, sine)

    pool = prefix_kv.shape[1]
    back_send = pl.pallas_call(
        functools.partial(
            owner_kernel, heads=local_heads, requests=requests, leaf_len=leaf_len, scale=scale
        ),
        out_shape=shape((slot_rows, send_width), bf16),
        in_specs=[whole()] * 2,
        out_specs=whole(),
        scratch_shapes=[
            pltpu.VMEM((3 * rows, local_width), bf16),
            pltpu.VMEM((3 * rows, send_width), bf16),
        ],
        compiler_params=params(16),
        cost_estimate=cost(4 * slot_rows * pool * local_width, 4 * pool * local_width),
        name="owner",
    )(query_arrived, prefix_kv)

    back = exchange(back_send, groups)

    out_step = min(512, model_width)
    partial_out = pl.pallas_call(
        functools.partial(merge_kernel, heads=local_heads, step=out_step),
        out_shape=shape((rows, model_width), bf16),
        in_specs=[pl.BlockSpec(memory_space=pl.ANY)]
        + [whole()] * 4
        + [pl.BlockSpec(memory_space=pltpu.HBM)],
        out_specs=whole(),
        scratch_shapes=[
            pltpu.VMEM((local_width, model_width), bf16),
            pltpu.VMEM((rows, local_width), bf16),
            pltpu.SemaphoreType.DMA((model_width // out_step,)),
        ],
        compiler_params=params(10),
        cost_estimate=cost(2 * rows * local_width * model_width, 2 * local_width * model_width),
        name="merge",
    )(far_table, back, pick, leaf_out, leaf_lse, in_hbm(w_out))

    out_pieces = ring_get(partial_out, tensors)

    half = (lax.axis_index("dp") // (groups // 2)).astype(jnp.int32).reshape(1)
    send, gate_high, gate_low, final = pl.pallas_call(
        functools.partial(
            routing_kernel, tensors=tensors, leaf_len=leaf_len, groups=groups,
            capacity=capacity, experts=experts, choices=top_count,
        ),
        out_shape=[
            shape((slots, 2 * rows), bf16),
            shape((2 * rows, slots), bf16),
            shape((2 * rows, slots), bf16),
            shape((slot_rows, 2 * rows), bf16),
        ],
        in_specs=[scalar(), pl.BlockSpec(memory_space=pl.ANY)] + [whole()] * 2,
        out_specs=[whole()] * 4,
        compiler_params=params(6),
        cost_estimate=cost(1, 1),
        name="routing",
    )(half, partial_out, table, far_table)

    normed_mlp, own_columns, resid_own = pl.pallas_call(
        functools.partial(middle_kernel, tensors=tensors),
        out_shape=[
            shape((rows, model_width), bf16),
            shape((rows, column_share), bf16),
            shape((rows, column_share), f32),
        ],
        in_specs=[scalar(), pl.BlockSpec(memory_space=pl.ANY)] + [whole()] * (2 + tensors),
        out_specs=[whole()] * 3,
        scratch_shapes=[pltpu.VMEM((rows, model_width), f32)],
        compiler_params=params(4),
        name="middle",
    )(index, send, raw, mlp_gain.reshape(1, -1), *out_pieces)

    far_columns = from_partner(own_columns, groups)
    hbm = pl.BlockSpec(memory_space=pltpu.HBM)
    hidden = shared_out.shape[0]
    expert_hidden = expert_out.shape[1]
    expert_in = in_hbm(jnp.transpose(expert_in, (0, 2, 3, 1)))
    expert_out = in_hbm(expert_out)
    early = max(1, local_experts // 2)
    *shared_pieces, early_in, early_down = pl.pallas_call(
        functools.partial(shared_kernel, tensors=tensors),
        out_shape=[shape((rows, column_share), bf16)] * tensors
        + [
            pltpu.VMEM((early, 2, expert_hidden, model_width), bf16),
            pltpu.VMEM((expert_hidden, model_width), bf16),
        ],
        in_specs=[scalar(), whole()] + [hbm] * 4,
        out_specs=[whole()] * (tensors + 2),
        scratch_shapes=[
            pltpu.VMEM((2, hidden, model_width), bf16),
            pltpu.VMEM((hidden, model_width), bf16),
            pltpu.VMEM((rows, model_width), f32),
            pltpu.SemaphoreType.DMA((5,)),
        ],
        compiler_params=params(11),
        cost_estimate=cost(1, 1),
        name="shared",
    )(
        index, normed_mlp, in_hbm(jnp.transpose(shared_in, (1, 2, 0))), in_hbm(shared_out),
        expert_in, expert_out,
    )

    send_rows = pl.pallas_call(
        dispatch_kernel,
        out_shape=shape((slots, column_share), bf16),
        in_specs=[pl.BlockSpec(memory_space=pl.ANY)] * 2 + [whole()] * 3,
        out_specs=whole(),
        compiler_params=params(3),
        name="dispatch",
    )(shared_pieces[0], early_down, send, own_columns, far_columns)

    arrived = exchange(send_rows, groups, halves=True)

    block = local_experts * capacity
    arrived_pieces = ring_get(arrived.reshape(groups, block, column_share), tensors)
    early_in = pltpu.with_memory_space_constraint(early_in, pltpu.VMEM)
    own_half = pl.pallas_call(
        functools.partial(own_half_kernel, experts=local_experts, capacity=capacity),
        out_shape=shape((early, 2, groups * capacity, expert_hidden), f32),
        in_specs=[scalar()] + [whole()] * 2,
        out_specs=whole(),
        compiler_params=params(8),
        cost_estimate=cost(1, 1),
        name="own_half",
    )(index, arrived_pieces[0], early_in)
    partial_pieces = pl.pallas_call(
        functools.partial(
            expert_kernel, tensors=tensors, experts=local_experts, capacity=capacity
        ),
        out_shape=[shape((groups, block, column_share), bf16)] * tensors,
        in_specs=[scalar()] + [whole()] * (tensors + 3) + [hbm, hbm],
        out_specs=[whole()] * tensors,
        scratch_shapes=[
            pltpu.VMEM((local_experts - early, 2, expert_hidden, model_width), bf16),
            pltpu.VMEM((local_experts - 1, expert_hidden, model_width), bf16),
            pltpu.VMEM((local_experts, groups * capacity, model_width), bf16),
            pltpu.SemaphoreType.DMA((2, local_experts)),
        ],
        compiler_params=params(28),
        cost_estimate=cost(
            6 * slots * expert_hidden * model_width,
            6 * local_experts * expert_hidden * model_width,
        ),
        name="experts",
    )(
        index,
        *arrived_pieces,
        own_half,
        early_in,
        pltpu.with_memory_space_constraint(early_down, pltpu.VMEM),
        expert_in,
        expert_out,
    )
    partial_pieces, shared_pieces = lax.optimization_barrier((partial_pieces, shared_pieces))
    shared_pieces = ring_send(shared_pieces)
    partial_pieces = ring_send(partial_pieces)
    summed = pl.pallas_call(
        add_kernel,
        out_shape=shape((groups, block, column_share), bf16),
        in_specs=[pl.BlockSpec(memory_space=pl.ANY)] + [whole()] * tensors,
        out_specs=whole(),
        compiler_params=params(6),
        name="add",
    )(shared_pieces[-1], *partial_pieces)

    returned = exchange(summed.reshape(slots, column_share), groups, halves=True)

    final_send = pl.pallas_call(
        functools.partial(combine_kernel, tensors=tensors),
        out_shape=shape((slot_rows, column_share), bf16),
        in_specs=[whole()] * (5 + tensors),
        out_specs=whole(),
        compiler_params=params(6),
        name="combine",
    )(returned, gate_high, gate_low, resid_own, final, *shared_pieces)

    devices = groups * tensors
    blocks = final_send.reshape(devices, slot_rows // devices, column_share)
    final_arrived = lax.all_to_all(
        blocks, ("dp", "tensor"), split_axis=0, concat_axis=0, tiled=True
    ).reshape(slot_rows, column_share)

    return pl.pallas_call(
        functools.partial(settle_kernel, tensors=tensors, leaf_len=leaf_len, groups=groups),
        grid=(1,),
        out_shape=shape((requests, leaf_len // tensors, model_width), bf16),
        in_specs=[
            pl.BlockSpec((slot_rows, LANES), lambda i: (0, local_heads)),
            fixed(slot_rows, column_share),
        ],
        out_specs=fixed(requests, leaf_len // tensors, model_width),
        compiler_params=params(4, 1),
        name="settle",
    )(query_arrived, final_arrived)


def solution(mesh):
    in_specs = (
        P(("dp", "tensor"), None, None),
        P(),
        P(None, "tensor"),
        P(None, "tensor"),
        P(None, "tensor"),
        P("tensor", None),
        P(None, "dp", "tensor"),
        P("dp", None),
        P("dp", None),
        P("dp", None),
        P(),
        P(None, None, "tensor"),
        P("tensor", None),
        P("dp", None, None, "tensor"),
        P("dp", "tensor", None),
        P("dp", None, None),
        P("dp", None, None),
        P("dp"),
    )
    out_specs = P("dp", "tensor", None)
    return jax.shard_map(
        on_device, mesh=mesh, in_specs=in_specs, out_specs=out_specs, check_vma=False
    )
```

```python
import functools
import math

import jax
import jax.numpy as jnp
from jax import lax
from jax.experimental import pallas as pl
from jax.experimental.pallas import tpu as pltpu
from jax.sharding import PartitionSpec as P

HEAD_DIM = 128
EPS = 1e-06
ROPE_BASE = 10000.0
LANES = 128
HIDE = -1e30
LOG2E = 1.4426950408889634
LN2 = 0.6931471805599453
LEVEL_KEYS = (512, 256, 128)
MIB = 1 << 20

f32 = jnp.float32
bf16 = jnp.bfloat16


def dot(a, b):
    return lax.dot_general(a, b, (((1,), (0,)), ((), ())), preferred_element_type=f32)


def dot_nt(a, b):
    return lax.dot_general(a, b, (((1,), (1,)), ((), ())), preferred_element_type=f32)


def iota(shape, dim):
    return lax.broadcasted_iota(jnp.int32, shape, dim).astype(f32)


def divided(index, by):
    quotient = jnp.floor((index + 0.5) * (1.0 / by))
    return quotient, index - by * quotient


def one_hot(condition):
    return jnp.where(condition, 1.0, 0.0).astype(bf16)


def rms(values, gain):
    mean_square = jnp.mean(values * values, axis=-1, keepdims=True)
    return (values * lax.rsqrt(mean_square + EPS) * gain).astype(bf16)


def ring_get(piece, count):
    pieces = [piece]
    for step in range(1, count):
        pieces.append(
            lax.ppermute(piece, "tensor", [((i + step) % count, i) for i in range(count)])
        )
    return pieces


def ring_send(pieces):
    count = len(pieces)
    arrived = [pieces[0]]
    for step in range(1, count):
        arrived.append(
            lax.ppermute(pieces[step], "tensor", [(i, (i + step) % count) for i in range(count)])
        )
    return arrived


def exchange(rows, groups, halves=False):
    size = groups // 2 if halves else groups
    blocks = rows.reshape(size, rows.shape[0] // size, rows.shape[1])
    parts = [list(range(size)), list(range(size, groups))] if halves else None
    return lax.all_to_all(
        blocks, "dp", split_axis=0, concat_axis=0, tiled=True, axis_index_groups=parts
    ).reshape(rows.shape)


def from_partner(array, groups):
    return lax.ppermute(array, "dp", [(i, (i + groups // 2) % groups) for i in range(groups)])


def in_hbm(array):
    return pltpu.with_memory_space_constraint(array, pltpu.HBM)


def whole():
    return pl.BlockSpec(memory_space=pltpu.VMEM)


def scalar():
    return pl.BlockSpec(memory_space=pltpu.SMEM)


def params(mib, grid=0):
    return pltpu.CompilerParams(
        vmem_limit_bytes=mib * MIB,
        dimension_semantics=("arbitrary",) * grid if grid else None,
    )


def cost(flops, nbytes):
    return pl.CostEstimate(flops=int(flops), bytes_accessed=int(nbytes), transcendentals=0)


def upright(row):
    size = row.shape[1]
    diagonal = iota((size, size), 0) == iota((size, size), 1)
    return jnp.sum(jnp.where(diagonal, row, 0.0), axis=1, keepdims=True)


def in_rows(values, leaf_len):
    choices, requests, _ = values.shape
    rows = requests * leaf_len
    request_of_row, token_of_row = divided(iota((1, rows), 1), leaf_len)
    flat = values.astype(f32).reshape(choices * requests, leaf_len).astype(bf16)
    spread = dot(flat, one_hot(iota((leaf_len, 1), 0) == token_of_row))
    _, request = divided(iota((choices * requests, 1), 0), requests)
    kept = jnp.where(request == request_of_row, spread, 0.0)
    return jnp.sum(kept.reshape(choices, requests, rows), axis=1)


def across_rows(column):
    size = column.shape[0]
    diagonal = iota((size, size), 0) == iota((size, size), 1)
    return jnp.sum(jnp.where(diagonal, column, 0.0), axis=0, keepdims=True)


def owner_slots(owner):
    rows = []
    for level in range(3):
        mine, repeated = owner[level : level + 1], 0.0
        for earlier in range(level):
            same = upright(owner[earlier : earlier + 1]) == mine
            repeated = repeated + jnp.max(jnp.where(same, 1.0, 0.0), axis=0, keepdims=True)
        rows.append(mine * 2.0 + repeated)
    return rows


def prelude_kernel(
    owner_ref, start_ref, length_ref, request_ref, ids_ref, gates_ref,
    place_ref, meta_ref, cos_ref, sin_ref, table_ref, pick_ref,
    *, leaf_len,
):
    requests = owner_ref.shape[1]
    slot_rows, rows = place_ref.shape
    start, length = start_ref[...].astype(f32), length_ref[...].astype(f32)
    row_slot, row_token = divided(iota((slot_rows, 1), 0), leaf_len)
    request_of_row, token_of_row = divided(iota((1, rows), 1), leaf_len)
    row_request, row_place = divided(iota((rows, 1), 0), leaf_len)
    mine = iota((1, requests), 1) == row_request
    slot_across, token_across = divided(iota((1, slot_rows), 1), leaf_len)
    named, first_key, key_count = 0.0, 0.0, 0.0
    for level, slot in enumerate(owner_slots(owner_ref[...].astype(f32))):
        slot_down = jnp.sum(jnp.where(mine, slot, 0.0), axis=1, keepdims=True)
        pick_ref[level] = one_hot((slot_down == slot_across) & (row_place == token_across))
        here = jnp.where(slot == row_slot, 1.0, 0.0)
        named = named + here
        first_key = first_key + here * start[level : level + 1]
        key_count = key_count + here * length[level : level + 1]
    placed = dot(named.astype(bf16), one_hot(iota((requests, 1), 0) == request_of_row))
    place_ref[...] = jnp.where(row_token == token_of_row, placed, 0.0).astype(bf16)

    first_key = jnp.sum(first_key, axis=1, keepdims=True)
    key_count = jnp.sum(key_count, axis=1, keepdims=True)
    dest, place = divided(request_ref[...].astype(f32), requests)
    row_group, _ = divided(row_slot, 2)
    tag = jnp.sum(jnp.where(dest == row_group, place + 1.0, 0.0), axis=1, keepdims=True)
    lane = iota((1, LANES), 1)
    meta = jnp.zeros((slot_rows, LANES), f32)
    for at, value in enumerate(divided(first_key, 32) + divided(key_count, 32) + (tag,)):
        meta = jnp.where(lane == at, value, meta)
    meta_ref[...] = meta.astype(bf16)

    offsets = length[0:1] + length[1:2] + length[2:3]
    position = jnp.sum(jnp.where(mine, offsets, 0.0), axis=1, keepdims=True) + row_place
    half = HEAD_DIM // 2
    pair = jnp.where(lane < half, lane, lane - half)
    angle = position * jnp.exp(pair * (-2.0 * math.log(ROPE_BASE) / HEAD_DIM))
    cos_ref[...] = jnp.cos(angle)
    sin_ref[...] = jnp.sin(angle) * jnp.where(lane < half, -1.0, 1.0)

    gates = gates_ref[...]
    gates_high = gates.astype(bf16).astype(f32)
    choices = gates.shape[0]
    for at, values in enumerate((ids_ref[...], gates_high, gates - gates_high)):
        table_ref[at * choices : (at + 1) * choices, :] = in_rows(values, leaf_len)
    dest_down = jnp.sum(jnp.where(mine, dest, 0.0), axis=1, keepdims=True)
    last = 3 * choices
    size = table_ref.shape[0] - last
    table_ref[last:, :] = jnp.broadcast_to(across_rows(dest_down), (size, rows))


def routing_kernel(
    half_ref, after_ref, table_ref, far_table_ref,
    send_ref, high_ref, low_ref, final_ref,
    *, tensors, leaf_len, groups, capacity, experts, choices,
):
    rows = table_ref.shape[1]
    final_rows = final_ref.shape[0]
    share = leaf_len // tensors
    _, token_of_row = divided(iota((1, rows), 1), leaf_len)

    slots = send_ref.shape[0]
    local = experts // groups
    block, slot_place = divided(iota((slots, 1), 0), capacity)
    block, local_expert = divided(block, local)
    device, slot_source = divided(block, 2)
    first_expert = (half_ref[0] * (experts // 2)).astype(f32)
    spread = one_hot(first_expert + device * local + local_expert == iota((1, experts), 1))
    expert_down = iota((experts, 1), 0)
    ahead = one_hot(iota((rows, rows), 0) < iota((rows, rows), 1))
    block, final_place = divided(iota((final_rows, 1), 0), share)
    block, final_source = divided(block, 2)
    final_group, final_half = divided(block, tensors)
    final_token = final_half * share + final_place
    send, high, low, final = [], [], [], []
    for source, table in enumerate((table_ref[...], far_table_ref[...])):
        member, gate_high, gate_low = 0.0, 0.0, 0.0
        for choice in range(choices):
            hit = jnp.where(table[choice : choice + 1] == expert_down, 1.0, 0.0)
            member = member + hit
            gate_high = gate_high + hit * table[choices + choice : choices + choice + 1]
            gate_low = gate_low + hit * table[2 * choices + choice : 2 * choices + choice + 1]
        member = member.astype(bf16)
        before = dot(member, ahead).astype(bf16)
        taken = (dot(spread, member) > 0.5) & (dot(spread, before) == slot_place)
        taken = taken & (slot_source == source)
        send.append(jnp.where(taken, 1.0, 0.0))
        high.append(jnp.where(taken, dot(spread, gate_high.astype(bf16)), 0.0))
        low.append(jnp.where(taken, dot(spread, gate_low.astype(bf16)), 0.0))
        going = (table[3 * choices : 3 * choices + 1] == final_group) & (final_source == source)
        final.append(jnp.where(going & (final_token == token_of_row), 1.0, 0.0))
    send_ref[...] = jnp.concatenate(send, axis=1).astype(bf16)
    high_ref[...] = jnp.transpose(jnp.concatenate(high, axis=1)).astype(bf16)
    low_ref[...] = jnp.transpose(jnp.concatenate(low, axis=1)).astype(bf16)
    final_ref[...] = jnp.concatenate(final, axis=1).astype(bf16)


def rotated(product, cosine, sine, heads):
    columns = []
    for head in range(heads):
        part = product[:, head * HEAD_DIM : (head + 1) * HEAD_DIM]
        columns.append(part * cosine + pltpu.roll(part, HEAD_DIM // 2, 1) * sine)
    return jnp.concatenate(columns, axis=1).astype(bf16)


def query_kernel(*refs, tensors, heads):
    index_ref, pieces, refs = refs[0], refs[1 : 1 + tensors], refs[1 + tensors :]
    (gain_ref, weight_ref, cos_ref, sin_ref, place_ref, meta_ref,
     raw_ref, normed_ref, query_ref, send_ref, buffer_ref, semaphores) = refs
    width = heads * HEAD_DIM
    copies = column_copies(weight_ref, buffer_ref, semaphores, width)
    shard = pieces[0].shape[0]
    for at, piece in enumerate(pieces):
        owner = lax.rem(index_ref[0] + at, tensors)
        raw_ref[pl.ds(pl.multiple_of(owner * shard, shard), shard), :] = piece[...]
    normed_ref[...] = rms(raw_ref[...].astype(f32), gain_ref[...])
    send_ref[:, send_ref.shape[1] - LANES :] = meta_ref[...]
    for at, copy in enumerate(copies):
        copy.wait()
        columns = slice(at * width, (at + 1) * width)
        product = dot(normed_ref[...], buffer_ref[:, columns])
        query = rotated(product, cos_ref[...], sin_ref[...], heads)
        query_ref[:, columns] = query
        send_ref[:, columns] = dot(place_ref[...], query).astype(bf16)


def leaf_kernel(
    normed_ref, query_ref, key_ref, value_ref, cos_ref, sin_ref, out_ref, lse_ref,
    *, heads, leaf_len, scale,
):
    step = pl.program_id(0)
    normed = normed_ref[...]
    rows = normed.shape[0]
    keys = rotated(dot(normed, key_ref[...]), cos_ref[...], sin_ref[...], heads)
    values = dot(normed, value_ref[...]).astype(bf16)
    down, across = iota((rows, 1), 0), iota((1, rows), 1)
    visible = (divided(down, leaf_len)[0] == divided(across, leaf_len)[0]) & (across <= down)
    lane = lax.broadcasted_iota(jnp.int32, (1, LANES), 1)

    @pl.when(step == 0)
    def _():
        lse_ref[...] = jnp.zeros_like(lse_ref)

    for head in range(heads):
        at = slice(head * HEAD_DIM, (head + 1) * HEAD_DIM)
        scores = jnp.where(visible, dot_nt(query_ref[:, at], keys[:, at]) * scale, HIDE)
        highest = jnp.max(scores, axis=1, keepdims=True)
        weights = jnp.exp(scores - highest)
        total = jnp.sum(weights, axis=1, keepdims=True)
        out_ref[:, at] = dot(weights.astype(bf16), values[:, at]) / total
        lse = highest + jnp.log(total)
        lse_ref[...] = jnp.where(lane == step * heads + head, lse, lse_ref[...])


def owner_kernel(
    arrived_ref, kv_ref, back_ref, query_ref, out_ref,
    *, heads, requests, leaf_len, scale,
):
    slot_rows = arrived_ref.shape[0]
    width = heads * HEAD_DIM
    count = requests * leaf_len
    packed = arrived_ref[:, width:]
    meta = packed.astype(f32)
    first = meta[:, 0:1] * 32.0 + meta[:, 1:2]
    used = meta[:, 2:3] + meta[:, 3:4] > 0.0
    begins = [sum(LEVEL_KEYS[:level]) for level in range(3)]
    level = jnp.where(first >= begins[1], 1.0, 0.0) + jnp.where(first >= begins[2], 1.0, 0.0)
    level = jnp.where(used, level, 3.0)
    lane = lax.broadcasted_iota(jnp.int32, (1, LANES), 1)
    of_level = level == lane.astype(f32)
    ahead = one_hot(iota((slot_rows, slot_rows), 1) < iota((slot_rows, slot_rows), 0))
    rank = dot(ahead, one_hot(of_level))
    rank = jnp.sum(jnp.where(of_level, rank, 0.0), axis=1, keepdims=True)
    target = jnp.where(used, level * count + rank, -1.0)
    spread = jnp.where(target == iota((1, 3 * count), 1), 1.0, 0.0)
    ordered = jnp.transpose(spread).astype(bf16)
    query_ref[...] = dot(ordered, arrived_ref[:, :width]).astype(bf16)
    meta = dot(ordered, packed)
    first = meta[:, 0:1] * 32.0 + meta[:, 1:2]
    last = first + meta[:, 2:3] * 32.0 + meta[:, 3:4]
    for level in range(3):
        size = LEVEL_KEYS[level]
        part = slice(level * count, (level + 1) * count)
        keys = slice(begins[level], begins[level] + size)
        key = iota((1, size), 1) + float(begins[level])
        bias = jnp.where((key >= first[part]) & (key < last[part]), 0.0, HIDE)
        ones = jnp.ones((size, HEAD_DIM), bf16)
        sums = jnp.zeros((count, LANES), f32)
        at = [slice(head * HEAD_DIM, (head + 1) * HEAD_DIM) for head in range(heads)]
        scores = [
            dot_nt(query_ref[part, one], kv_ref[0, keys, one]) * (scale * LOG2E) + bias
            for one in at
        ]
        highest = [jnp.max(one, axis=1, keepdims=True) for one in scores]
        weights = [jnp.exp2(one - high).astype(bf16) for one, high in zip(scores, highest)]
        for head in range(heads):
            both = dot(weights[head], jnp.concatenate([kv_ref[1, keys, at[head]], ones], axis=1))
            total = both[:, HEAD_DIM:]
            out_ref[part, at[head]] = (both[:, :HEAD_DIM] / total).astype(bf16)
            lse = highest[head] * LN2 + jnp.log(total)
            lse_high = lse.astype(bf16).astype(f32)
            sums = jnp.where(lane == head, lse_high, sums)
            sums = jnp.where(lane == head + heads, lse - lse_high, sums)
        out_ref[part, width:] = sums.astype(bf16)
    back_ref[...] = dot(spread.astype(bf16), out_ref[...]).astype(bf16)


def column_copies(source_ref, target_ref, semaphores, step):
    copies = []
    for at in range(source_ref.shape[1] // step):
        columns = pl.ds(at * step, step)
        copy = pltpu.make_async_copy(
            source_ref.at[:, columns], target_ref.at[:, columns], semaphores.at[at]
        )
        copy.start()
        copies.append(copy)
    return copies


def merge_kernel(
    after_ref, back_ref, pick_ref, leaf_ref, lse_ref, weight_ref, out_ref, buffer_ref, attended_ref, semaphores,
    *, heads, step,
):
    copies = column_copies(weight_ref, buffer_ref, semaphores, step)
    width = heads * HEAD_DIM
    back = back_ref[...]
    outputs, sums = [leaf_ref[...]], [lse_ref[...]]
    for level in range(3):
        rows = dot(pick_ref[level], back)
        outputs.append(rows[:, :width])
        tail = rows[:, width:]
        sums.append(tail + pltpu.roll(tail, LANES - heads, 1))
    highest = functools.reduce(jnp.maximum, sums)
    scales = [jnp.exp(one - highest) for one in sums]
    total = sum(scales[1:], scales[0])
    scales = [one / total for one in scales]
    for head in range(heads):
        at = slice(head * HEAD_DIM, (head + 1) * HEAD_DIM)
        mixed = sum(scales[i][:, head : head + 1] * outputs[i][:, at] for i in range(4))
        attended_ref[:, at] = mixed.astype(bf16)
    for at, copy in enumerate(copies):
        copy.wait()
        columns = slice(at * step, (at + 1) * step)
        out_ref[:, columns] = dot(attended_ref[...], buffer_ref[:, columns]).astype(bf16)


def middle_kernel(*refs, tensors):
    index_ref, _, raw_ref, gain_ref = refs[:4]
    pieces = refs[4 : 4 + tensors]
    normed_ref, own_ref, resid_own_ref, resid_ref = refs[4 + tensors :]
    width = own_ref.shape[1]
    own = pl.ds(pl.multiple_of(index_ref[0] * width, width), width)
    total = raw_ref[...].astype(f32)
    for piece in pieces:
        total = total + piece[...].astype(f32)
    resid_ref[...] = total
    resid_own_ref[...] = resid_ref[:, own]
    normed_ref[...] = rms(total, gain_ref[...])
    own_ref[...] = normed_ref[:, own]


def dispatch_kernel(after_ref, also_after_ref, send_ref, own_ref, far_ref, out_ref):
    both = jnp.concatenate([own_ref[...], far_ref[...]], axis=0)
    out_ref[...] = dot(send_ref[...], both).astype(bf16)


def shared_kernel(*refs, tensors):
    index_ref, rows_ref, in_hbm_ref, down_hbm_ref, expert_in_ref, expert_down_ref = refs[:6]
    pieces, refs = refs[6 : 6 + tensors], refs[6 + tensors :]
    early_in_ref, early_down_ref, in_ref, down_ref, total_ref, semaphores = refs
    early = early_in_ref.shape[0]
    copies = [
        pltpu.make_async_copy(in_hbm_ref.at[0], in_ref.at[0], semaphores.at[0]),
        pltpu.make_async_copy(in_hbm_ref.at[1], in_ref.at[1], semaphores.at[1]),
        pltpu.make_async_copy(down_hbm_ref, down_ref, semaphores.at[2]),
        pltpu.make_async_copy(expert_in_ref.at[0:early], early_in_ref, semaphores.at[3]),
        pltpu.make_async_copy(expert_down_ref.at[0], early_down_ref, semaphores.at[4]),
    ]
    for copy in copies:
        copy.start()
    rows = rows_ref[...]
    copies[0].wait()
    gate = dot_nt(rows, in_ref[0])
    copies[1].wait()
    up = dot_nt(rows, in_ref[1])
    hidden = (gate / (1.0 + jnp.exp(-gate)) * up).astype(bf16)
    copies[2].wait()
    total_ref[...] = dot(hidden, down_ref[...])
    width = pieces[0].shape[1]
    for at, piece in enumerate(pieces):
        column = lax.rem(index_ref[0] + at, tensors) * width
        piece[...] = total_ref[:, pl.ds(pl.multiple_of(column, width), width)].astype(bf16)
    copies[3].wait()
    copies[4].wait()


def rows_of_experts(piece, experts, capacity):
    groups, _, width = piece.shape
    values = piece[...].astype(f32)
    for e in range(experts):
        mine = values[:, e * capacity : (e + 1) * capacity, :].reshape(groups * capacity, width)
        yield mine.astype(bf16)


def own_half_kernel(index_ref, piece, early_in_ref, out_ref, *, experts, capacity):
    width = piece.shape[2]
    columns = pl.ds(pl.multiple_of(index_ref[0] * width, width), width)
    rows = list(rows_of_experts(piece, experts, capacity))
    for e in range(early_in_ref.shape[0]):
        for part in range(2):
            out_ref[e, part] = dot_nt(rows[e], early_in_ref[e, part, :, columns])


def expert_kernel(*refs, tensors, experts, capacity):
    index_ref, arrived, refs = refs[0], refs[1 : 1 + tensors], refs[1 + tensors :]
    (half_ref, early_in_ref, early_down_ref, in_hbm_ref, down_hbm_ref), refs = refs[:5], refs[5:]
    pieces, refs = refs[:tensors], refs[tensors:]
    in_ref, down_ref, rows_ref, semaphores = refs
    early = early_in_ref.shape[0]
    in_copies, down_copies = {}, {}
    for e in range(1, experts):
        down_copies[e] = pltpu.make_async_copy(
            down_hbm_ref.at[e], down_ref.at[e - 1], semaphores.at[0, e]
        )
        if e >= early:
            in_copies[e] = pltpu.make_async_copy(
                in_hbm_ref.at[e], in_ref.at[e - early], semaphores.at[1, e]
            )
            in_copies[e].start()
        down_copies[e].start()
    groups, _, width = arrived[0].shape
    columns = [
        pl.ds(pl.multiple_of(lax.rem(index_ref[0] + at, tensors) * width, width), width)
        for at in range(tensors)
    ]
    for at, piece in enumerate(arrived):
        for e, rows in enumerate(rows_of_experts(piece, experts, capacity)):
            rows_ref[e, :, columns[at]] = rows
    together = max(1, 16 // capacity)
    values = []
    for e in range(experts):
        if e < early:
            weights = early_in_ref.at[e]
        else:
            weights = in_ref.at[e - early]
            in_copies[e].wait()
        down = early_down_ref if e == 0 else down_ref.at[e - 1]
        if e < early:
            gate, up = half_ref[e, 0], half_ref[e, 1]
            for at in range(1, tensors):
                other = rows_ref[e, :, columns[at]]
                gate = gate + dot_nt(other, weights[0, :, columns[at]])
                up = up + dot_nt(other, weights[1, :, columns[at]])
        else:
            gate = dot_nt(rows_ref[e], weights[0])
            up = dot_nt(rows_ref[e], weights[1])
        hidden = (gate / (1.0 + jnp.exp(-gate)) * up).astype(bf16)
        if e > 0:
            down_copies[e].wait()
        values.append(
            [
                dot(hidden, down[:, columns[at]]).reshape(groups, capacity, width)
                for at in range(tensors)
            ]
        )
        if len(values) == together or e == experts - 1:
            mine = slice((e + 1 - len(values)) * capacity, (e + 1) * capacity)
            for at, piece in enumerate(pieces):
                parts = [value[at] for value in values]
                piece[:, mine, :] = jnp.concatenate(parts, axis=1).astype(bf16)
            values = []


def add_kernel(after_ref, *refs):
    out_ref = refs[-1]
    out_ref[...] = sum(piece[...].astype(f32) for piece in refs[:-1]).astype(bf16)


def combine_kernel(*refs, tensors):
    returned_ref, high_ref, low_ref, resid_ref, final_ref = refs[:5]
    shared, out_ref = refs[5 : 5 + tensors], refs[5 + tensors]
    returned = returned_ref[...]
    routed = dot(high_ref[...], returned) + dot(low_ref[...], returned)
    rows = resid_ref.shape[0]
    total = resid_ref[...]
    for piece in shared:
        total = total + piece[...].astype(f32)
    both = jnp.concatenate([total + routed[:rows], routed[rows:]], axis=0).astype(bf16)
    out_ref[...] = dot(final_ref[...], both).astype(bf16)


def settle_kernel(meta_ref, rows_ref, out_ref, *, tensors, leaf_len, groups):
    slot_rows, final_rows = meta_ref.shape[0], rows_ref.shape[0]
    requests, share, _ = out_ref.shape
    width = rows_ref.shape[1]
    tag_down = meta_ref[...].astype(f32)[:, 4:5]
    block, place = divided(iota((1, final_rows), 1), share)
    block, source = divided(block, 2)
    group, half = divided(block, tensors)
    _, home = divided(group + source * (groups // 2), groups)
    tagged = iota((slot_rows, 1), 0) == home * (2.0 * leaf_len)
    tag = jnp.sum(jnp.where(tagged, tag_down, 0.0), axis=0, keepdims=True)
    request, position = divided(iota((requests * share, 1), 0), share)
    wanted = (tag == request + 1.0) & (place == position)
    for at in range(tensors):
        value = dot(one_hot(wanted & (half == at)), rows_ref[...])
        for r in range(requests):
            out_ref[r, :, at * width : (at + 1) * width] = value[
                r * share : (r + 1) * share
            ].astype(bf16)


def on_device(
    leaf_tokens,
    attn_gain,
    w_query,
    w_key,
    w_value,
    w_out,
    prefix_kv,
    prefix_owner,
    prefix_start,
    prefix_len,
    mlp_gain,
    shared_in,
    shared_out,
    expert_in,
    expert_out,
    expert_ids,
    gate_weights,
    request_of,
):
    groups = lax.axis_size("dp")
    tensors = lax.axis_size("tensor")
    index = lax.axis_index("tensor").astype(jnp.int32).reshape(1)
    shard_requests, leaf_len, model_width = leaf_tokens.shape
    requests = prefix_owner.shape[0]
    rows = requests * leaf_len
    local_width = w_query.shape[1]
    local_heads = local_width // HEAD_DIM
    scale = HEAD_DIM ** (-0.5)
    column_share = model_width // tensors
    top_count = expert_ids.shape[2]
    local_experts = expert_in.shape[0]
    experts = local_experts * groups
    assignments = rows * top_count
    capacity = tensors * max(1, assignments * 4 // (experts * 3 * tensors))
    slots = experts * capacity
    slot_rows = groups * 2 * leaf_len
    shape = jax.ShapeDtypeStruct

    raw_pieces = ring_get(leaf_tokens.reshape(shard_requests * leaf_len, model_width), tensors)

    owner_rows, request_row = prefix_owner.T, request_of.reshape(1, requests)
    table_rows = -(-(3 * top_count + 1) // 8) * 8
    place, meta, cosine, sine, table, pick = pl.pallas_call(
        functools.partial(prelude_kernel, leaf_len=leaf_len),
        out_shape=[
            shape((slot_rows, rows), bf16),
            shape((slot_rows, LANES), bf16),
            shape((rows, LANES), f32),
            shape((rows, LANES), f32),
            shape((table_rows, rows), f32),
            shape((3, rows, slot_rows), bf16),
        ],
        in_specs=[whole()] * 6,
        out_specs=[whole()] * 6,
        compiler_params=params(4),
        name="prelude",
    )(
        in_hbm(owner_rows), in_hbm(prefix_start.T), in_hbm(prefix_len.T), in_hbm(request_row),
        in_hbm(jnp.transpose(expert_ids, (2, 0, 1))),
        in_hbm(jnp.transpose(gate_weights, (2, 0, 1))),
    )
    far_table = from_partner(table, groups)

    step_heads = min(2, local_heads)
    step_width = step_heads * HEAD_DIM
    steps = local_heads // step_heads
    query_heads = min(4, local_heads)
    fixed = lambda *dims: pl.BlockSpec(dims, lambda i: (0,) * len(dims))
    columns = lambda *dims: pl.BlockSpec(dims, lambda i: (0,) * (len(dims) - 1) + (i,))
    send_width = local_width + LANES
    raw, normed, query, query_send = pl.pallas_call(
        functools.partial(query_kernel, tensors=tensors, heads=query_heads),
        out_shape=[
            shape((rows, model_width), bf16),
            shape((rows, model_width), bf16),
            shape((rows, local_width), bf16),
            shape((slot_rows, send_width), bf16),
        ],
        in_specs=[scalar()]
        + [whole()] * (tensors + 1)
        + [pl.BlockSpec(memory_space=pltpu.HBM)]
        + [whole()] * 4,
        out_specs=[whole()] * 4,
        scratch_shapes=[
            pltpu.VMEM((model_width, local_width), bf16),
            pltpu.SemaphoreType.DMA((local_heads // query_heads,)),
        ],
        compiler_params=params(10),
        cost_estimate=cost(2 * rows * model_width * local_width, 2 * model_width * local_width),
        name="queries",
    )(
        index, in_hbm(raw_pieces[0]), *raw_pieces[1:], in_hbm(attn_gain.reshape(1, -1)), in_hbm(w_query),
        cosine, sine, place, meta,
    )

    query_arrived = exchange(query_send, groups)

    leaf_out, leaf_lse = pl.pallas_call(
        functools.partial(leaf_kernel, heads=step_heads, leaf_len=leaf_len, scale=scale),
        grid=(steps,),
        out_shape=[shape((rows, local_width), f32), shape((rows, LANES), f32)],
        in_specs=[
            fixed(rows, model_width),
            columns(rows, step_width),
            columns(model_width, step_width),
            columns(model_width, step_width),
            fixed(rows, LANES),
            fixed(rows, LANES),
        ],
        out_specs=[columns(rows, step_width), fixed(rows, LANES)],
        compiler_params=params(10, 1),
        cost_estimate=cost(4 * rows * model_width * local_width, 4 * model_width * local_width),
        name="leaf",
    )(normed, query, in_hbm(w_key), in_hbm(w_value), cosine, sine)

    pool = prefix_kv.shape[1]
    back_send = pl.pallas_call(
        functools.partial(
            owner_kernel, heads=local_heads, requests=requests, leaf_len=leaf_len, scale=scale
        ),
        out_shape=shape((slot_rows, send_width), bf16),
        in_specs=[whole()] * 2,
        out_specs=whole(),
        scratch_shapes=[
            pltpu.VMEM((3 * rows, local_width), bf16),
            pltpu.VMEM((3 * rows, send_width), bf16),
        ],
        compiler_params=params(16),
        cost_estimate=cost(4 * slot_rows * pool * local_width, 4 * pool * local_width),
        name="owner",
    )(query_arrived, prefix_kv)

    back = exchange(back_send, groups)

    out_step = min(512, model_width)
    partial_out = pl.pallas_call(
        functools.partial(merge_kernel, heads=local_heads, step=out_step),
        out_shape=shape((rows, model_width), bf16),
        in_specs=[pl.BlockSpec(memory_space=pl.ANY)]
        + [whole()] * 4
        + [pl.BlockSpec(memory_space=pltpu.HBM)],
        out_specs=whole(),
        scratch_shapes=[
            pltpu.VMEM((local_width, model_width), bf16),
            pltpu.VMEM((rows, local_width), bf16),
            pltpu.SemaphoreType.DMA((model_width // out_step,)),
        ],
        compiler_params=params(10),
        cost_estimate=cost(2 * rows * local_width * model_width, 2 * local_width * model_width),
        name="merge",
    )(far_table, back, pick, leaf_out, leaf_lse, in_hbm(w_out))

    out_pieces = ring_get(partial_out, tensors)

    half = (lax.axis_index("dp") // (groups // 2)).astype(jnp.int32).reshape(1)
    send, gate_high, gate_low, final = pl.pallas_call(
        functools.partial(
            routing_kernel, tensors=tensors, leaf_len=leaf_len, groups=groups,
            capacity=capacity, experts=experts, choices=top_count,
        ),
        out_shape=[
            shape((slots, 2 * rows), bf16),
            shape((2 * rows, slots), bf16),
            shape((2 * rows, slots), bf16),
            shape((slot_rows, 2 * rows), bf16),
        ],
        in_specs=[scalar(), pl.BlockSpec(memory_space=pl.ANY)] + [whole()] * 2,
        out_specs=[whole()] * 4,
        compiler_params=params(6),
        cost_estimate=cost(1, 1),
        name="routing",
    )(half, partial_out, table, far_table)

    normed_mlp, own_columns, resid_own = pl.pallas_call(
        functools.partial(middle_kernel, tensors=tensors),
        out_shape=[
            shape((rows, model_width), bf16),
            shape((rows, column_share), bf16),
            shape((rows, column_share), f32),
        ],
        in_specs=[scalar(), pl.BlockSpec(memory_space=pl.ANY)] + [whole()] * (2 + tensors),
        out_specs=[whole()] * 3,
        scratch_shapes=[pltpu.VMEM((rows, model_width), f32)],
        compiler_params=params(4),
        name="middle",
    )(index, send, raw, mlp_gain.reshape(1, -1), *out_pieces)

    far_columns = from_partner(own_columns, groups)
    hbm = pl.BlockSpec(memory_space=pltpu.HBM)
    hidden = shared_out.shape[0]
    expert_hidden = expert_out.shape[1]
    expert_in = in_hbm(jnp.transpose(expert_in, (0, 2, 3, 1)))
    expert_out = in_hbm(expert_out)
    early = max(1, local_experts // 2)
    *shared_pieces, early_in, early_down = pl.pallas_call(
        functools.partial(shared_kernel, tensors=tensors),
        out_shape=[shape((rows, column_share), bf16)] * tensors
        + [
            pltpu.VMEM((early, 2, expert_hidden, model_width), bf16),
            pltpu.VMEM((expert_hidden, model_width), bf16),
        ],
        in_specs=[scalar(), whole()] + [hbm] * 4,
        out_specs=[whole()] * (tensors + 2),
        scratch_shapes=[
            pltpu.VMEM((2, hidden, model_width), bf16),
            pltpu.VMEM((hidden, model_width), bf16),
            pltpu.VMEM((rows, model_width), f32),
            pltpu.SemaphoreType.DMA((5,)),
        ],
        compiler_params=params(11),
        cost_estimate=cost(1, 1),
        name="shared",
    )(
        index, normed_mlp, in_hbm(jnp.transpose(shared_in, (1, 2, 0))), in_hbm(shared_out),
        expert_in, expert_out,
    )

    send_rows = pl.pallas_call(
        dispatch_kernel,
        out_shape=shape((slots, column_share), bf16),
        in_specs=[pl.BlockSpec(memory_space=pl.ANY)] * 2 + [whole()] * 3,
        out_specs=whole(),
        compiler_params=params(3),
        name="dispatch",
    )(shared_pieces[0], early_down, send, own_columns, far_columns)

    arrived = exchange(send_rows, groups, halves=True)

    block = local_experts * capacity
    arrived_pieces = ring_get(arrived.reshape(groups, block, column_share), tensors)
    early_in = pltpu.with_memory_space_constraint(early_in, pltpu.VMEM)
    own_half = pl.pallas_call(
        functools.partial(own_half_kernel, experts=local_experts, capacity=capacity),
        out_shape=shape((early, 2, groups * capacity, expert_hidden), f32),
        in_specs=[scalar()] + [whole()] * 2,
        out_specs=whole(),
        compiler_params=params(8),
        cost_estimate=cost(1, 1),
        name="own_half",
    )(index, arrived_pieces[0], early_in)
    partial_pieces = pl.pallas_call(
        functools.partial(
            expert_kernel, tensors=tensors, experts=local_experts, capacity=capacity
        ),
        out_shape=[shape((groups, block, column_share), bf16)] * tensors,
        in_specs=[scalar()] + [whole()] * (tensors + 3) + [hbm, hbm],
        out_specs=[whole()] * tensors,
        scratch_shapes=[
            pltpu.VMEM((local_experts - early, 2, expert_hidden, model_width), bf16),
            pltpu.VMEM((local_experts - 1, expert_hidden, model_width), bf16),
            pltpu.VMEM((local_experts, groups * capacity, model_width), bf16),
            pltpu.SemaphoreType.DMA((2, local_experts)),
        ],
        compiler_params=params(28),
        cost_estimate=cost(
            6 * slots * expert_hidden * model_width,
            6 * local_experts * expert_hidden * model_width,
        ),
        name="experts",
    )(
        index,
        *arrived_pieces,
        own_half,
        early_in,
        pltpu.with_memory_space_constraint(early_down, pltpu.VMEM),
        expert_in,
        expert_out,
    )
    partial_pieces, shared_pieces = lax.optimization_barrier((partial_pieces, shared_pieces))
    shared_pieces = ring_send(shared_pieces)
    partial_pieces = ring_send(partial_pieces)
    summed = pl.pallas_call(
        add_kernel,
        out_shape=shape((groups, block, column_share), bf16),
        in_specs=[pl.BlockSpec(memory_space=pl.ANY)] + [whole()] * tensors,
        out_specs=whole(),
        compiler_params=params(6),
        name="add",
    )(shared_pieces[-1], *partial_pieces)

    returned = exchange(summed.reshape(slots, column_share), groups, halves=True)

    final_send = pl.pallas_call(
        functools.partial(combine_kernel, tensors=tensors),
        out_shape=shape((slot_rows, column_share), bf16),
        in_specs=[whole()] * (5 + tensors),
        out_specs=whole(),
        compiler_params=params(6),
        name="combine",
    )(returned, gate_high, gate_low, resid_own, final, *shared_pieces)

    devices = groups * tensors
    blocks = final_send.reshape(devices, slot_rows // devices, column_share)
    final_arrived = lax.all_to_all(
        blocks, ("dp", "tensor"), split_axis=0, concat_axis=0, tiled=True
    ).reshape(slot_rows, column_share)

    return pl.pallas_call(
        functools.partial(settle_kernel, tensors=tensors, leaf_len=leaf_len, groups=groups),
        grid=(1,),
        out_shape=shape((requests, leaf_len // tensors, model_width), bf16),
        in_specs=[
            pl.BlockSpec((slot_rows, LANES), lambda i: (0, local_heads)),
            fixed(slot_rows, column_share),
        ],
        out_specs=fixed(requests, leaf_len // tensors, model_width),
        compiler_params=params(4, 1),
        name="settle",
    )(query_arrived, final_arrived)


def solution(mesh):
    in_specs = (
        P(("dp", "tensor"), None, None),
        P(),
        P(None, "tensor"),
        P(None, "tensor"),
        P(None, "tensor"),
        P("tensor", None),
        P(None, "dp", "tensor"),
        P("dp", None),
        P("dp", None),
        P("dp", None),
        P(),
        P(None, None, "tensor"),
        P("tensor", None),
        P("dp", None, None, "tensor"),
        P("dp", "tensor", None),
        P("dp", None, None),
        P("dp", None, None),
        P("dp"),
    )
    out_specs = P("dp", "tensor", None)
    return jax.shard_map(
        on_device, mesh=mesh, in_specs=in_specs, out_specs=out_specs, check_vma=False
    )
```
